32 devices in a mesh: seq: 8 (over z, x), ffn: 4 (over y, core).
Axes of the slice: x: 2, y: 2, z: 4, core: 2. Of those that a mesh axis runs over, the one named last changes fastest.
Arguments:
- block_in: bfloat16 [32768, 768], P(('seq', 'ffn')), may hold values from -6 to 6
- block_cot: bfloat16 [32768, 768], P(('seq', 'ffn')), may hold values from -6 to 6
- cluster_perm: int32 [8, 12, 4096], P('seq', 'ffn'), may hold values from 0 to 4095, each once within a row
- w_qkv: float32 [3, 768, 12, 64], P(None, None, 'ffn', 'seq'), may hold values from -0.21875 to 0.21875
- w_out: float32 [12, 64, 768], P('ffn', 'seq'), may hold values from -1.5 to 1.5
- w_up: float32 [768, 3072], P(None, ('seq', 'ffn')), may hold values from -0.21875 to 0.21875
- w_down: float32 [3072, 768], P(('seq', 'ffn')), may hold values from -0.109375 to 0.109375
- mom_qkv: float32 [3, 768, 12, 64], P(None, None, 'ffn', 'seq'), may hold values from -512 to 512
- mom_out: float32 [12, 64, 768], P('ffn', 'seq'), may hold values from -160 to 160
- mom_up: float32 [768, 3072], P(None, ('seq', 'ffn')), may hold values from -256 to 256
- mom_down: float32 [3072, 768], P(('seq', 'ffn')), may hold values from -512 to 512
- norm_params: float32 [4, 768], replicated, may hold values from -0.9 to 1.45, as said below
- norm_first: float32 [4, 768], replicated, may hold values from -112 to 112
- norm_second: float32 [4, 768], replicated, may hold values from 16.384 to 131.072
Outputs:
- block_out: bfloat16 [32768, 768], P(('seq', 'ffn'))
- input_grad: float32 [32768, 768], P(('seq', 'ffn'))
- grad_qkv: float32 [3, 768, 12, 64], P(None, None, 'ffn', 'seq')
- grad_out: float32 [12, 64, 768], P('ffn', 'seq')
- grad_up: float32 [768, 3072], P(None, ('seq', 'ffn'))
- grad_down: float32 [3072, 768], P(('seq', 'ffn'))
- grad_norm: float32 [4, 768], replicated
- moment_qkv: float32 [3, 768, 12, 64], P(None, None, 'ffn', 'seq')
- moment_out: float32 [12, 64, 768], P('ffn', 'seq')
- moment_up: float32 [768, 3072], P(None, ('seq', 'ffn'))
- moment_down: float32 [3072, 768], P(('seq', 'ffn'))
- master_qkv: float32 [3, 768, 12, 64], P(None, None, 'ffn', 'seq')
- master_out: float32 [12, 64, 768], P('ffn', 'seq')
- master_up: float32 [768, 3072], P(None, ('seq', 'ffn'))
- master_down: float32 [3072, 768], P(('seq', 'ffn'))
- first_new: float32 [4, 768], replicated
- second_new: float32 [4, 768], replicated
- norm_new: float32 [4, 768], replicated
- occupancy: float32 [12, 32], replicated
The draws below stay inside these ranges and needn't reach their ends.
Inputs may be any that keep to these rules, and one draw needn't show every extreme that they name: `cluster_perm`: each head's row is an order of the 4096 positions of its sequence; its aligned runs of 128 are the clusters. `norm_params`: rows 0 and 2 are gains, rows 1 and 3 biases.
All inputs are finite; a program needn't handle non-finite values.
Results may differ from the reference program's by a relative error of at most 0.02.
Values may be sent and summed in bfloat16 or wider, within the bound.
No kernel may reach another device: no remote copies, remote signals or barrier semaphores. Data moves between devices by JAX's collectives and lax.ppermute only.
A program may use at most 192 MiB of HBM per device.

```python
import math
import jax
import jax.numpy as jnp
from jax import lax

D = 768
HEADS = 12
HD = 64
FF = 3072
CLUSTER = 128
LEN = 4096
NS_STEPS = 3
ADAM_STEP = 10
SEQS = 8
TOKENS = 32768


def draw_norm_params(key, part):
    key_gain, key_bias = jax.random.split(key)
    gains = 1.0 + 0.15 * jnp.clip(jax.random.normal(key_gain, (4, D), jnp.float32), -3.0, 3.0)
    biases = 0.3 * jnp.clip(jax.random.normal(key_bias, (4, D), jnp.float32), -3.0, 3.0)
    row_index = lax.broadcasted_iota(jnp.int32, (4, D), 0)
    return jnp.where(row_index % 2 == 0, gains, biases)


def shard_levels(key, extent, pieces, least, top_value):
    def one(axis_at, parts):
        draws = jax.random.uniform(jax.random.fold_in(jax.random.fold_in(key, 6), axis_at), (parts,), jnp.float32, least / len(pieces), top_value / len(pieces))
        return jnp.repeat(jnp.exp(draws), extent[axis_at] // parts).reshape((-1,) + (1,) * (len(extent) - axis_at - 1))

    loudness = one(*pieces[0])
    for cut in pieces[1:]:
        loudness = loudness * one(*cut)
    return loudness


def gaussian(key, extent, scale, most, cuts=(), kind=jnp.bfloat16):
    values = jax.random.normal(key, extent, jnp.float32) * scale
    if len(cuts) > 0:
        values = shard_levels(key, extent, cuts, -0.22, 0.18) * values
    return jnp.clip(values, min=-most, max=most).astype(kind)


def setup_inputs(seed: int = 0) -> dict:
    arg_keys = jax.random.split(jax.random.key(seed), 15)
    block_in = gaussian(arg_keys[0], (TOKENS, D), 1.0, 6.0, ((0, 32),))
    block_cot = gaussian(arg_keys[1], (TOKENS, D), 1.0, 6.0, ((0, 32),))
    cluster_perm = jax.vmap(lambda own: jax.random.permutation(own, LEN))(jax.random.split(arg_keys[2], SEQS * HEADS)).reshape((SEQS, HEADS, LEN)).astype(jnp.int32)
    w_qkv = gaussian(arg_keys[3], (3, D, HEADS, HD), D ** -0.5, 0.21875, ((2, 4), (3, 8)), jnp.float32)
    w_out = gaussian(arg_keys[4], (HEADS, HD, D), (D * 3 // CLUSTER) ** -0.5, 1.5, ((0, 4), (1, 8)), jnp.float32)
    w_up = gaussian(arg_keys[5], (D, FF), D ** -0.5, 0.21875, ((1, 32),), jnp.float32)
    w_down = gaussian(arg_keys[6], (FF, D), FF ** -0.5, 0.109375, ((0, 32),), jnp.float32)
    mom_qkv = gaussian(arg_keys[7], (3, D, HEADS, HD), (0.5 * (LEN * SEQS) ** 0.5), 512.0, ((2, 4), (3, 8)), jnp.float32)
    mom_out = gaussian(arg_keys[8], (HEADS, HD, D), (0.15 * (LEN * SEQS) ** 0.5), 160.0, ((0, 4), (1, 8)), jnp.float32)
    mom_up = gaussian(arg_keys[9], (D, FF), (0.25 * (LEN * SEQS) ** 0.5), 256.0, ((1, 32),), jnp.float32)
    mom_down = gaussian(arg_keys[10], (FF, D), (0.5 * (LEN * SEQS) ** 0.5), 512.0, ((0, 32),), jnp.float32)
    norm_params = draw_norm_params(jax.random.fold_in(arg_keys[14], 71), 0)
    norm_first = gaussian(arg_keys[12], (4, D), (0.1 * (LEN * SEQS) ** 0.5), 112.0, (), jnp.float32)
    norm_second = jnp.clip(jnp.exp(jax.random.uniform(arg_keys[13], (4, D), jnp.float32, math.log(16.384), math.log(131.072))), 16.384, 131.072)
    return dict(block_in=block_in, block_cot=block_cot, cluster_perm=cluster_perm, w_qkv=w_qkv, w_out=w_out, w_up=w_up, w_down=w_down, mom_qkv=mom_qkv, mom_out=mom_out, mom_up=mom_up, mom_down=mom_down, norm_params=norm_params, norm_first=norm_first, norm_second=norm_second)


@jax.custom_vjp
def low(v):
    return lax.optimization_barrier(v.astype(jnp.bfloat16)).astype(jnp.float32)

@jax.custom_vjp
def low_back(v):
    return v

def low_keep(v):
    return (low(v), None)

def low_pass(kept, grad):
    return (grad,)

def back_keep(v):
    return (v, None)

def back_low(kept, grad):
    return (low(grad),)
low.defvjp(low_keep, low_pass)
low_back.defvjp(back_keep, back_low)
highest = lax.Precision.HIGHEST
schulz_coeffs = (3.4445, -4.775, 2.0315)
norm_epsilon = 1e-05

def layer_norm(inputs, gains, biases):
    center = inputs - lax.optimization_barrier(jnp.mean(inputs, axis=-1, keepdims=True))
    spread = lax.optimization_barrier(jnp.mean(center * center, axis=-1, keepdims=True))
    return center * lax.rsqrt(spread + norm_epsilon) * gains + biases

def gelu_value(preact):
    return preact * 0.5 * (1.0 + jax.scipy.special.erf(preact * 0.7071067811865476))

def by_rows(lookup, indices):
    return lookup[indices]

def attention(projected, cluster_order):
    head_count = cluster_order.shape[0]
    seq_len = cluster_order.shape[1]
    clusters = seq_len // CLUSTER
    positions = jnp.broadcast_to(jnp.arange(seq_len, dtype=jnp.int32)[None, :], cluster_order.shape)
    inverse = jnp.zeros_like(cluster_order).at[jnp.arange(head_count)[:, None], cluster_order].set(positions)
    grouped = jax.vmap(by_rows)(jnp.moveaxis(projected, 2, 0), cluster_order)
    grouped = grouped.reshape(head_count, clusters, CLUSTER, 3, HD)
    scores = jnp.einsum('hcqd,hckd->hcqk', grouped[:, :, :, 0], grouped[:, :, :, 1], precision=highest)
    scores = low_back(scores * (1.0 / math.sqrt(HD)))
    weights_p = low(jax.nn.softmax(scores, axis=-1))
    attended = jnp.einsum('hcqk,hckd->hcqd', weights_p, grouped[:, :, :, 2], precision=highest)
    restored = jax.vmap(by_rows)(attended.reshape(head_count, seq_len, HD), inverse)
    return jnp.moveaxis(restored, 0, 1)

def forward(tokens, cluster_order, w_qkv, w_out, w_up, w_down, norm_params):
    weight_qkv = low(w_qkv)
    weight_out = low(w_out)
    weight_up = low(w_up)
    weight_down = low(w_down)
    projected = low(low_back(jnp.einsum('td,kdhe->tkhe', tokens, weight_qkv, precision=highest)))
    attended = low(low_back(attention(projected, cluster_order)))
    attn_rows = low_back(jnp.einsum('the,hed->td', attended, weight_out, precision=highest))
    hidden = layer_norm(tokens + attn_rows, norm_params[0], norm_params[1])
    inner_pre = low_back(jnp.dot(low(hidden), weight_up, precision=highest))
    branch = low_back(jnp.dot(low(gelu_value(inner_pre)), weight_down, precision=highest))
    return layer_norm(hidden + branch, norm_params[2], norm_params[3])

def gram_qkv(matrix):
    return jnp.einsum('kdhe,kfhe->df', matrix, matrix, precision=highest)

def gram_out(matrix):
    return jnp.einsum('hed,hef->df', matrix, matrix, precision=highest)

def gram_up(matrix):
    return jnp.einsum('dn,fn->df', matrix, matrix, precision=highest)

def gram_down(matrix):
    return jnp.einsum('nd,nf->df', matrix, matrix, precision=highest)

def apply_qkv(mixing, matrix):
    return jnp.einsum('df,kfhe->kdhe', mixing, matrix, precision=highest)

def apply_out(mixing, matrix):
    return jnp.einsum('hef,fd->hed', matrix, mixing, precision=highest)

def apply_up(mixing, matrix):
    return jnp.dot(mixing, matrix, precision=highest)

def apply_down(mixing, matrix):
    return jnp.dot(matrix, mixing, precision=highest)

def newton_schulz(moment, gram_fn, apply_fn):
    magnitude = jnp.sqrt(jnp.sum(moment * moment))
    iterate = moment / (magnitude + 1e-07)
    for iteration in range(NS_STEPS):
        gram_now = gram_fn(iterate)
        mixing = schulz_coeffs[1] * gram_now + schulz_coeffs[2] * jnp.dot(gram_now, gram_now, precision=highest)
        iterate = schulz_coeffs[0] * iterate + apply_fn(mixing, iterate)
    return iterate

def reference(block_in, block_cot, cluster_perm, w_qkv, w_out, w_up, w_down, mom_qkv, mom_out, mom_up, mom_down, norm_params, norm_first, norm_second):
    seq_count = cluster_perm.shape[0]
    seq_len = cluster_perm.shape[2]
    tokens = block_in.astype(jnp.float32).reshape(seq_count, seq_len, D)
    cotangents = block_cot.astype(jnp.float32).reshape(seq_count, seq_len, D)
    weights = (w_qkv, w_out, w_up, w_down, norm_params)

    def one_sequence(running, item):
        seq_tokens, seq_cot, seq_order = item

        def local(inputs, weight_qkv, weight_out, weight_up, weight_down, norms):
            return forward(inputs, seq_order, weight_qkv, weight_out, weight_up, weight_down, norms)
        result, pullback = jax.vjp(local, seq_tokens, w_qkv, w_out, w_up, w_down, norm_params)
        grads = pullback(seq_cot)
        running = tuple((before + added for before, added in zip(running, grads[1:])))
        return (running, (result.astype(jnp.bfloat16), grads[0]))
    zeros = tuple((jnp.zeros_like(weight) for weight in weights))
    running, (outputs, input_grads) = lax.scan(one_sequence, zeros, (tokens, cotangents, cluster_perm))
    grad_qkv, grad_out, grad_up, grad_down, grad_norm = running
    block_out = outputs.reshape(seq_count * seq_len, D)
    input_grad = input_grads.reshape(seq_count * seq_len, D)
    early_half = (cluster_perm < seq_len // 2).astype(jnp.float32)
    early_half = early_half.reshape(seq_count, HEADS, seq_len // CLUSTER, CLUSTER)
    occupancy = lax.optimization_barrier(jnp.sum(early_half, axis=(0, 3))) / CLUSTER
    moment_qkv = 0.5 * mom_qkv + grad_qkv
    moment_out = 0.5 * mom_out + grad_out
    moment_up = 0.5 * mom_up + grad_up
    moment_down = 0.5 * mom_down + grad_down
    step_rates = (0.5 * math.sqrt(3.0), 0.5 * math.sqrt(CLUSTER / 3.0), 0.5 * math.sqrt(FF / D), 0.5)
    master_qkv = w_qkv - step_rates[0] * newton_schulz(moment_qkv, gram_qkv, apply_qkv)
    master_out = w_out - step_rates[1] * newton_schulz(moment_out, gram_out, apply_out)
    master_up = w_up - step_rates[2] * newton_schulz(moment_up, gram_up, apply_up)
    master_down = w_down - step_rates[3] * newton_schulz(moment_down, gram_down, apply_down)
    first_fix = 1.0 - 0.9 ** ADAM_STEP
    second_fix = 1.0 - 0.999 ** ADAM_STEP
    first_new = 0.9 * norm_first + 0.1 * grad_norm
    second_new = 0.999 * norm_second + 0.001 * grad_norm * grad_norm
    first_hat = first_new / first_fix
    second_hat = second_new / second_fix
    norm_new = norm_params - 0.5 * (first_hat / (jnp.sqrt(second_hat) + 1e-08) + 0.01 * norm_params)
    return (block_out, input_grad, grad_qkv, grad_out, grad_up, grad_down, grad_norm, moment_qkv, moment_out, moment_up, moment_down, master_qkv, master_out, master_up, master_down, first_new, second_new, norm_new, occupancy)
```

```python
import math

import jax
import jax.numpy as jnp
from jax import lax
from jax.experimental import pallas as pl
from jax.experimental.pallas import tpu as pltpu
from jax.sharding import PartitionSpec as P

D = 768
HD = 64
FF = 3072
CLUSTER = 128
NS_STEPS = 3
ADAM_STEP = 10

schulz_coeffs = (3.4445, -4.775, 2.0315)
norm_epsilon = 1e-05
low = jnp.bfloat16
full = jnp.float32
LANES = 128
GROUP = 8
UNROLL = 32
score_scale = 1.0 / math.sqrt(HD)


def contract(left, right, left_axis, right_axis):
    return lax.dot_general(
        left, right, (((left_axis,), (right_axis,)), ((), ())), preferred_element_type=full
    )


def swap(value, axis, bit):
    size = lax.axis_size(axis)
    return lax.ppermute(value, axis, [(place, place ^ bit) for place in range(size)])


def seq_bits():
    bits = []
    bit = lax.axis_size("seq") // 2
    while bit >= 1:
        bits.append(bit)
        bit //= 2
    return bits


def seq_stages():
    return [("seq", bit) for bit in seq_bits()]


def all_stages():
    far = [("seq", bit) for bit in seq_bits() if bit > 1]
    return far + [("ffn", 2), ("seq", 1), ("ffn", 1)]


def spread(shard, stages):
    for axis, bit in stages:
        shard = jnp.concatenate([shard, swap(shard, axis, bit)], axis=0)
    return shard


def fold(partial, stages):
    for axis, bit in reversed(stages):
        half = partial.shape[0] // 2
        kept = partial[:half]
        other = swap(partial[half:].astype(low), axis, bit)
        partial = kept.astype(full) + other.astype(full)
    return partial


def total(value, stages):
    for axis, bit in stages:
        value = value + swap(value, axis, bit)
    return value


def total_halves(value, stages):
    sides = [(lax.axis_index(axis) & bit) != 0 for axis, bit in stages]
    for (axis, bit), side in reversed(list(zip(stages, sides))):
        half = value.shape[0] // 2
        kept = jnp.where(side, value[half:], value[:half])
        sent = jnp.where(side, value[:half], value[half:]).astype(low)
        value = kept.astype(full) + swap(sent, axis, bit).astype(full)
    value = value.astype(low)
    for (axis, bit), side in zip(stages, sides):
        other = swap(value, axis, bit)
        value = jnp.concatenate([jnp.where(side, other, value), jnp.where(side, value, other)], axis=0)
    return value.astype(full)


def move_rows(perm_ref, base, count, move):
    def step(turn, carry):
        for inner in range(UNROLL):
            row = turn * UNROLL + inner
            move(perm_ref[0, 0, base + row], row)
        return carry

    lax.fori_loop(0, count // UNROLL, step, 0)


def softmax_rows(scores):
    peak = jnp.max(scores, axis=1, keepdims=True)
    powers = jnp.exp((scores - peak) * score_scale)
    return powers * (1.0 / jnp.sum(powers, axis=1, keepdims=True))


def left_half(rows):
    return lax.broadcasted_iota(jnp.int32, (rows, LANES), 1) < HD


def attend_kernel(
    perm_ref, x0, x1, x2, x3, w_ref, out_ref, qv_ref, key_ref, qv_rows, key_rows, qv_got, key_got, o_got, o_rows
):
    head = pl.program_id(0)
    here = x0.shape[0]
    seq_len = 4 * here
    half = here // 2
    for block, x_ref in enumerate((x0, x1, x2, x3)):
        for cut in range(2):
            both = contract(x_ref[pl.ds(cut * half, half), :], w_ref[...], 1, 1)
            rows = pl.ds(block * here + cut * half, half)
            qv_rows[rows, :] = both[:, :LANES]
            key_rows[rows, :] = both[:, LANES:]
    count = GROUP * CLUSTER

    def group(turn, carry):
        base = turn * count

        def fetch(index, row):
            qv_got[pl.ds(row, 1), :] = qv_rows[pl.ds(index, 1), :]
            key_got[pl.ds(row, 1), :] = key_rows[pl.ds(index, 1), :]

        move_rows(perm_ref, base, count, fetch)
        spans = [slice(part * CLUSTER, (part + 1) * CLUSTER) for part in range(GROUP)]
        qvs = [qv_got[span].astype(low) for span in spans]
        keys = [key_got[span].astype(low) for span in spans]
        for part in range(GROUP):
            rows = pl.ds(base + part * CLUSTER, CLUSTER)
            qv_ref[0, rows, :] = qvs[part]
            key_ref[0, rows, :] = keys[part]
        scores = [contract(qv, key, 1, 1) for qv, key in zip(qvs, keys)]
        probs = [softmax_rows(score).astype(low) for score in scores]
        for part in range(GROUP):
            o_got[spans[part]] = contract(probs[part], qvs[part], 1, 0)

        def place(index, row):
            o_rows[pl.ds(index, 1), :] = o_got[pl.ds(row, 1), :]

        move_rows(perm_ref, base, count, place)
        return carry

    lax.fori_loop(0, seq_len // count, group, 0)

    @pl.when(head == 0)
    def _():
        for block in range(4):
            out_ref[block, pl.ds(0, here), :] = o_rows[pl.ds(block * here, here), :].astype(low)

    @pl.when(head == 1)
    def _():
        for block in range(4):
            turned = pltpu.roll(o_rows[pl.ds(block * here, here), :], HD, 1).astype(low)
            before = out_ref[block, pl.ds(0, here), :]
            out_ref[block, pl.ds(0, here), :] = jnp.where(left_half(here), turned, before)

    @pl.when(head == 2)
    def _():
        for block in range(4):
            top = pltpu.roll(o_rows[pl.ds(block * here, half), :], HD, 1)
            bottom = o_rows[pl.ds(block * here + half, half), :]
            out_ref[block, pl.ds(here, half), :] = jnp.where(left_half(half), top, bottom).astype(low)


def attend(perm, tokens, weights):
    heads, seq_len = perm.shape
    here = tokens[0].shape[0]
    whole = pl.BlockSpec((here, D), lambda head: (0, 0), pipeline_mode=pl.Buffered(1))
    per_head = pl.BlockSpec((1, seq_len, LANES), lambda head: (head, 0, 0))
    return pl.pallas_call(
        attend_kernel,
        grid=(heads,),
        in_specs=[
            pl.BlockSpec((1, 1, seq_len), lambda head: (head, 0, 0), memory_space=pltpu.SMEM),
            whole,
            whole,
            whole,
            whole,
            pl.BlockSpec((2 * LANES, D), lambda head: (head, 0)),
        ],
        out_specs=[
            pl.BlockSpec((4, here + here // 2, LANES), lambda head: (0, 0, 0), pipeline_mode=pl.Buffered(1)),
            per_head,
            per_head,
        ],
        out_shape=[
            jax.ShapeDtypeStruct((4, here + here // 2, LANES), low),
            jax.ShapeDtypeStruct((heads, seq_len, LANES), low),
            jax.ShapeDtypeStruct((heads, seq_len, LANES), low),
        ],
        scratch_shapes=[
            pltpu.VMEM((seq_len, LANES), full),
            pltpu.VMEM((seq_len, LANES), full),
            pltpu.VMEM((GROUP * CLUSTER, LANES), full),
            pltpu.VMEM((GROUP * CLUSTER, LANES), full),
            pltpu.VMEM((GROUP * CLUSTER, LANES), full),
            pltpu.VMEM((seq_len, LANES), full),
        ],
        compiler_params=pltpu.CompilerParams(vmem_limit_bytes=52 * 2**20),
        cost_estimate=pl.CostEstimate(
            flops=2 * heads * seq_len * (2 * LANES * D + 2 * LANES * LANES),
            bytes_accessed=30 * 2**20,
            transcendentals=heads * seq_len * CLUSTER,
        ),
        name="attend",
    )(perm.reshape(heads, 1, seq_len), *tokens, weights)


def attend_back_kernel(
    perm_ref, qv_ref, key_ref, do_ref, x0, x1, x2, x3, w_ref, gw_ref, gx_ref, d_rows, d_got, dqv_got, dkey_got, dqv_rows, dkey_rows, gx_sum
):
    head = pl.program_id(0)
    here = x0.shape[0]
    seq_len = 4 * here
    half = here // 2

    @pl.when(head == 0)
    def _():
        for block in range(4):
            rows = do_ref[block, pl.ds(0, here), :].astype(full)
            d_rows[pl.ds(block * here, here), :] = jnp.where(left_half(here), 0.0, rows)

    @pl.when(head == 1)
    def _():
        for block in range(4):
            rows = pltpu.roll(do_ref[block, pl.ds(0, here), :].astype(full), HD, 1)
            d_rows[pl.ds(block * here, here), :] = jnp.where(left_half(here), 0.0, rows)

    @pl.when(head == 2)
    def _():
        for block in range(4):
            rows = do_ref[block, pl.ds(here, half), :].astype(full)
            top = pltpu.roll(rows, HD, 1)
            d_rows[pl.ds(block * here, half), :] = jnp.where(left_half(half), 0.0, top)
            d_rows[pl.ds(block * here + half, half), :] = jnp.where(left_half(half), 0.0, rows)

    count = GROUP * CLUSTER

    def group(turn, carry):
        base = turn * count

        def fetch(index, row):
            d_got[pl.ds(row, 1), :] = d_rows[pl.ds(index, 1), :]

        move_rows(perm_ref, base, count, fetch)
        spans = [slice(part * CLUSTER, (part + 1) * CLUSTER) for part in range(GROUP)]
        rows = [pl.ds(base + part * CLUSTER, CLUSTER) for part in range(GROUP)]
        qvs = [qv_ref[0, span, :] for span in rows]
        keys = [key_ref[0, span, :] for span in rows]
        dos = [d_got[span].astype(low) for span in spans]
        scores = [contract(qv, key, 1, 1) for qv, key in zip(qvs, keys)]
        dprobs = [contract(do, qv, 1, 1) for do, qv in zip(dos, qvs)]
        probs = [softmax_rows(score) for score in scores]
        probs_low = [prob.astype(low) for prob in probs]
        dscores = [
            (prob * (dprob - jnp.sum(prob * dprob, axis=1, keepdims=True))).astype(low)
            for prob, dprob in zip(probs, dprobs)
        ]
        for part in range(GROUP):
            dqv_got[spans[part]] = score_scale * contract(dscores[part], keys[part], 1, 0) + contract(
                probs_low[part], dos[part], 0, 0
            )
            dkey_got[spans[part]] = score_scale * contract(dscores[part], qvs[part], 0, 0)

        def place(index, row):
            dqv_rows[pl.ds(index, 1), :] = dqv_got[pl.ds(row, 1), :]
            dkey_rows[pl.ds(index, 1), :] = dkey_got[pl.ds(row, 1), :]

        move_rows(perm_ref, base, count, place)
        return carry

    lax.fori_loop(0, seq_len // count, group, 0)

    gw = jnp.zeros((2 * LANES, D), full)
    for block, x_ref in enumerate((x0, x1, x2, x3)):
        slot = (0, 2, 1, 3)[block]
        rows = pl.ds(block * here, here)
        dboth = jnp.concatenate([dqv_rows[rows, :].astype(low), dkey_rows[rows, :].astype(low)], axis=1)
        gw = gw + contract(dboth, x_ref[...], 0, 0)
        for cut in range(4):
            part = here // 4
            piece = contract(dboth[cut * part : (cut + 1) * part], w_ref[...], 1, 0)
            at = pl.ds(cut * part, part)

            @pl.when(head == 0)
            def _():
                gx_sum[slot, at, :] = piece

            @pl.when(head == 1)
            def _():
                gx_sum[slot, at, :] += piece

            @pl.when(head == 2)
            def _():
                gx_ref[slot, at, :] = (gx_sum[slot, at, :] + piece).astype(low)

    gw_ref[...] = gw.astype(low)


def attend_back(perm, qv, key, do, tokens, weights):
    heads, seq_len = perm.shape
    here = tokens[0].shape[0]
    whole = pl.BlockSpec((here, D), lambda head: (0, 0), pipeline_mode=pl.Buffered(1))
    per_head = pl.BlockSpec((1, seq_len, LANES), lambda head: (head, 0, 0))
    rows_got = pltpu.VMEM((GROUP * CLUSTER, LANES), full)
    rows_all = pltpu.VMEM((seq_len, LANES), full)
    return pl.pallas_call(
        attend_back_kernel,
        grid=(heads,),
        in_specs=[
            pl.BlockSpec((1, 1, seq_len), lambda head: (head, 0, 0), memory_space=pltpu.SMEM),
            per_head,
            per_head,
            pl.BlockSpec((4, here + here // 2, LANES), lambda head: (0, 0, 0), pipeline_mode=pl.Buffered(1)),
            whole,
            whole,
            whole,
            whole,
            pl.BlockSpec((2 * LANES, D), lambda head: (head, 0)),
        ],
        out_specs=[
            pl.BlockSpec((2 * LANES, D), lambda head: (head, 0)),
            pl.BlockSpec((4, here, D), lambda head: (0, 0, 0), pipeline_mode=pl.Buffered(1)),
        ],
        out_shape=[
            jax.ShapeDtypeStruct((heads * 2 * LANES, D), low),
            jax.ShapeDtypeStruct((4, here, D), low),
        ],
        scratch_shapes=[rows_all, rows_got, rows_got, rows_got, rows_all, rows_all, pltpu.VMEM((4, here, D), full)],
        compiler_params=pltpu.CompilerParams(vmem_limit_bytes=60 * 2**20),
        cost_estimate=pl.CostEstimate(
            flops=2 * heads * seq_len * (4 * LANES * D + 5 * LANES * LANES),
            bytes_accessed=30 * 2**20,
            transcendentals=heads * seq_len * CLUSTER,
        ),
        name="attend_back",
    )(perm.reshape(heads, 1, seq_len), qv, key, do, *tokens, weights)


def norm_forward(inputs, gains, biases):
    center = inputs - jnp.mean(inputs, axis=-1, keepdims=True)
    spread_of = jnp.mean(center * center, axis=-1, keepdims=True)
    inv_std = lax.rsqrt(spread_of + norm_epsilon)
    normed = center * inv_std
    return (normed * gains + biases, normed, inv_std)


def norm_backward(upstream, normed, inv_std, gains):
    scaled = upstream * gains
    inside = (
        scaled
        - jnp.mean(scaled, axis=-1, keepdims=True)
        - normed * jnp.mean(scaled * normed, axis=-1, keepdims=True)
    )
    return (inside * inv_std, jnp.sum(upstream * normed, axis=0), jnp.sum(upstream, axis=0))


def gelu_value(preact):
    return preact * 0.5 * (1.0 + jax.scipy.special.erf(preact * 0.7071067811865476))


def gelu_slope(preact):
    cumulative = 0.5 * (1.0 + jax.scipy.special.erf(preact * 0.7071067811865476))
    density = jnp.exp(-0.5 * preact * preact) * 0.3989422804014327
    return cumulative + preact * density


def rows_qkv(value):
    kinds, depth, heads, cut = value.shape
    return value.transpose(0, 2, 3, 1).reshape(kinds * heads * cut, depth)


def unrows_qkv(rows, shape):
    kinds, depth, heads, cut = shape
    return rows.reshape(kinds, heads, cut, depth).transpose(0, 3, 1, 2)


def on_device(
    block_in,
    block_cot,
    cluster_perm,
    w_qkv,
    w_out,
    w_up,
    w_down,
    mom_qkv,
    mom_out,
    mom_up,
    mom_down,
    norm_params,
    norm_first,
    norm_second,
):
    ffn_here = lax.axis_index("ffn")
    seqs = lax.axis_size("seq")
    n_bits = len(seq_bits())
    here = block_in.shape[0]
    half = here // 2
    heads = w_out.shape[0]
    cut = w_out.shape[1]
    seq_len = cluster_perm.shape[2]
    clusters = seq_len // CLUSTER

    weights = [rows_qkv(w_qkv), w_out.reshape(heads * cut, D), w_up.T, w_down]
    momenta = [rows_qkv(mom_qkv), mom_out.reshape(heads * cut, D), mom_up.T, mom_down]

    tokens = [block_in, swap(block_in, "ffn", 1), swap(block_in, "ffn", 2)]
    tokens.append(swap(tokens[2], "ffn", 1))
    wide_qkv = spread(weights[0].astype(low), seq_stages())
    wide_qkv = wide_qkv.reshape(seqs, 3, heads, cut, D).transpose(1, 2, 0, 3, 4).reshape(3, heads, HD, D)
    head_rows = jnp.stack(
        [wide_qkv[0], wide_qkv[2], wide_qkv[1], jnp.zeros_like(wide_qkv[1])], axis=1
    ).reshape(heads * 2 * LANES, D)

    stages = all_stages()
    up_rows = spread(weights[2].astype(low), stages)
    down_rows = spread(weights[3].astype(low), stages)
    out_wide = spread(weights[1].astype(low), stages)

    digits = (2, 2, 2) + (2,) * (n_bits - 1)
    order = (2, 0, 2 + n_bits, 1) + tuple(range(3, 2 + n_bits)) + (3 + n_bits, 4 + n_bits)
    back = tuple(sorted(range(len(order)), key=lambda at: order[at]))
    sizes = digits + (heads, cut, D)
    out_rows = out_wide.reshape(sizes).transpose(order).reshape(4 * heads * HD, D)

    perm = jnp.bitwise_xor(cluster_perm[0], ffn_here * here)
    o_blocks, kept_qv, kept_key = attend(perm, tokens, head_rows)
    got = [o_blocks[0]] + [swap(o_blocks[turn], "ffn", turn) for turn in (1, 2, 3)]
    pieces = []
    for block in got:
        third = jnp.concatenate([block[here:, :HD], block[here:, HD:]], axis=0)
        pieces += [block[:here, HD:], block[:here, :HD], third]
    o_rows = jnp.concatenate(pieces, axis=1)

    residual = block_in.astype(full) + contract(o_rows, out_rows, 1, 0)
    hidden, normed_one, inv_one = norm_forward(residual, norm_params[0], norm_params[1])
    hidden_low = hidden.astype(low)
    inner_pre = contract(hidden_low, up_rows, 1, 1)
    gelu_low = gelu_value(inner_pre).astype(low)
    branch = contract(gelu_low, down_rows, 1, 0)
    output_rows, normed_two, inv_two = norm_forward(hidden + branch, norm_params[2], norm_params[3])
    block_out = output_rows.astype(low)
    upstream = block_cot.astype(full)
    dsum_two, gain_two, bias_two = norm_backward(upstream, normed_two, inv_two, norm_params[2])
    dbranch = dsum_two.astype(low)
    dinner = (contract(dbranch, down_rows, 1, 1) * gelu_slope(inner_pre)).astype(low)
    dhidden = dsum_two + contract(dinner, up_rows, 1, 0)
    dresidual, gain_one, bias_one = norm_backward(dhidden, normed_one, inv_one, norm_params[0])
    dattn = dresidual.astype(low)
    do_rows = contract(dattn, out_rows, 1, 1).astype(low)
    do_blocks = []
    for block in range(4):
        part = do_rows[:, block * heads * HD : (block + 1) * heads * HD]
        pair = jnp.concatenate([part[:, HD : 2 * HD], part[:, :HD]], axis=1)
        third = jnp.concatenate([part[:half, 2 * HD :], part[half:, 2 * HD :]], axis=1)
        do_blocks.append(jnp.concatenate([pair, third], axis=0))
    do_got = jnp.stack([do_blocks[0]] + [swap(do_blocks[turn], "ffn", turn) for turn in (1, 2, 3)])

    part_down = contract(gelu_low, dbranch, 0, 0).astype(low)
    part_up = contract(dinner, hidden_low, 0, 0).astype(low)
    part_out = contract(o_rows, dattn, 0, 0).astype(low)
    part_out = part_out.reshape(tuple(sizes[at] for at in order)).transpose(back)
    part_out = part_out.reshape(4 * heads * HD, D)
    grad_down = fold(part_down, stages)
    grad_up = fold(part_up, stages)
    grad_out = fold(part_out, stages)

    part_qkv, gx_blocks = attend_back(perm, kept_qv, kept_key, do_got, tokens, head_rows)
    part_qkv = part_qkv.reshape(heads, 4, HD, D)
    part_qkv = jnp.stack([part_qkv[:, 0], part_qkv[:, 2], part_qkv[:, 1]])
    part_qkv = part_qkv.reshape(3, heads, seqs, cut, D).transpose(2, 0, 1, 3, 4)
    grad_qkv = fold(part_qkv.reshape(seqs * 3 * heads * cut, D), seq_stages())
    gx = fold(gx_blocks.reshape(4 * here, D), [("ffn", 2), ("ffn", 1)])
    input_grad = dresidual + gx

    early_half = (cluster_perm[0] < seq_len // 2).astype(full).reshape(heads, clusters, CLUSTER)
    share = lax.dynamic_update_slice(
        jnp.zeros((4 * heads, clusters), full), jnp.sum(early_half, axis=2) / CLUSTER, (ffn_here * heads, 0)
    ).reshape(1, 4 * heads * clusters)
    small = jnp.concatenate(
        [jnp.stack([gain_one, bias_one, gain_two, bias_two]), jnp.pad(share, ((0, 0), (0, D - share.shape[1])))]
    )
    small = total(small, seq_stages() + [("ffn", 2), ("ffn", 1)])
    grad_norm = small[:4]
    occupancy = small[4, : 4 * heads * clusters].reshape(4 * heads, clusters)

    grads = [grad_qkv, grad_out, grad_up, grad_down]
    moments = [0.5 * mom + grad for mom, grad in zip(momenta, grads)]
    most = max(moment.shape[0] for moment in moments)
    stack = jnp.stack(
        [jnp.pad(moment.astype(low), ((0, most - moment.shape[0]), (0, 0))) for moment in moments]
    )

    def pick(turn):
        return lax.dynamic_index_in_dim(stack, jnp.bitwise_xor(ffn_here, turn), keepdims=False)

    matrix = jnp.concatenate([pick(0)] + [swap(pick(turn), "ffn", turn) for turn in (1, 2, 3)], axis=0)
    gram = total_halves(contract(matrix, matrix, 0, 0), seq_stages())
    diag = jnp.where(jnp.eye(D, dtype=bool), gram, 0.0)
    shrink = 1.0 / (jnp.sqrt(jnp.sum(diag)) + 1e-07)
    gram = gram * (shrink * shrink)
    iterate = matrix.astype(full) * shrink
    one, two, three = schulz_coeffs
    for step in range(NS_STEPS):
        gram_low = gram.astype(low)
        mixing = two * gram + three * contract(gram_low, gram_low, 1, 0)
        mixing_low = mixing.astype(low)
        iterate = one * iterate + contract(iterate.astype(low), mixing_low, 1, 0)
        if step < NS_STEPS - 1:
            once = contract(mixing_low, gram_low, 1, 0)
            gram = one * one * gram + 2.0 * one * once + contract(once.astype(low), mixing_low, 1, 0)
    steps = iterate.astype(low).reshape(4, most, D)
    home = jnp.stack([steps[0]] + [swap(steps[turn], "ffn", turn) for turn in (1, 2, 3)])
    step_rates = (
        0.5 * math.sqrt(3.0),
        0.5 * math.sqrt(CLUSTER / 3.0),
        0.5 * math.sqrt(FF / D),
        0.5,
    )
    masters = []
    for member in range(4):
        own = lax.dynamic_index_in_dim(home, jnp.bitwise_xor(ffn_here, member), keepdims=False)
        own = own[: moments[member].shape[0]].astype(full)
        masters.append(weights[member] - step_rates[member] * own)

    first_fix = 1.0 - 0.9**ADAM_STEP
    second_fix = 1.0 - 0.999**ADAM_STEP
    first_new = 0.9 * norm_first + 0.1 * grad_norm
    second_new = 0.999 * norm_second + 0.001 * grad_norm * grad_norm
    first_hat = first_new / first_fix
    second_hat = second_new / second_fix
    norm_new = norm_params - 0.5 * (first_hat / (jnp.sqrt(second_hat) + 1e-08) + 0.01 * norm_params)

    def shaped(four):
        return (unrows_qkv(four[0], w_qkv.shape), four[1].reshape(w_out.shape), four[2].T, four[3])

    return (
        (block_out, input_grad)
        + shaped(grads)
        + (grad_norm,)
        + shaped(moments)
        + shaped(masters)
        + (first_new, second_new, norm_new, occupancy)
    )


def solution(mesh):
    rows = P(("seq", "ffn"), None)
    placed = (
        rows,
        rows,
        P("seq", "ffn", None),
        P(None, None, "ffn", "seq"),
        P("ffn", "seq", None),
        P(None, ("seq", "ffn")),
        rows,
        P(None, None, "ffn", "seq"),
        P("ffn", "seq", None),
        P(None, ("seq", "ffn")),
        rows,
        P(),
        P(),
        P(),
    )
    four = placed[3:7]
    return jax.shard_map(
        on_device,
        mesh=mesh,
        in_specs=placed,
        out_specs=(rows, rows) + four + (P(),) + four + four + (P(), P(), P(), P()),
        check_vma=False,
    )
```

```python
import math

import jax
import jax.numpy as jnp
from jax import lax
from jax.experimental import pallas as pl
from jax.experimental.pallas import tpu as pltpu
from jax.sharding import PartitionSpec as P

D = 768
HD = 64
FF = 3072
CLUSTER = 128
NS_STEPS = 3
ADAM_STEP = 10

schulz_coeffs = (3.4445, -4.775, 2.0315)
norm_epsilon = 1e-05
low = jnp.bfloat16
full = jnp.float32
LANES = 128
GROUP = 8
UNROLL = 32
score_scale = 1.0 / math.sqrt(HD)


def contract(left, right, left_axis, right_axis):
    return lax.dot_general(
        left, right, (((left_axis,), (right_axis,)), ((), ())), preferred_element_type=full
    )


def swap(value, axis, bit):
    size = lax.axis_size(axis)
    return lax.ppermute(value, axis, [(place, place ^ bit) for place in range(size)])


def seq_bits():
    bits = []
    bit = lax.axis_size("seq") // 2
    while bit >= 1:
        bits.append(bit)
        bit //= 2
    return bits


def seq_stages():
    return [("seq", bit) for bit in seq_bits()]


def far_stages():
    return [("seq", bit) for bit in seq_bits() if bit > 1]


def spread(shard, stages):
    for axis, bit in stages:
        shard = jnp.concatenate([shard, swap(shard, axis, bit)], axis=0)
    return shard


def fold(partial, stages):
    for axis, bit in reversed(stages):
        half = partial.shape[0] // 2
        kept = partial[:half]
        other = swap(partial[half:].astype(low), axis, bit)
        partial = kept.astype(full) + other.astype(full)
    return partial


def after(values, *tokens):
    return lax.optimization_barrier((values, tokens))[0]


def join_inner(near, other):
    rows = near.shape[0] // 2
    return jnp.concatenate([near[:rows], other[:rows], near[rows:], other[rows:]], axis=0)


def cut_outer(value):
    half = value.shape[0] // 2
    return value[:half], value[half:]


def cut_inner(value):
    rows = value.shape[0] // 4
    quarters = [value[part * rows : (part + 1) * rows] for part in range(4)]
    return tuple(jnp.concatenate(quarters[side::2], axis=0) for side in range(2))


def add_low(kept, other):
    return (kept.astype(full) + other.astype(full)).astype(low)


def fold_step(value, cut, axis, bit):
    kept, sent = cut(value)
    return add_low(kept, swap(sent, axis, bit))


def send_on(near, far_got):
    return swap(jnp.concatenate([near, far_got], axis=0), "ffn", 1)


def sides_of(stages):
    return [(axis, bit, (lax.axis_index(axis) & bit) != 0) for axis, bit in stages]


def sum_halves(value, stages):
    for axis, bit, side in reversed(sides_of(stages)):
        half = value.shape[0] // 2
        kept = jnp.where(side, value[half:], value[:half])
        sent = jnp.where(side, value[:half], value[half:]).astype(low)
        value = kept.astype(full) + swap(sent, axis, bit).astype(full)
    return value.astype(low)


def spread_halves(value, stages):
    for axis, bit, side in sides_of(stages):
        other = swap(value, axis, bit)
        value = jnp.concatenate([jnp.where(side, other, value), jnp.where(side, value, other)], axis=0)
    return value


def move_rows(perm_ref, head, base, count, move):
    def step(turn, carry):
        for inner in range(UNROLL):
            row = turn * UNROLL + inner
            move(perm_ref[head, base + row], row)
        return carry

    lax.fori_loop(0, count // UNROLL, step, 0)


def softmax_rows(scores):
    peak = jnp.max(scores, axis=1, keepdims=True)
    powers = jnp.exp((scores - peak) * score_scale)
    return powers * (1.0 / jnp.sum(powers, axis=1, keepdims=True))


def left_half(rows):
    return lax.broadcasted_iota(jnp.int32, (rows, LANES), 1) < HD


def attend_kernel(
    perm_ref, x0, x1, x2, x3, w_ref, own_ref, near_ref, far_ref, qv_ref, key_ref, qv_rows, key_rows, qv_got, key_got, o_got, o_rows
):
    here = x0.shape[0]
    seq_len = 4 * here
    half = here // 2
    for block, x_ref in enumerate((x0, x1, x2, x3)):
        for cut in range(2):
            both = contract(x_ref[pl.ds(cut * half, half), :], w_ref[...], 1, 1)
            rows = pl.ds(block * here + cut * half, half)
            qv_rows[rows, :] = both[:, :LANES]
            key_rows[rows, :] = both[:, LANES:]
    count = GROUP * CLUSTER

    def group(turn, carry):
        base = turn * count

        def fetch(index, row):
            qv_got[pl.ds(row, 1), :] = qv_rows[pl.ds(index, 1), :]
            key_got[pl.ds(row, 1), :] = key_rows[pl.ds(index, 1), :]

        move_rows(perm_ref, 0, base, count, fetch)
        spans = [slice(part * CLUSTER, (part + 1) * CLUSTER) for part in range(GROUP)]
        qvs = [qv_got[span].astype(low) for span in spans]
        keys = [key_got[span].astype(low) for span in spans]
        for part in range(GROUP):
            rows = pl.ds(base + part * CLUSTER, CLUSTER)
            qv_ref[rows, :] = qvs[part]
            key_ref[rows, :] = keys[part]
        scores = [contract(qv, key, 1, 1) for qv, key in zip(qvs, keys)]
        probs = [softmax_rows(score).astype(low) for score in scores]
        for part in range(GROUP):
            o_got[spans[part]] = contract(probs[part], qvs[part], 1, 0)

        def place(index, row):
            o_rows[pl.ds(index, 1), :] = o_got[pl.ds(row, 1), :]

        move_rows(perm_ref, 0, base, count, place)
        return carry

    lax.fori_loop(0, seq_len // count, group, 0)
    outs = (own_ref, near_ref, far_ref.at[pl.ds(0, half), :], far_ref.at[pl.ds(half, half), :])
    for block, out_ref in enumerate(outs):
        top = pltpu.roll(o_rows[pl.ds(block * here, half), :], HD, 1)
        bottom = o_rows[pl.ds(block * here + half, half), :]
        out_ref[...] = jnp.where(left_half(half), top, bottom).astype(low)


def vmem(*shape):
    return pl.BlockSpec(shape, memory_space=pltpu.VMEM)


def attend(perm, tokens, weights, name):
    seq_len = perm.shape[1]
    here = tokens[0].shape[0]
    rows_got = pltpu.VMEM((GROUP * CLUSTER, LANES), full)
    rows_all = pltpu.VMEM((seq_len, LANES), full)
    in_vmem = pl.BlockSpec(memory_space=pltpu.VMEM)
    return pl.pallas_call(
        attend_kernel,
        in_specs=[pl.BlockSpec(memory_space=pltpu.SMEM)] + [in_vmem] * 5,
        out_specs=[in_vmem] * 5,
        out_shape=[
            jax.ShapeDtypeStruct((here // 2, LANES), low),
            jax.ShapeDtypeStruct((here // 2, LANES), low),
            jax.ShapeDtypeStruct((here, LANES), low),
            jax.ShapeDtypeStruct((seq_len, LANES), low),
            jax.ShapeDtypeStruct((seq_len, LANES), low),
        ],
        scratch_shapes=[rows_all, rows_all, rows_got, rows_got, rows_got, rows_all],
        compiler_params=pltpu.CompilerParams(vmem_limit_bytes=40 * 2**20),
        cost_estimate=pl.CostEstimate(flops=18 * 10**9, bytes_accessed=1000, transcendentals=0),
        name=name,
    )(perm, *tokens, weights)


def attend_back_kernel(heads, *refs):
    perm_ref = refs[0]
    per_head = [refs[1 + 6 * head : 7 + 6 * head] for head in range(heads)]
    x_refs = refs[1 + 6 * heads : 5 + 6 * heads]
    outs = refs[5 + 6 * heads : 5 + 8 * heads]
    d_rows, d_got, dqv_got, dkey_got, dqv_rows, dkey_rows = refs[5 + 8 * heads :]
    here = x_refs[0].shape[0]
    seq_len = 4 * here
    half = here // 2
    count = GROUP * CLUSTER
    for head in range(heads):
        qv_ref, key_ref, *do_refs = per_head[head]
        gw_ref, dboth_ref = outs[2 * head : 2 * head + 2]
        for block, do_ref in enumerate(do_refs):
            rows = do_ref[...].astype(full)
            top = pltpu.roll(rows, HD, 1)
            d_rows[pl.ds(block * here, half), :] = jnp.where(left_half(half), 0.0, top)
            d_rows[pl.ds(block * here + half, half), :] = jnp.where(left_half(half), 0.0, rows)

        def group(turn, carry):
            base = turn * count

            def fetch(index, row):
                d_got[pl.ds(row, 1), :] = d_rows[pl.ds(index, 1), :]

            move_rows(perm_ref, head, base, count, fetch)
            spans = [slice(part * CLUSTER, (part + 1) * CLUSTER) for part in range(GROUP)]
            rows = [pl.ds(base + part * CLUSTER, CLUSTER) for part in range(GROUP)]
            qvs = [qv_ref[span, :] for span in rows]
            keys = [key_ref[span, :] for span in rows]
            dos = [d_got[span].astype(low) for span in spans]
            scores = [contract(qv, key, 1, 1) for qv, key in zip(qvs, keys)]
            dprobs = [contract(do, qv, 1, 1) for do, qv in zip(dos, qvs)]
            probs = [softmax_rows(score) for score in scores]
            probs_low = [prob.astype(low) for prob in probs]
            dscores = [
                (prob * (dprob - jnp.sum(prob * dprob, axis=1, keepdims=True))).astype(low)
                for prob, dprob in zip(probs, dprobs)
            ]
            for part in range(GROUP):
                dqv_got[spans[part]] = score_scale * contract(dscores[part], keys[part], 1, 0) + contract(
                    probs_low[part], dos[part], 0, 0
                )
                dkey_got[spans[part]] = score_scale * contract(dscores[part], qvs[part], 0, 0)

            def place(index, row):
                dqv_rows[pl.ds(index, 1), :] = dqv_got[pl.ds(row, 1), :]
                dkey_rows[pl.ds(index, 1), :] = dkey_got[pl.ds(row, 1), :]

            move_rows(perm_ref, head, base, count, place)
            return carry

        lax.fori_loop(0, seq_len // count, group, 0)

        gw = jnp.zeros((2 * LANES, D), full)
        for block, x_ref in enumerate(x_refs):
            rows = pl.ds(block * here, here)
            dboth_ref[rows, :LANES] = dqv_rows[rows, :].astype(low)
            dboth_ref[rows, LANES:] = dkey_rows[rows, :].astype(low)
            gw = gw + contract(dboth_ref[rows, :], x_ref[...], 0, 0)
        gw_ref[...] = gw.astype(low)


def attend_back(perm, head, kept, do, tokens):
    seq_len = perm.shape[1]
    here = tokens[0].shape[0]
    half = here // 2
    rows_got = pltpu.VMEM((GROUP * CLUSTER, LANES), full)
    rows_all = pltpu.VMEM((seq_len, LANES), full)
    in_vmem = pl.BlockSpec(memory_space=pltpu.VMEM)
    own, near, far = do

    def part(turn):
        return pl.BlockSpec((None, None, half, LANES), lambda step: (turn, head, 0, 0))

    return pl.pallas_call(
        lambda *refs: attend_back_kernel(1, *refs),
        grid=(1,),
        in_specs=[pl.BlockSpec(memory_space=pltpu.SMEM)]
        + [in_vmem] * 2
        + [part(0), part(0), part(0), part(1)]
        + [in_vmem] * 4,
        out_specs=[in_vmem] * 2,
        out_shape=[
            jax.ShapeDtypeStruct((2 * LANES, D), low),
            jax.ShapeDtypeStruct((seq_len, 2 * LANES), low),
        ],
        scratch_shapes=[rows_all, rows_got, rows_got, rows_got, rows_all, rows_all],
        compiler_params=pltpu.CompilerParams(vmem_limit_bytes=40 * 2**20),
        cost_estimate=pl.CostEstimate(flops=22 * 10**9, bytes_accessed=1000, transcendentals=0),
        name="attend_back",
    )(perm, *kept, own, near, far, near, *tokens)


def token_grad_kernel(d0, d1, d2, w_ref, kept_ref, sent_ref):
    sums = None
    for head, d_ref in enumerate((d0, d1, d2)):
        piece = contract(d_ref[...], w_ref[pl.ds(head * 2 * LANES, 2 * LANES), :], 1, 0)
        sums = piece if sums is None else sums + piece

    @pl.when(pl.program_id(0) < 2)
    def _():
        sent_ref[...] = sums.astype(low)

    @pl.when(pl.program_id(0) >= 2)
    def _():
        kept_ref[...] = sums.astype(low)


def token_grad(dboth, weights, here):
    split = 2
    rows = here // split

    def from_block(slot, part):
        return ((2 * (slot % 2) + 1 - slot // 2) * split + part, 0)

    def to_sent(slot, part):
        return (jnp.minimum(slot * split + part, 2 * split - 1), 0)

    def to_kept(slot, part):
        return (jnp.maximum(slot * split + part - 2 * split, 0), 0)

    return pl.pallas_call(
        token_grad_kernel,
        grid=(4, split),
        in_specs=[pl.BlockSpec((rows, 2 * LANES), from_block)] * 3
        + [pl.BlockSpec((6 * LANES, D), lambda slot, part: (0, 0))],
        out_specs=[pl.BlockSpec((rows, D), to_kept), pl.BlockSpec((rows, D), to_sent)],
        out_shape=[jax.ShapeDtypeStruct((2 * here, D), low)] * 2,
        compiler_params=pltpu.CompilerParams(vmem_limit_bytes=32 * 2**20),
        cost_estimate=pl.CostEstimate(flops=8 * 10**9, bytes_accessed=1000, transcendentals=0),
        name="token_grad",
    )(*dboth, weights)


def row_mean(value):
    return jnp.mean(value, axis=-1, keepdims=True)


def norm_forward(inputs, gains, biases):
    center = inputs - row_mean(inputs)
    inv_std = lax.rsqrt(row_mean(center * center) + norm_epsilon)
    normed = center * inv_std
    return (normed * gains + biases, normed, inv_std)


def norm_backward(upstream, normed, inv_std, gains):
    scaled = upstream * gains
    inside = scaled - row_mean(scaled) - normed * row_mean(scaled * normed)
    sums = [jnp.sum(upstream * normed, axis=0, keepdims=True), jnp.sum(upstream, axis=0, keepdims=True)]
    return (inside * inv_std, sums)


def layer_kernel(heads, *refs):
    o_refs = refs[: 4 * heads]
    (x_ref, cot_ref, wo_ref, norm_ref) = refs[4 * heads : 4 * heads + 4]
    up_refs = refs[4 * heads + 4 : 4 * heads + 8]
    down_refs = refs[4 * heads + 8 : 4 * heads + 12]
    outs = refs[4 * heads + 12 :]
    (do_own, do_near, do_far, block_ref, da_ref) = outs[:5]
    do_refs = (do_own.at[0], do_near.at[0], do_far.at[0], do_far.at[1])
    g_refs = outs[5:7]
    du_refs = outs[7:9]
    (df_ref, hb_ref, dattn_ref, o_ref, sums_ref, slope_ref) = outs[9:]
    part = x_ref.shape[1]
    rows = 2 * part
    left = left_half(part)

    def load(ref):
        return jnp.concatenate([ref[0], ref[1]], axis=0)

    def store(ref, value):
        ref[0] = value[:part]
        ref[1] = value[part:]

    packed = []
    for turn in range(4):
        for head in range(heads):
            packed.append(o_refs[4 * head + turn][...].astype(full))
    for pair in range(len(packed) // 2):
        first, second = packed[2 * pair], packed[2 * pair + 1]
        lanes = slice(pair * LANES, (pair + 1) * LANES)
        o_ref[0, :, lanes] = jnp.where(left, first, pltpu.roll(second, HD, 1)).astype(low)
        o_ref[1, :, lanes] = jnp.where(left, pltpu.roll(first, HD, 1), second).astype(low)

    gain_a, bias_a = norm_ref[0:1, :], norm_ref[1:2, :]
    gain_b, bias_b = norm_ref[2:3, :], norm_ref[3:4, :]
    residual = load(x_ref).astype(full) + contract(load(o_ref), wo_ref[...], 1, 0)
    hidden, normed_a, inv_a = norm_forward(residual, gain_a, bias_a)
    hidden_low = hidden.astype(low)
    store(hb_ref, hidden_low)
    branch = jnp.zeros((rows, D), full)
    quarter = FF // 4
    cuts = [slice(at, at + quarter) for at in range(0, FF, quarter)]
    for turn, cut in enumerate(cuts):
        side = turn // 2
        columns = slice(turn % 2 * quarter, (turn % 2 + 1) * quarter)
        preact = contract(hidden_low, up_refs[turn][...], 1, 1)
        cumulative = 0.5 * (1.0 + lax.erf(preact * 0.7071067811865476))
        gelu_low = (preact * cumulative).astype(low)
        slope_ref[:, cut] = cumulative + preact * (jnp.exp(-0.5 * preact * preact) * 0.3989422804014327)
        g_refs[side][0, :, columns] = gelu_low[:part]
        g_refs[side][1, :, columns] = gelu_low[part:]
        branch = branch + contract(gelu_low, down_refs[turn][...], 1, 0)
    outputs, normed_b, inv_b = norm_forward(hidden + branch, gain_b, bias_b)
    store(block_ref, outputs.astype(low))
    dsum, sums_b = norm_backward(load(cot_ref).astype(full), normed_b, inv_b, gain_b)
    dsum_low = dsum.astype(low)
    store(df_ref, dsum_low)
    dhidden = dsum
    for turn, cut in enumerate(cuts):
        side = turn // 2
        columns = slice(turn % 2 * quarter, (turn % 2 + 1) * quarter)
        dinner = (contract(dsum_low, down_refs[turn][...], 1, 1) * slope_ref[:, cut]).astype(low)
        du_refs[side][0, :, columns] = dinner[:part]
        du_refs[side][1, :, columns] = dinner[part:]
        dhidden = dhidden + contract(dinner, up_refs[turn][...], 1, 0)
    dresidual, sums_a = norm_backward(dhidden, normed_a, inv_a, gain_a)
    store(da_ref, dresidual)
    dattn = dresidual.astype(low)
    store(dattn_ref, dattn)
    dheads = contract(dattn, wo_ref[...], 1, 1)
    for pair in range(len(packed) // 2):
        lanes = slice(pair * LANES, (pair + 1) * LANES)
        top, bottom = dheads[:part, lanes], dheads[part:, lanes]
        both = (
            jnp.where(left, top, pltpu.roll(bottom, HD, 1)).astype(low),
            jnp.where(left, pltpu.roll(top, HD, 1), bottom).astype(low),
        )
        for side in range(2):
            turn, head = divmod(2 * pair + side, heads)
            do_refs[turn][head] = both[side]
    sums = jnp.concatenate(sums_a + sums_b, axis=0)

    @pl.when(pl.program_id(0) == 0)
    def _():
        sums_ref[...] = sums

    @pl.when(pl.program_id(0) > 0)
    def _():
        sums_ref[...] += sums


LAYER_STEPS = 4


def layer(o_got, block_in, block_cot, out_rows, up_rows, down_rows, norm_params):
    heads = len(o_got)
    here = block_in.shape[0]
    half = here // 2
    part = half // LAYER_STEPS
    once = pl.Buffered(1)

    def lead(count, width):
        return pl.BlockSpec((count, part, width), lambda step: (0, step, 0))

    def do_part(turns):
        return pl.BlockSpec((turns, heads, part, LANES), lambda step: (0, 0, step, 0))

    def still(rows):
        return pl.BlockSpec((rows, D), lambda step: (0, 0), pipeline_mode=once)

    def pairs(width, kind):
        return jax.ShapeDtypeStruct((2, half, width), kind)

    o_args = [piece for own, near, far in o_got for piece in (own, near, far, near)]
    later = pl.BlockSpec((part, LANES), lambda step: (step + LAYER_STEPS, 0))
    lanes = pl.BlockSpec((part, LANES), lambda step: (step, 0))
    two = lead(2, D)
    wide = lead(2, FF // 2)
    flat = pl.pallas_call(
        lambda *refs: layer_kernel(heads, *refs),
        grid=(LAYER_STEPS,),
        in_specs=[lanes, lanes, lanes, later] * heads
        + [two, two, still(D), still(4)]
        + [still(FF // 4)] * 8,
        out_specs=[do_part(1), do_part(1), do_part(2), two, two] + [wide] * 4 + [two] * 4
        + [pl.BlockSpec((4, D), lambda step: (0, 0))],
        out_shape=[jax.ShapeDtypeStruct((turns, heads, half, LANES), low) for turns in (1, 1, 2)]
        + [
            pairs(D, low),
            pairs(D, full),
            pairs(FF // 2, low),
            pairs(FF // 2, low),
            pairs(FF // 2, low),
            pairs(FF // 2, low),
            pairs(D, low),
            pairs(D, low),
            pairs(D, low),
            pairs(D, low),
            jax.ShapeDtypeStruct((4, D), full),
        ],
        scratch_shapes=[pltpu.VMEM((2 * part, FF), full)],
        compiler_params=pltpu.CompilerParams(vmem_limit_bytes=60 * 2**20),
        cost_estimate=pl.CostEstimate(flops=40 * 10**9, bytes_accessed=1000, transcendentals=0),
        name="layer",
    )(
        *o_args,
        block_in.reshape(2, half, D),
        block_cot.reshape(2, half, D),
        out_rows,
        norm_params,
        *up_rows,
        *down_rows,
    )
    tokenwise = [value.reshape(here, value.shape[2]) for value in flat[3:-1]]
    return flat[:3], tokenwise, flat[-1]


def weight_grad_kernel(left_ref, right_ref, *refs):
    value = contract(left_ref[...], right_ref[...], 0, 0)
    if len(refs) > 1:
        value = value + refs[0][...].astype(full)
    refs[-1][...] = value.astype(low)


def weight_grad(left, right, other=None):
    rows, width = left.shape
    part = 384
    args = [left, right]
    in_specs = [
        pl.BlockSpec((rows, part), lambda step: (0, step)),
        pl.BlockSpec((rows, D), lambda step: (0, 0)),
    ]
    block = pl.BlockSpec((part, D), lambda step: (step, 0))
    if other is not None:
        args.append(other)
        in_specs.append(block)
    return pl.pallas_call(
        weight_grad_kernel,
        grid=(width // part,),
        in_specs=in_specs,
        out_specs=block,
        out_shape=jax.ShapeDtypeStruct((width, D), low),
        compiler_params=pltpu.CompilerParams(vmem_limit_bytes=32 * 2**20),
        cost_estimate=pl.CostEstimate(flops=5 * 10**9, bytes_accessed=1000, transcendentals=0),
        name="weight_grad",
    )(*args)


def packed_gram(matrix):
    gram = contract(matrix, matrix, 0, 0)
    panels = [gram[: at + LANES, at : at + LANES] for at in range(0, D, LANES)]
    return jnp.concatenate(panels, axis=0)


def schulz_kernel(panels_ref, matrix_ref, out_ref, gram_ref, low_ref, mix_ref, once_ref, it_ref):
    one, two, three = schulz_coeffs
    blocks = D // LANES
    diagonal = lax.broadcasted_iota(jnp.int32, (LANES, LANES), 0) == lax.broadcasted_iota(
        jnp.int32, (LANES, LANES), 1
    )
    trace = jnp.zeros((1, 1), full)
    first = 0
    for col in range(blocks):
        for row in range(col + 1):
            block = panels_ref[first : first + LANES, :].astype(full)
            first += LANES
            rows = slice(row * LANES, (row + 1) * LANES)
            cols = slice(col * LANES, (col + 1) * LANES)
            gram_ref[rows, cols] = block
            if row < col:
                gram_ref[cols, rows] = block.T
            else:
                mine = jnp.where(diagonal, block, 0.0)
                trace = trace + jnp.sum(jnp.sum(mine, axis=1, keepdims=True), axis=0, keepdims=True)
    shrink = 1.0 / (jnp.sqrt(trace) + 1e-07)
    cuts = [slice(at, at + SCHULZ_CUT) for at in range(0, D, SCHULZ_CUT)]
    its = [slice(at, at + SCHULZ_ITS) for at in range(0, matrix_ref.shape[0], SCHULZ_ITS)]
    for cut in cuts:
        gram = gram_ref[cut, :] * (shrink * shrink)
        gram_ref[cut, :] = gram
        low_ref[cut, :] = gram.astype(low)
    for part in its:
        it_ref[part, :] = matrix_ref[part, :].astype(full) * shrink
    for step in range(NS_STEPS):
        for cut in cuts:
            square = contract(low_ref[cut, :], low_ref[...], 1, 0)
            mix_ref[cut, :] = (two * gram_ref[cut, :] + three * square).astype(low)
        for part in its:
            iterate = it_ref[part, :]
            iterate = one * iterate + contract(iterate.astype(low), mix_ref[...], 1, 0)
            if step < NS_STEPS - 1:
                it_ref[part, :] = iterate
            else:
                out_ref[part, :] = iterate.astype(low)
        if step < NS_STEPS - 1:
            for cut in cuts:
                once = contract(mix_ref[cut, :], low_ref[...], 1, 0)
                gram_ref[cut, :] = one * one * gram_ref[cut, :] + 2.0 * one * once
                once_ref[cut, :] = once.astype(low)
            for cut in cuts:
                gram = gram_ref[cut, :] + contract(once_ref[cut, :], mix_ref[...], 1, 0)
                gram_ref[cut, :] = gram
            for cut in cuts:
                low_ref[cut, :] = gram_ref[cut, :].astype(low)


SCHULZ_CUT = 256
SCHULZ_ITS = 192


def schulz(panels, matrix):
    in_vmem = pl.BlockSpec(memory_space=pltpu.VMEM)
    return pl.pallas_call(
        schulz_kernel,
        in_specs=[in_vmem, in_vmem],
        out_specs=in_vmem,
        out_shape=jax.ShapeDtypeStruct(matrix.shape, low),
        scratch_shapes=[
            pltpu.VMEM((D, D), full),
            pltpu.VMEM((D, D), low),
            pltpu.VMEM((D, D), low),
            pltpu.VMEM((D, D), low),
            pltpu.VMEM(matrix.shape, full),
        ],
        compiler_params=pltpu.CompilerParams(vmem_limit_bytes=32 * 2**20),
        cost_estimate=pl.CostEstimate(flops=8 * 10**9, bytes_accessed=1000, transcendentals=0),
        name="schulz",
    )(panels, matrix)


def rows_qkv(value):
    kinds, depth, heads, cut = value.shape
    return value.transpose(0, 2, 3, 1).reshape(kinds * heads * cut, depth)


def unrows_qkv(rows, shape):
    kinds, depth, heads, cut = shape
    return rows.reshape(kinds, heads, cut, depth).transpose(0, 3, 1, 2)


def on_device(
    block_in,
    block_cot,
    cluster_perm,
    w_qkv,
    w_out,
    w_up,
    w_down,
    mom_qkv,
    mom_out,
    mom_up,
    mom_down,
    norm_params,
    norm_first,
    norm_second,
):
    ffn_here = lax.axis_index("ffn")
    seqs = lax.axis_size("seq")
    n_bits = len(seq_bits())
    here = block_in.shape[0]
    half = here // 2
    heads = w_out.shape[0]
    cut = w_out.shape[1]
    seq_len = cluster_perm.shape[2]
    clusters = seq_len // CLUSTER

    weights = [rows_qkv(w_qkv), w_out.reshape(heads * cut, D), w_up.T, w_down]
    momenta = [rows_qkv(mom_qkv), mom_out.reshape(heads * cut, D), mom_up.T, mom_down]

    wide_qkv = weights[0].astype(low)
    far = seq_stages()[0]
    first = swap(wide_qkv, *far)
    tokens = [block_in, swap(block_in, "ffn", 1), swap(block_in, "ffn", 2)]
    tokens.append(swap(tokens[2], "ffn", 1))
    wide_qkv = jnp.concatenate([wide_qkv, first], axis=0)
    shards = (weights[2].astype(low), weights[1].astype(low), weights[3].astype(low))
    for stage in seq_stages()[1:]:
        if stage == seq_stages()[-1]:
            shards = after(shards, wide_qkv)
        wide_qkv = spread(wide_qkv, [stage])
    up_rows, out_wide, down_rows = shards
    wide_qkv = wide_qkv.reshape(seqs, 3, heads, cut, D).transpose(1, 2, 0, 3, 4).reshape(3, heads, HD, D)
    head_rows = jnp.stack(
        [wide_qkv[0], wide_qkv[2], wide_qkv[1], jnp.zeros_like(wide_qkv[1])], axis=1
    ).reshape(heads * 2 * LANES, D)
    for stage in far_stages():
        up_rows, out_wide, down_rows = [spread(value, [stage]) for value in (up_rows, out_wide, down_rows)]
    low_rows = down_rows.shape[0]
    shards = (up_rows, jnp.concatenate([down_rows, out_wide], axis=0))
    first_at = (("seq", 1), ("ffn", 2))
    then_at = (("ffn", 2), ("seq", 1))

    def swaps(values, places):
        return tuple(swap(value, *place) for value, place in zip(values, places))

    first_got = swaps(shards, first_at)
    own_got = swaps(shards, then_at)

    perm = jnp.bitwise_xor(cluster_perm[0], ffn_here * here)
    kept = []
    o_sent = []
    far_got = []
    near_got = []
    for head in range(heads):
        mine = head_rows[head * 2 * LANES : (head + 1) * 2 * LANES]
        order_rows = perm[head : head + 1]
        if head == 1:
            order_rows, first_got = after((order_rows, first_got), kept[0])
            other_got = swaps(first_got, then_at)
            up_pieces = [jnp.concatenate([shards[0], first_got[0]], axis=0)]
            up_pieces.append(swap(up_pieces[0], "ffn", 1))
        if head == 2:
            order_rows, own_got, far_got[0], up_pieces[1] = after(
                (order_rows, own_got, far_got[0], up_pieces[1]), kept[1]
            )
            near_got.append(send_on(o_sent[0][0], far_got[0][half:]))
            down_pieces = [jnp.concatenate([shards[1][:low_rows], own_got[1][:low_rows]], axis=0)]
            down_pieces.append(swap(down_pieces[0], "ffn", 1))
        own, near, far, qv, key = attend(order_rows, tokens, mine, "attend")
        kept.append((qv, key))
        o_sent.append((near, own))
        far_got.append(swap(far, "ffn", 2))
    other_got, far_got[1], near_got[0], down_pieces[1] = after(
        (other_got, far_got[1], near_got[0], down_pieces[1]), kept[2]
    )
    up_pieces.insert(1, jnp.concatenate([own_got[0], other_got[0]], axis=0))
    down_pieces.insert(1, jnp.concatenate([first_got[1][:low_rows], other_got[1][:low_rows]], axis=0))
    out_wide = jnp.concatenate(
        [value[low_rows:] for value in (shards[1], own_got[1], first_got[1], other_got[1])], axis=0
    )
    out_wide = spread(out_wide, [("ffn", 1)])
    up_pieces.append(swap(up_pieces[1], "ffn", 1))
    down_pieces.append(swap(down_pieces[1], "ffn", 1))
    near_got += [send_on(o_sent[head][0], far_got[head][half:]) for head in (1, 2)]
    o_got = [(sent[1], near, far) for sent, near, far in zip(o_sent, near_got, far_got)]
    up_rows, down_rows = up_pieces, down_pieces

    digits = (2, 2, 2) + (2,) * (n_bits - 1)
    order = (1, 0, 2 + n_bits, 2) + tuple(range(3, 2 + n_bits)) + (3 + n_bits, 4 + n_bits)
    back = tuple(sorted(range(len(order)), key=lambda at: order[at]))
    sizes = digits + (heads, cut, D)
    out_rows = out_wide.reshape(sizes).transpose(order).reshape(4 * heads * HD, D)

    do_blocks, tokenwise, norm_part = layer(
        o_got, block_in, block_cot, out_rows, up_rows, down_rows, norm_params
    )
    block_out, dresidual, gelu_a, gelu_b, dinner_a, dinner_b, dbranch, hidden_low, dattn, o_rows = tokenwise
    do_far = swap(do_blocks[2], "ffn", 2)
    do_got = (do_blocks[0], send_on(do_blocks[1], do_far[1:]), do_far)

    early_half = (cluster_perm[0] < seq_len // 2).astype(full).reshape(heads, clusters, CLUSTER)
    share = lax.dynamic_update_slice(
        jnp.zeros((4 * heads, clusters), full), jnp.sum(early_half, axis=2) / CLUSTER, (ffn_here * heads, 0)
    ).reshape(1, 4 * heads * clusters)
    small = jnp.concatenate([norm_part, jnp.pad(share, ((0, 0), (0, D - share.shape[1])))])

    down_sent = weight_grad(gelu_b, dbranch)
    up_sent = weight_grad(dinner_b, hidden_low)
    part_out = weight_grad(o_rows, dattn)
    part_out = part_out.reshape(tuple(sizes[at] for at in order)).transpose(back)
    part_out = part_out.reshape(4 * heads * HD, D)
    out_kept, out_sent = cut_outer(part_out)
    down_sum = weight_grad(gelu_a, dbranch, swap(down_sent, "ffn", 1))
    up_sum = weight_grad(dinner_a, hidden_low, swap(up_sent, "ffn", 1))
    out_sum = add_low(out_kept, swap(out_sent, "ffn", 1))
    small = small + swap(small, "ffn", 1)

    def quarters(value):
        rows = value.shape[0] // 4
        return [value[part * rows : (part + 1) * rows] for part in range(4)]

    low_sums = [jnp.concatenate(pair, axis=0) for pair in zip(quarters(down_sum), quarters(out_sum))]
    up_sums = [quarters(up_sum)[part] for part in (0, 2, 1, 3)]
    sums = list(zip(up_sums, low_sums))
    places = (("ffn", 2), ("seq", 1))
    then_places = (("seq", 1), ("ffn", 2))

    def cut_all(values):
        cuts = [cut_outer(value) for value in values]
        return [pair[0] for pair in cuts], jnp.concatenate([pair[1] for pair in cuts], axis=0)

    def add_all(kept_parts, got):
        values = []
        at = 0
        for part in kept_parts:
            values.append(add_low(part, got[at : at + part.shape[0]]))
            at += part.shape[0]
        return values

    do_got = after(do_got, sums)
    far_places = list(reversed(far_stages()))
    part_heads = []
    dboth = []
    for head in range(heads):
        if head == 0:
            first_got = swaps(sums[3], places)
            small_got = swap(small, "ffn", 2)
        if head == 1:
            do_got, first_got, small_got = after((do_got, first_got, small_got), part_heads[0])
            then_sent = [add_low(value, other) for value, other in zip(sums[2], first_got)]
            second_got = swaps(sums[1], places)
            then_got = swaps(then_sent, then_places)
            small = small + small_got
            small_got = swap(small, "seq", 1)
        if head == 2:
            do_got, second_got, then_got, small_got = after(
                (do_got, second_got, then_got, small_got), part_heads[1]
            )
            up_sum, low_sum = [
                (value.astype(full) + second.astype(full) + then.astype(full)).astype(low)
                for value, second, then in zip(sums[0], second_got, then_got)
            ]
            small = small + small_got
            rest, sent = cut_all([up_sum, low_sum[:low_rows], low_sum[low_rows:]])
            rest_got = swap(sent, *far_places[0])
            small_got = swap(small, *far_places[0])
        gw, both = attend_back(perm[head : head + 1], head, kept[head], do_got, tokens)
        part_heads.append(gw)
        dboth.append(both)
    rest_got, small_got, dboth = after((rest_got, small_got, dboth), part_heads[2])
    rest = add_all(rest, rest_got)
    small = small + small_got
    part_qkv = jnp.stack(part_heads).reshape(heads, 4, HD, D)
    part_qkv = jnp.stack([part_qkv[:, 0], part_qkv[:, 2], part_qkv[:, 1]])
    part_qkv = part_qkv.reshape(3, heads, seqs, cut, D).transpose(2, 0, 1, 3, 4)
    qkv_kept, qkv_sent = cut_outer(part_qkv.reshape(seqs * 3 * heads * cut, D))
    qkv_got = swap(qkv_sent, "seq", 1)
    gx_kept, gx_sent = token_grad(dboth, head_rows, here)
    qkv_got, gx_kept, gx_sent = after((qkv_got, gx_kept, gx_sent))
    qkv_sum = add_low(qkv_kept, qkv_got)
    gx_got = swap(gx_sent, "ffn", 1)
    for turn, place in enumerate(far_places):
        qkv_kept, qkv_sent = cut_outer(qkv_sum)
        qkv_got = swap(qkv_sent, *place)
        if turn + 1 < len(far_places):
            kept_parts, sent = cut_all(rest)
            rest_got = swap(sent, *far_places[turn + 1])
            small_got = swap(small, *far_places[turn + 1])
            qkv_got, rest_got, small_got, gx_got = after((qkv_got, rest_got, small_got, gx_got))
            rest = add_all(kept_parts, rest_got)
            small = small + small_got
        qkv_sum = add_low(qkv_kept, qkv_got)
        if turn == 0:
            gx_kept, gx_sent = cut_outer(add_low(gx_kept, gx_got))
            gx_cuts = cut_outer(gx_sent)
            gx_first = swap(gx_cuts[0], "ffn", 2)
    up_sum, down_sum, out_sum = rest
    grad_qkv, grad_out, grad_up, grad_down = [
        value.astype(full) for value in (qkv_sum, out_sum, up_sum, down_sum)
    ]
    grad_norm = small[:4]
    occupancy = small[4, : 4 * heads * clusters].reshape(4 * heads, clusters)

    grads = [grad_qkv, grad_out, grad_up, grad_down]
    moments = [0.5 * mom + grad for mom, grad in zip(momenta, grads)]
    most = max(moment.shape[0] for moment in moments)
    stack = jnp.stack(
        [jnp.pad(moment.astype(low), ((0, most - moment.shape[0]), (0, 0))) for moment in moments]
    )

    def pick(turn):
        return lax.dynamic_index_in_dim(stack, jnp.bitwise_xor(ffn_here, turn), keepdims=False)

    picked = [swap(pick(turn), "ffn", turn) for turn in (1, 2, 3)]
    picked, gx_first = after((picked, gx_first))
    matrix = jnp.concatenate([pick(0)] + picked, axis=0)
    gx_second = swap(gx_cuts[1], "ffn", 2)
    panels = sum_halves(packed_gram(matrix), seq_stages())
    panels = spread_halves(panels, seq_stages())
    panels, gx_second = after((panels, gx_second))
    gx_other = jnp.concatenate([gx_first, gx_second], axis=0)
    steps = schulz(panels, matrix).reshape(4, most, D)
    input_grad = dresidual + (gx_kept.astype(full) + gx_other.astype(full))
    home = jnp.stack([steps[0]] + [swap(steps[turn], "ffn", turn) for turn in (1, 2, 3)])
    step_rates = (
        0.5 * math.sqrt(3.0),
        0.5 * math.sqrt(CLUSTER / 3.0),
        0.5 * math.sqrt(FF / D),
        0.5,
    )
    masters = []
    for member in range(4):
        own = lax.dynamic_index_in_dim(home, jnp.bitwise_xor(ffn_here, member), keepdims=False)
        own = own[: moments[member].shape[0]].astype(full)
        masters.append(weights[member] - step_rates[member] * own)

    first_fix = 1.0 - 0.9**ADAM_STEP
    second_fix = 1.0 - 0.999**ADAM_STEP
    first_new = 0.9 * norm_first + 0.1 * grad_norm
    second_new = 0.999 * norm_second + 0.001 * grad_norm * grad_norm
    first_hat = first_new / first_fix
    second_hat = second_new / second_fix
    norm_new = norm_params - 0.5 * (first_hat / (jnp.sqrt(second_hat) + 1e-08) + 0.01 * norm_params)

    def shaped(four):
        return (unrows_qkv(four[0], w_qkv.shape), four[1].reshape(w_out.shape), four[2].T, four[3])

    return (
        (block_out, input_grad)
        + shaped(grads)
        + (grad_norm,)
        + shaped(moments)
        + shaped(masters)
        + (first_new, second_new, norm_new, occupancy)
    )


def solution(mesh):
    rows = P(("seq", "ffn"), None)
    placed = (
        rows,
        rows,
        P("seq", "ffn", None),
        P(None, None, "ffn", "seq"),
        P("ffn", "seq", None),
        P(None, ("seq", "ffn")),
        rows,
        P(None, None, "ffn", "seq"),
        P("ffn", "seq", None),
        P(None, ("seq", "ffn")),
        rows,
        P(),
        P(),
        P(),
    )
    four = placed[3:7]
    return jax.shard_map(
        on_device,
        mesh=mesh,
        in_specs=placed,
        out_specs=(rows, rows) + four + (P(),) + four + four + (P(), P(), P(), P()),
        check_vma=False,
    )
```

```python
import math

import jax
import jax.numpy as jnp
from jax import lax
from jax.experimental import pallas as pl
from jax.experimental.pallas import tpu as pltpu
from jax.sharding import PartitionSpec as P

D = 768
HD = 64
FF = 3072
CLUSTER = 128
NS_STEPS = 3
ADAM_STEP = 10

schulz_coeffs = (3.4445, -4.775, 2.0315)
norm_epsilon = 1e-05
low = jnp.bfloat16
full = jnp.float32
LANES = 128
GROUP = 4
score_scale = 1.0 / math.sqrt(HD)


def contract(left, right, left_axis, right_axis):
    return lax.dot_general(
        left, right, (((left_axis,), (right_axis,)), ((), ())), preferred_element_type=full
    )


def swap(value, axis, bit):
    size = lax.axis_size(axis)
    return lax.ppermute(value, axis, [(place, place ^ bit) for place in range(size)])


def seq_bits():
    bits = []
    bit = lax.axis_size("seq") // 2
    while bit >= 1:
        bits.append(bit)
        bit //= 2
    return bits


def seq_stages():
    return [("seq", bit) for bit in seq_bits()]


def far_stages():
    return [("seq", bit) for bit in seq_bits() if bit > 1]


def spread(shard, stages):
    for axis, bit in stages:
        shard = jnp.concatenate([shard, swap(shard, axis, bit)], axis=0)
    return shard


def fold(partial, stages):
    for axis, bit in reversed(stages):
        half = partial.shape[0] // 2
        kept = partial[:half]
        other = swap(partial[half:].astype(low), axis, bit)
        partial = kept.astype(full) + other.astype(full)
    return partial


def after(values, *tokens):
    return lax.optimization_barrier((values, tokens))[0]


def join_inner(near, other):
    rows = near.shape[0] // 2
    return jnp.concatenate([near[:rows], other[:rows], near[rows:], other[rows:]], axis=0)


def cut_outer(value):
    half = value.shape[0] // 2
    return value[:half], value[half:]


def cut_inner(value):
    rows = value.shape[0] // 4
    quarters = [value[part * rows : (part + 1) * rows] for part in range(4)]
    return tuple(jnp.concatenate(quarters[side::2], axis=0) for side in range(2))


def add_low(kept, other):
    return (kept.astype(full) + other.astype(full)).astype(low)


def fold_step(value, cut, axis, bit):
    kept, sent = cut(value)
    return add_low(kept, swap(sent, axis, bit))


def send_on(near, far_got, axis=0):
    return swap(jnp.concatenate([near, far_got], axis=axis), "ffn", 1)


def add_many(first, others):
    value = first.astype(full)
    for other in others:
        value = value + other.astype(full)
    return value


def seq_groups():
    bits = sorted(seq_bits())
    return [tuple(bits[:1])] + [tuple(bits[at : at + 2]) for at in range(1, len(bits), 2)]


def masks_of(bits):
    masks = [0]
    for bit in bits:
        masks = [mask | more for mask in masks for more in (0, bit)]
    return masks


def cut_many(value, count):
    rows = value.shape[0] // count
    return [value[part * rows : (part + 1) * rows] for part in range(count)]


def place_in(bits):
    me = lax.axis_index("seq")
    place = 0
    for bit in bits:
        place = 2 * place + ((me & bit) != 0).astype(jnp.int32)
    return place


def sum_parts(value):
    for bits in seq_groups():
        masks = masks_of(bits)
        place = place_in(bits)
        parts = value.reshape((len(masks), value.shape[0] // len(masks)) + value.shape[1:])

        def part(turn):
            return lax.dynamic_index_in_dim(parts, jnp.bitwise_xor(place, turn), keepdims=False)

        got = [swap(part(turn), "seq", masks[turn]) for turn in range(1, len(masks))]
        value = add_many(part(0), got).astype(low)
    return value


def spread_parts(value, beside):
    for turn, bits in enumerate(reversed(seq_groups())):
        masks = masks_of(bits)
        got = [value] + [swap(value, "seq", mask) for mask in masks[1:]]
        if turn == 0:
            got, beside = after((got, beside))
        me = lax.axis_index("seq")
        for at, bit in enumerate(bits):
            flip = 2 ** (len(bits) - 1 - at)
            side = (me & bit) != 0
            got = [jnp.where(side, got[turn ^ flip], got[turn]) for turn in range(len(masks))]
        value = jnp.concatenate(got, axis=0)
    return value, beside


def in_turns(perm_ref, seq_len, fetch, work, place):
    count = GROUP * CLUSTER
    groups = seq_len // count

    def rows_of(turn):
        return pl.multiple_of(jnp.clip(turn, 0, groups - 1) * count, count)

    def fetch_some(side, turn, rows):
        base = rows_of(turn)
        for row in rows:
            fetch(side, perm_ref[0, base + row], row)

    def place_some(side, turn, rows):
        base = rows_of(turn)
        for row in rows:
            place(side, perm_ref[0, base + row], row)

    def step(pair, carry):
        for side in range(2):
            turn = 2 * pair + side
            done = 0
            for at in work(side, rows_of(turn)):
                rows = range(done, min(count, int(at * count)))
                fetch_some(1 - side, turn + 1, rows)
                place_some(1 - side, turn - 1, rows)
                done = max(done, rows.stop)
            fetch_some(1 - side, turn + 1, range(done, count))
            place_some(1 - side, turn - 1, range(done, count))
        return carry

    fetch_some(0, 0, range(count))
    lax.fori_loop(0, groups // 2, step, 0)
    place_some(1, groups - 1, range(count))


def softmax_rows(scores):
    peak = jnp.max(scores, axis=1, keepdims=True)
    powers = jnp.exp((scores - peak) * score_scale)
    return powers * (1.0 / jnp.sum(powers, axis=1, keepdims=True))


def left_half(rows):
    return lax.broadcasted_iota(jnp.int32, (rows, LANES), 1) < HD


def attend_kernel(
    perm_ref, x0, x1, x2, x3, w_ref, own_ref, near_ref, far_ref, qv_ref, key_ref, qv_rows, key_rows, o_rows, *got
):
    qv_got, key_got, o_got = got[0:2], got[2:4], got[4:6]
    here = x0.shape[0]
    seq_len = 4 * here
    half = here // 2
    for block, x_ref in enumerate((x0, x1, x2, x3)):
        for cut in range(2):
            both = contract(x_ref[pl.ds(cut * half, half), :], w_ref[...], 1, 1)
            rows = pl.ds(block * here + cut * half, half)
            qv_rows[rows, :] = both[:, :LANES]
            key_rows[rows, :] = both[:, LANES:]
    spans = [slice(part * CLUSTER, (part + 1) * CLUSTER) for part in range(GROUP)]

    def fetch(side, index, row):
        qv_got[side][pl.ds(row, 1), :] = qv_rows[pl.ds(index, 1), :]
        key_got[side][pl.ds(row, 1), :] = key_rows[pl.ds(index, 1), :]

    def work(side, base):
        qvs = [qv_got[side][span].astype(low) for span in spans]
        keys = [key_got[side][span].astype(low) for span in spans]
        for part in range(GROUP):
            rows = pl.ds(base + part * CLUSTER, CLUSTER)
            qv_ref[rows, :] = qvs[part]
            key_ref[rows, :] = keys[part]
        scores = [contract(qv, key, 1, 1) for qv, key in zip(qvs, keys)]
        yield 0.3
        probs = []
        for part in range(GROUP):
            probs.append(softmax_rows(scores[part]).astype(low))
            yield 0.3 + 0.6 * (part + 1) / GROUP
        for part in range(GROUP):
            o_got[side][spans[part]] = contract(probs[part], qvs[part], 1, 0)

    def place(side, index, row):
        o_rows[pl.ds(index, 1), :] = o_got[side][pl.ds(row, 1), :]

    in_turns(perm_ref, seq_len, fetch, work, place)
    outs = (own_ref, near_ref, far_ref.at[pl.ds(0, half), :], far_ref.at[pl.ds(half, half), :])
    for block, out_ref in enumerate(outs):
        top = pltpu.roll(o_rows[pl.ds(block * here, half), :], HD, 1)
        bottom = o_rows[pl.ds(block * here + half, half), :]
        out_ref[...] = jnp.where(left_half(half), top, bottom).astype(low)


def vmem(*shape):
    return pl.BlockSpec(shape, memory_space=pltpu.VMEM)


def attend(perm, tokens, weights, name):
    seq_len = perm.shape[1]
    here = tokens[0].shape[0]
    rows_got = pltpu.VMEM((GROUP * CLUSTER, LANES), full)
    rows_all = pltpu.VMEM((seq_len, LANES), full)
    in_vmem = pl.BlockSpec(memory_space=pltpu.VMEM)
    return pl.pallas_call(
        attend_kernel,
        in_specs=[pl.BlockSpec(memory_space=pltpu.SMEM)] + [in_vmem] * 5,
        out_specs=[in_vmem] * 5,
        out_shape=[
            jax.ShapeDtypeStruct((here // 2, LANES), low),
            jax.ShapeDtypeStruct((here // 2, LANES), low),
            jax.ShapeDtypeStruct((here, LANES), low),
            jax.ShapeDtypeStruct((seq_len, LANES), low),
            jax.ShapeDtypeStruct((seq_len, LANES), low),
        ],
        scratch_shapes=[rows_all] * 3 + [rows_got] * 6,
        compiler_params=pltpu.CompilerParams(vmem_limit_bytes=40 * 2**20),
        cost_estimate=pl.CostEstimate(flops=18 * 10**9, bytes_accessed=1000, transcendentals=0),
        name=name,
    )(perm, *tokens, weights)


def attend_back_kernel(
    perm_ref, qv_ref, key_ref, do0, do1, do2, do3, x0, x1, x2, x3, gw_ref, dboth_ref, d_rows, dqv_rows, dkey_rows, *got
):
    d_got, dqv_got, dkey_got = got[0:2], got[2:4], got[4:6]
    here = x0.shape[0]
    seq_len = 4 * here
    half = here // 2
    for block, do_ref in enumerate((do0, do1, do2, do3)):
        rows = do_ref[...].astype(full)
        top = pltpu.roll(rows, HD, 1)
        d_rows[pl.ds(block * here, half), :] = jnp.where(left_half(half), 0.0, top)
        d_rows[pl.ds(block * here + half, half), :] = jnp.where(left_half(half), 0.0, rows)
    spans = [slice(part * CLUSTER, (part + 1) * CLUSTER) for part in range(GROUP)]

    def fetch(side, index, row):
        d_got[side][pl.ds(row, 1), :] = d_rows[pl.ds(index, 1), :]

    def work(side, base):
        rows = [pl.ds(base + part * CLUSTER, CLUSTER) for part in range(GROUP)]
        qvs = [qv_ref[span, :] for span in rows]
        keys = [key_ref[span, :] for span in rows]
        dos = [d_got[side][span].astype(low) for span in spans]
        scores = [contract(qv, key, 1, 1) for qv, key in zip(qvs, keys)]
        dprobs = [contract(do, qv, 1, 1) for do, qv in zip(dos, qvs)]
        yield 0.2
        probs = []
        for part in range(GROUP):
            probs.append(softmax_rows(scores[part]))
            yield 0.2 + 0.3 * (part + 1) / GROUP
        probs_low = [prob.astype(low) for prob in probs]
        dscores = []
        for prob, dprob in zip(probs, dprobs):
            dscores.append((prob * (dprob - jnp.sum(prob * dprob, axis=1, keepdims=True))).astype(low))
            yield 0.5 + 0.3 * len(dscores) / GROUP
        for part in range(GROUP):
            dqv_got[side][spans[part]] = score_scale * contract(dscores[part], keys[part], 1, 0) + contract(
                probs_low[part], dos[part], 0, 0
            )
            dkey_got[side][spans[part]] = score_scale * contract(dscores[part], qvs[part], 0, 0)

    def place(side, index, row):
        dqv_rows[pl.ds(index, 1), :] = dqv_got[side][pl.ds(row, 1), :]
        dkey_rows[pl.ds(index, 1), :] = dkey_got[side][pl.ds(row, 1), :]

    in_turns(perm_ref, seq_len, fetch, work, place)
    gw = jnp.zeros((2 * LANES, D), full)
    for block, x_ref in enumerate((x0, x1, x2, x3)):
        rows = pl.ds(block * here, here)
        dboth_ref[rows, :LANES] = dqv_rows[rows, :].astype(low)
        dboth_ref[rows, LANES:] = dkey_rows[rows, :].astype(low)
        gw = gw + contract(dboth_ref[rows, :], x_ref[...], 0, 0)
    gw_ref[...] = gw.astype(low)


def attend_back(perm, head, kept, do, tokens):
    seq_len = perm.shape[1]
    here = tokens[0].shape[0]
    half = here // 2
    rows_got = pltpu.VMEM((GROUP * CLUSTER, LANES), full)
    rows_all = pltpu.VMEM((seq_len, LANES), full)
    in_vmem = pl.BlockSpec(memory_space=pltpu.VMEM)
    own, near, far = do

    def part(at, turn):
        return pl.BlockSpec((None, None, half, LANES), lambda step: (at, turn, 0, 0))

    at = 0 if head == 0 else head - 1

    return pl.pallas_call(
        attend_back_kernel,
        grid=(1,),
        in_specs=[pl.BlockSpec(memory_space=pltpu.SMEM)]
        + [in_vmem] * 2
        + [part(head, 0), part(at, 0), part(at, 0), part(at, 1)]
        + [in_vmem] * 4,
        out_specs=[in_vmem] * 2,
        out_shape=[
            jax.ShapeDtypeStruct((2 * LANES, D), low),
            jax.ShapeDtypeStruct((seq_len, 2 * LANES), low),
        ],
        scratch_shapes=[rows_all] * 3 + [rows_got] * 6,
        compiler_params=pltpu.CompilerParams(vmem_limit_bytes=40 * 2**20),
        cost_estimate=pl.CostEstimate(flops=22 * 10**9, bytes_accessed=1000, transcendentals=0),
        name="attend_back",
    )(perm, *kept, own, near, far, near, *tokens)


def token_grad_kernel(d0, d1, d2, w_ref, kept_ref, sent_ref):
    sums = None
    for head, d_ref in enumerate((d0, d1, d2)):
        piece = contract(d_ref[...], w_ref[pl.ds(head * 2 * LANES, 2 * LANES), :], 1, 0)
        sums = piece if sums is None else sums + piece

    @pl.when(pl.program_id(0) < 2)
    def _():
        sent_ref[...] = sums.astype(low)

    @pl.when(pl.program_id(0) >= 2)
    def _():
        kept_ref[...] = sums.astype(low)


def token_grad(dboth, weights, here):
    split = 2
    rows = here // split

    def from_block(slot, part):
        return ((2 * (slot % 2) + 1 - slot // 2) * split + part, 0)

    def to_sent(slot, part):
        return (jnp.minimum(slot * split + part, 2 * split - 1), 0)

    def to_kept(slot, part):
        return (jnp.maximum(slot * split + part - 2 * split, 0), 0)

    return pl.pallas_call(
        token_grad_kernel,
        grid=(4, split),
        in_specs=[pl.BlockSpec((rows, 2 * LANES), from_block)] * 3
        + [pl.BlockSpec((6 * LANES, D), lambda slot, part: (0, 0))],
        out_specs=[pl.BlockSpec((rows, D), to_kept), pl.BlockSpec((rows, D), to_sent)],
        out_shape=[jax.ShapeDtypeStruct((2 * here, D), low)] * 2,
        compiler_params=pltpu.CompilerParams(vmem_limit_bytes=32 * 2**20),
        cost_estimate=pl.CostEstimate(flops=8 * 10**9, bytes_accessed=1000, transcendentals=0),
        name="token_grad",
    )(*dboth, weights)


def row_mean(value):
    return jnp.mean(value, axis=-1, keepdims=True)


def norm_forward(inputs, gains, biases):
    center = inputs - row_mean(inputs)
    inv_std = lax.rsqrt(row_mean(center * center) + norm_epsilon)
    normed = center * inv_std
    return (normed * gains + biases, normed, inv_std)


def norm_backward(upstream, normed, inv_std, gains):
    scaled = upstream * gains
    inside = scaled - row_mean(scaled) - normed * row_mean(scaled * normed)
    sums = [jnp.sum(upstream * normed, axis=0, keepdims=True), jnp.sum(upstream, axis=0, keepdims=True)]
    return (inside * inv_std, sums)


def layer_kernel(heads, *refs):
    o_refs = refs[: 4 * heads]
    (x_ref, cot_ref, wo_ref, norm_ref) = refs[4 * heads : 4 * heads + 4]
    up_refs = refs[4 * heads + 4 : 4 * heads + 8]
    down_refs = refs[4 * heads + 8 : 4 * heads + 12]
    outs = refs[4 * heads + 12 :]
    (do_own, near_first, near_rest, far_first, far_rest, block_ref, da_ref) = outs[:7]
    g_refs = outs[7:9]
    du_refs = outs[9:11]
    (df_ref, hb_ref, dattn_ref, o_ref, sums_ref, slope_ref) = outs[11:]

    def store_do(head, turn, value):
        near, far, at = (near_first, far_first, 0) if head == 0 else (near_rest, far_rest, head - 1)
        if turn == 0:
            do_own[head, 0] = value
        elif turn == 1:
            near[at, 0] = value
        else:
            far[at, turn - 2] = value
    part = x_ref.shape[1]
    rows = 2 * part
    left = left_half(part)

    def load(ref):
        return jnp.concatenate([ref[0], ref[1]], axis=0)

    def store(ref, value):
        ref[0] = value[:part]
        ref[1] = value[part:]

    packed = []
    for turn in range(4):
        for head in range(heads):
            packed.append(o_refs[4 * head + turn][...].astype(full))
    for pair in range(len(packed) // 2):
        first, second = packed[2 * pair], packed[2 * pair + 1]
        lanes = slice(pair * LANES, (pair + 1) * LANES)
        o_ref[0, :, lanes] = jnp.where(left, first, pltpu.roll(second, HD, 1)).astype(low)
        o_ref[1, :, lanes] = jnp.where(left, pltpu.roll(first, HD, 1), second).astype(low)

    gain_a, bias_a = norm_ref[0:1, :], norm_ref[1:2, :]
    gain_b, bias_b = norm_ref[2:3, :], norm_ref[3:4, :]
    residual = load(x_ref).astype(full) + contract(load(o_ref), wo_ref[...], 1, 0)
    hidden, normed_a, inv_a = norm_forward(residual, gain_a, bias_a)
    hidden_low = hidden.astype(low)
    store(hb_ref, hidden_low)
    branch = jnp.zeros((rows, D), full)
    quarter = FF // 4
    cuts = [slice(at, at + quarter) for at in range(0, FF, quarter)]
    for turn, cut in enumerate(cuts):
        side = turn // 2
        columns = slice(turn % 2 * quarter, (turn % 2 + 1) * quarter)
        preact = contract(hidden_low, up_refs[turn][...], 1, 1)
        cumulative = 0.5 * (1.0 + lax.erf(preact * 0.7071067811865476))
        gelu_low = (preact * cumulative).astype(low)
        slope_ref[:, cut] = cumulative + preact * (jnp.exp(-0.5 * preact * preact) * 0.3989422804014327)
        g_refs[side][0, :, columns] = gelu_low[:part]
        g_refs[side][1, :, columns] = gelu_low[part:]
        branch = branch + contract(gelu_low, down_refs[turn][...], 1, 0)
    outputs, normed_b, inv_b = norm_forward(hidden + branch, gain_b, bias_b)
    store(block_ref, outputs.astype(low))
    dsum, sums_b = norm_backward(load(cot_ref).astype(full), normed_b, inv_b, gain_b)
    dsum_low = dsum.astype(low)
    store(df_ref, dsum_low)
    dhidden = dsum
    for turn, cut in enumerate(cuts):
        side = turn // 2
        columns = slice(turn % 2 * quarter, (turn % 2 + 1) * quarter)
        dinner = (contract(dsum_low, down_refs[turn][...], 1, 1) * slope_ref[:, cut]).astype(low)
        du_refs[side][0, :, columns] = dinner[:part]
        du_refs[side][1, :, columns] = dinner[part:]
        dhidden = dhidden + contract(dinner, up_refs[turn][...], 1, 0)
    dresidual, sums_a = norm_backward(dhidden, normed_a, inv_a, gain_a)
    store(da_ref, dresidual)
    dattn = dresidual.astype(low)
    store(dattn_ref, dattn)
    dheads = contract(dattn, wo_ref[...], 1, 1)
    for pair in range(len(packed) // 2):
        lanes = slice(pair * LANES, (pair + 1) * LANES)
        top, bottom = dheads[:part, lanes], dheads[part:, lanes]
        both = (
            jnp.where(left, top, pltpu.roll(bottom, HD, 1)).astype(low),
            jnp.where(left, pltpu.roll(top, HD, 1), bottom).astype(low),
        )
        for side in range(2):
            turn, head = divmod(2 * pair + side, heads)
            store_do(head, turn, both[side])
    sums = jnp.concatenate(sums_a + sums_b, axis=0)

    @pl.when(pl.program_id(0) == 0)
    def _():
        sums_ref[...] = sums

    @pl.when(pl.program_id(0) > 0)
    def _():
        sums_ref[...] += sums


LAYER_STEPS = 4


def layer(o_got, block_in, block_cot, out_rows, up_rows, down_rows, norm_params):
    heads = len(o_got)
    here = block_in.shape[0]
    half = here // 2
    part = half // LAYER_STEPS
    once = pl.Buffered(1)

    def lead(count, width):
        return pl.BlockSpec((count, part, width), lambda step: (0, step, 0))

    do_sizes = ((heads, 1), (1, 1), (heads - 1, 1), (1, 2), (heads - 1, 2))

    def do_part(count, turns):
        return pl.BlockSpec((count, turns, part, LANES), lambda step: (0, 0, step, 0))

    def still(rows):
        return pl.BlockSpec((rows, D), lambda step: (0, 0), pipeline_mode=once)

    def pairs(width, kind):
        return jax.ShapeDtypeStruct((2, half, width), kind)

    o_args = [piece for own, near, far in o_got for piece in (own, near, far, near)]
    later = pl.BlockSpec((part, LANES), lambda step: (step + LAYER_STEPS, 0))
    lanes = pl.BlockSpec((part, LANES), lambda step: (step, 0))
    two = lead(2, D)
    wide = lead(2, FF // 2)
    flat = pl.pallas_call(
        lambda *refs: layer_kernel(heads, *refs),
        grid=(LAYER_STEPS,),
        in_specs=[lanes, lanes, lanes, later] * heads
        + [two, two, still(D), still(4)]
        + [still(FF // 4)] * 8,
        out_specs=[do_part(*sizes) for sizes in do_sizes] + [two, two] + [wide] * 4 + [two] * 4
        + [pl.BlockSpec((4, D), lambda step: (0, 0))],
        out_shape=[jax.ShapeDtypeStruct((count, turns, half, LANES), low) for count, turns in do_sizes]
        + [
            pairs(D, low),
            pairs(D, full),
            pairs(FF // 2, low),
            pairs(FF // 2, low),
            pairs(FF // 2, low),
            pairs(FF // 2, low),
            pairs(D, low),
            pairs(D, low),
            pairs(D, low),
            pairs(D, low),
            jax.ShapeDtypeStruct((4, D), full),
        ],
        scratch_shapes=[pltpu.VMEM((2 * part, FF), full)],
        compiler_params=pltpu.CompilerParams(vmem_limit_bytes=60 * 2**20),
        cost_estimate=pl.CostEstimate(flops=40 * 10**9, bytes_accessed=1000, transcendentals=0),
        name="layer",
    )(
        *o_args,
        block_in.reshape(2, half, D),
        block_cot.reshape(2, half, D),
        out_rows,
        norm_params,
        *up_rows,
        *down_rows,
    )
    tokenwise = [value.reshape(here, value.shape[2]) for value in flat[5:-1]]
    return flat[:5], tokenwise, flat[-1]


def weight_grad_kernel(left_ref, right_ref, *refs):
    value = contract(left_ref[...], right_ref[...], 0, 0)
    if len(refs) > 1:
        value = value + refs[0][...].astype(full)
    refs[-1][...] = value.astype(low)


def weight_grad(left, right, other=None):
    rows, width = left.shape
    part = 384
    args = [left, right]
    in_specs = [
        pl.BlockSpec((rows, part), lambda step: (0, step)),
        pl.BlockSpec((rows, D), lambda step: (0, 0)),
    ]
    block = pl.BlockSpec((part, D), lambda step: (step, 0))
    if other is not None:
        args.append(other)
        in_specs.append(block)
    return pl.pallas_call(
        weight_grad_kernel,
        grid=(width // part,),
        in_specs=in_specs,
        out_specs=block,
        out_shape=jax.ShapeDtypeStruct((width, D), low),
        compiler_params=pltpu.CompilerParams(vmem_limit_bytes=32 * 2**20),
        cost_estimate=pl.CostEstimate(flops=4 * 10**9, bytes_accessed=1000, transcendentals=0),
        name="weight_grad",
    )(*args)


def packed_gram(matrix):
    gram = contract(matrix, matrix, 0, 0)
    panels = [gram[: at + LANES, at : at + LANES] for at in range(0, D, LANES)]
    return jnp.concatenate(panels, axis=0)


def schulz_kernel(panels_ref, matrix_ref, out_ref, gram_ref, low_ref, mix_ref, once_ref, it_ref):
    one, two, three = schulz_coeffs
    blocks = D // LANES
    diagonal = lax.broadcasted_iota(jnp.int32, (LANES, LANES), 0) == lax.broadcasted_iota(
        jnp.int32, (LANES, LANES), 1
    )
    trace = jnp.zeros((1, 1), full)
    first = 0
    for col in range(blocks):
        for row in range(col + 1):
            block = panels_ref[first : first + LANES, :].astype(full)
            first += LANES
            rows = slice(row * LANES, (row + 1) * LANES)
            cols = slice(col * LANES, (col + 1) * LANES)
            gram_ref[rows, cols] = block
            if row < col:
                gram_ref[cols, rows] = block.T
            else:
                mine = jnp.where(diagonal, block, 0.0)
                trace = trace + jnp.sum(jnp.sum(mine, axis=1, keepdims=True), axis=0, keepdims=True)
    shrink = 1.0 / (jnp.sqrt(trace) + 1e-07)
    cuts = [slice(at, at + SCHULZ_CUT) for at in range(0, D, SCHULZ_CUT)]
    its = [slice(at, at + SCHULZ_ITS) for at in range(0, matrix_ref.shape[0], SCHULZ_ITS)]
    for cut in cuts:
        gram = gram_ref[cut, :] * (shrink * shrink)
        gram_ref[cut, :] = gram
        low_ref[cut, :] = gram.astype(low)
    for part in its:
        it_ref[part, :] = matrix_ref[part, :].astype(full) * shrink
    for step in range(NS_STEPS):
        for cut in cuts:
            square = contract(low_ref[cut, :], low_ref[...], 1, 0)
            mix_ref[cut, :] = (two * gram_ref[cut, :] + three * square).astype(low)
        for part in its:
            iterate = it_ref[part, :]
            iterate = one * iterate + contract(iterate.astype(low), mix_ref[...], 1, 0)
            if step < NS_STEPS - 1:
                it_ref[part, :] = iterate
            else:
                out_ref[part, :] = iterate.astype(low)
        if step < NS_STEPS - 1:
            for cut in cuts:
                once = contract(mix_ref[cut, :], low_ref[...], 1, 0)
                gram_ref[cut, :] = one * one * gram_ref[cut, :] + 2.0 * one * once
                once_ref[cut, :] = once.astype(low)
            for cut in cuts:
                gram = gram_ref[cut, :] + contract(once_ref[cut, :], mix_ref[...], 1, 0)
                gram_ref[cut, :] = gram
            for cut in cuts:
                low_ref[cut, :] = gram_ref[cut, :].astype(low)


SCHULZ_CUT = 256
SCHULZ_ITS = 192


def schulz(panels, matrix):
    in_vmem = pl.BlockSpec(memory_space=pltpu.VMEM)
    return pl.pallas_call(
        schulz_kernel,
        in_specs=[in_vmem, in_vmem],
        out_specs=in_vmem,
        out_shape=jax.ShapeDtypeStruct(matrix.shape, low),
        scratch_shapes=[
            pltpu.VMEM((D, D), full),
            pltpu.VMEM((D, D), low),
            pltpu.VMEM((D, D), low),
            pltpu.VMEM((D, D), low),
            pltpu.VMEM(matrix.shape, full),
        ],
        compiler_params=pltpu.CompilerParams(vmem_limit_bytes=32 * 2**20),
        cost_estimate=pl.CostEstimate(flops=8 * 10**9, bytes_accessed=1000, transcendentals=0),
        name="schulz",
    )(panels, matrix)


def rows_qkv(value):
    kinds, depth, heads, cut = value.shape
    return value.transpose(0, 2, 3, 1).reshape(kinds * heads * cut, depth)


def unrows_qkv(rows, shape):
    kinds, depth, heads, cut = shape
    return rows.reshape(kinds, heads, cut, depth).transpose(0, 3, 1, 2)


def on_device(
    block_in,
    block_cot,
    cluster_perm,
    w_qkv,
    w_out,
    w_up,
    w_down,
    mom_qkv,
    mom_out,
    mom_up,
    mom_down,
    norm_params,
    norm_first,
    norm_second,
):
    ffn_here = lax.axis_index("ffn")
    seqs = lax.axis_size("seq")
    n_bits = len(seq_bits())
    here = block_in.shape[0]
    half = here // 2
    heads = w_out.shape[0]
    cut = w_out.shape[1]
    seq_len = cluster_perm.shape[2]
    clusters = seq_len // CLUSTER

    weights = [rows_qkv(w_qkv), w_out.reshape(heads * cut, D), w_up.T, w_down]
    momenta = [rows_qkv(mom_qkv), mom_out.reshape(heads * cut, D), mom_up.T, mom_down]

    wide_qkv = weights[0].astype(low)
    far_groups = seq_groups()[1:]

    def gather_group(values, bits):
        sent = jnp.concatenate(values, axis=0)
        return [swap(sent, "seq", mask) for mask in masks_of(bits)[1:]]

    def join_group(values, got):
        joined = []
        at = 0
        for value in values:
            joined.append(jnp.concatenate([value] + [other[at : at + value.shape[0]] for other in got], axis=0))
            at += value.shape[0]
        return joined

    got = gather_group([wide_qkv], far_groups[-1])
    tokens = [block_in, swap(block_in, "ffn", 1), swap(block_in, "ffn", 2)]
    tokens.append(swap(tokens[2], "ffn", 1))
    for bits in reversed(far_groups[:-1]):
        (wide_qkv,) = join_group([wide_qkv], got)
        got = gather_group([wide_qkv], bits)
    shards = [weights[2].astype(low), weights[3].astype(low), weights[1].astype(low)]
    shards, got = after((shards, got))
    (wide_qkv,) = join_group([wide_qkv], got)
    last_got = swap(wide_qkv, "seq", 1)
    for turn, bits in enumerate(reversed(far_groups)):
        got = gather_group(shards, bits)
        if turn == 0:
            got, last_got = after((got, last_got))
        shards = join_group(shards, got)
    up_rows, down_rows, out_wide = shards
    wide_qkv = jnp.concatenate([wide_qkv, last_got], axis=0)
    wide_qkv = wide_qkv.reshape(seqs, 3, heads, cut, D).transpose(1, 2, 0, 3, 4).reshape(3, heads, HD, D)
    head_rows = jnp.stack(
        [wide_qkv[0], wide_qkv[2], wide_qkv[1], jnp.zeros_like(wide_qkv[1])], axis=1
    ).reshape(heads * 2 * LANES, D)
    low_rows = down_rows.shape[0]
    shards = (up_rows, jnp.concatenate([down_rows, out_wide], axis=0))
    first_at = (("seq", 1), ("ffn", 2))
    then_at = (("ffn", 2), ("seq", 1))

    def swaps(values, places):
        return tuple(swap(value, *place) for value, place in zip(values, places))

    first_got = swaps(shards, first_at)

    perm = jnp.bitwise_xor(cluster_perm[0], ffn_here * here)
    kept = []
    o_sent = []
    far_got = []
    near_got = []
    for head in range(heads):
        mine = head_rows[head * 2 * LANES : (head + 1) * 2 * LANES]
        order_rows = perm[head : head + 1]
        if head == 1:
            order_rows, first_got, shards = after((order_rows, first_got, shards), kept[0])
            own_got = swaps(shards, then_at)
            up_pieces = [jnp.concatenate([shards[0], first_got[0]], axis=0)]
            up_pieces.append(swap(up_pieces[0], "ffn", 1))
        if head == 2:
            order_rows, own_got, first_got, far_got[0], up_pieces[1] = after(
                (order_rows, own_got, first_got, far_got[0], up_pieces[1]), kept[1]
            )
            other_got = swaps(first_got, then_at)
            near_got.append(send_on(o_sent[0][0], far_got[0][half:]))
            down_pieces = [jnp.concatenate([shards[1][:low_rows], own_got[1][:low_rows]], axis=0)]
            down_pieces.append(swap(down_pieces[0], "ffn", 1))
        own, near, far, qv, key = attend(order_rows, tokens, mine, "attend")
        kept.append((qv, key))
        o_sent.append((near, own))
        far_got.append(swap(far, "ffn", 2))
    other_got, far_got[1], near_got[0], down_pieces[1] = after(
        (other_got, far_got[1], near_got[0], down_pieces[1]), kept[2]
    )
    up_pieces.insert(1, jnp.concatenate([own_got[0], other_got[0]], axis=0))
    down_pieces.insert(1, jnp.concatenate([first_got[1][:low_rows], other_got[1][:low_rows]], axis=0))
    out_wide = jnp.concatenate(
        [value[low_rows:] for value in (shards[1], own_got[1], first_got[1], other_got[1])], axis=0
    )
    out_wide = spread(out_wide, [("ffn", 1)])
    up_pieces.append(swap(up_pieces[1], "ffn", 1))
    down_pieces.append(swap(down_pieces[1], "ffn", 1))
    near_got += [send_on(o_sent[head][0], far_got[head][half:]) for head in (1, 2)]
    o_got = [(sent[1], near, far) for sent, near, far in zip(o_sent, near_got, far_got)]
    up_rows, down_rows = up_pieces, down_pieces

    digits = (2, 2, 2) + (2,) * (n_bits - 1)
    order = (1, 0, 2 + n_bits, 2) + tuple(range(3, 2 + n_bits)) + (3 + n_bits, 4 + n_bits)
    back = tuple(sorted(range(len(order)), key=lambda at: order[at]))
    sizes = digits + (heads, cut, D)
    out_rows = out_wide.reshape(sizes).transpose(order).reshape(4 * heads * HD, D)

    do_blocks, tokenwise, norm_part = layer(
        o_got, block_in, block_cot, out_rows, up_rows, down_rows, norm_params
    )
    block_out, dresidual, gelu_a, gelu_b, dinner_a, dinner_b, dbranch, hidden_low, dattn, o_rows = tokenwise
    do_own, *do_near, far_first, far_rest = do_blocks
    do_far = [swap(far_first, "ffn", 2), swap(far_rest, "ffn", 2)]

    early_half = (cluster_perm[0] < seq_len // 2).astype(full).reshape(heads, clusters, CLUSTER)
    share = lax.dynamic_update_slice(
        jnp.zeros((4 * heads, clusters), full), jnp.sum(early_half, axis=2) / CLUSTER, (ffn_here * heads, 0)
    ).reshape(1, 4 * heads * clusters)
    small = jnp.concatenate([norm_part, jnp.pad(share, ((0, 0), (0, D - share.shape[1])))])

    down_sent = weight_grad(gelu_b, dbranch)
    dinner_b, do_far[0] = after((dinner_b, do_far[0]), down_sent)
    do_near[0] = send_on(do_near[0], do_far[0][:, 1:], 1)
    up_sent = weight_grad(dinner_b, hidden_low)
    part_out = weight_grad(o_rows, dattn)
    part_out = part_out.reshape(tuple(sizes[at] for at in order)).transpose(back)
    part_out = part_out.reshape(4 * heads * HD, D)
    out_kept, out_sent = cut_outer(part_out)
    down_got, up_got, out_got = [swap(value, "ffn", 1) for value in (down_sent, up_sent, out_sent)]
    down_got, do_far[1] = after((down_got, do_far[1]))
    do_near[1] = send_on(do_near[1], do_far[1][:, 1:], 1)
    small = small + swap(after(small, down_got), "ffn", 1)
    down_sum = weight_grad(gelu_a, dbranch, down_got)
    up_got, do_near[0], out_got = after((up_got, do_near[0], out_got), down_sum)
    up_sum = weight_grad(dinner_a, hidden_low, up_got)
    out_sum = add_low(out_kept, out_got)

    def quarters(value):
        rows = value.shape[0] // 4
        return [value[part * rows : (part + 1) * rows] for part in range(4)]

    low_sums = [jnp.concatenate(pair, axis=0) for pair in zip(quarters(down_sum), quarters(out_sum))]
    up_sums = [quarters(up_sum)[part] for part in (0, 2, 1, 3)]
    sums = list(zip(up_sums, low_sums))
    places = (("ffn", 2), ("seq", 1))
    then_places = (("seq", 1), ("ffn", 2))

    def send_groups(values, bits):
        masks = masks_of(bits)
        cuts = [cut_many(value, len(masks)) for value in values]
        sent = [jnp.concatenate([parts[turn] for parts in cuts], axis=0) for turn in range(1, len(masks))]
        got = [swap(value, "seq", mask) for value, mask in zip(sent, masks[1:])]
        return [parts[0] for parts in cuts], got

    def add_groups(own, got):
        values = []
        at = 0
        for part in own:
            values.append(add_many(part, [other[at : at + part.shape[0]] for other in got]).astype(low))
            at += part.shape[0]
        return values

    def small_step(bit):
        return small + swap(small, "seq", bit)

    do_near[0] = after(do_near[0], sums)
    part_heads = []
    dboth = []
    for head in range(heads):
        if head == 0:
            first_got = swaps(sums[3], places)
            small_got = swap(small, "ffn", 2)
        if head == 1:
            do_near[1], first_got, small_got = after((do_near[1], first_got, small_got), part_heads[0])
            then_sent = [add_low(value, other) for value, other in zip(sums[2], first_got)]
            second_got = swaps(sums[1], places)
            then_got = swaps(then_sent, then_places)
            small = small + small_got
            small_got = swap(small, "seq", 1)
        if head == 2:
            do_near[1], second_got, then_got, small_got = after(
                (do_near[1], second_got, then_got, small_got), part_heads[1]
            )
            up_sum, low_sum = [
                (value.astype(full) + second.astype(full) + then.astype(full)).astype(low)
                for value, second, then in zip(sums[0], second_got, then_got)
            ]
            small = small + small_got
            rest = [up_sum, low_sum[:low_rows], low_sum[low_rows:]]
            own, rest_got = send_groups(rest, far_groups[0])
            small_got = swap(small, "seq", 2)
        do = (do_own, do_near[min(head, 1)], do_far[min(head, 1)])
        gw, both = attend_back(perm[head : head + 1], head, kept[head], do, tokens)
        part_heads.append(gw)
        dboth.append(both)
    small_got, dboth = after((small_got, dboth), part_heads[2])
    small = small + small_got
    part_qkv = jnp.stack(part_heads).reshape(heads, 4, HD, D)
    part_qkv = jnp.stack([part_qkv[:, 0], part_qkv[:, 2], part_qkv[:, 1]])
    part_qkv = part_qkv.reshape(3, heads, seqs, cut, D).transpose(2, 0, 1, 3, 4)
    qkv_kept, qkv_sent = cut_outer(part_qkv.reshape(seqs * 3 * heads * cut, D))
    qkv_got = swap(qkv_sent, "seq", 1)
    gx_kept, gx_sent = token_grad(dboth, head_rows, here)
    qkv_got, gx_kept, gx_sent, rest_got = after((qkv_got, gx_kept, gx_sent, rest_got))
    qkv_sum = add_low(qkv_kept, qkv_got)
    rest = add_groups(own, rest_got)
    gx_got = swap(gx_sent, "ffn", 1)
    for turn, bits in enumerate(far_groups):
        if turn > 0:
            rest = add_groups(*send_groups(rest, bits))
        qkv_own, qkv_got = send_groups([qkv_sum], bits)
        if turn == 0:
            qkv_got, gx_got = after((qkv_got, gx_got))
            gx_kept, gx_sent = cut_outer(add_low(gx_kept, gx_got))
        (qkv_sum,) = add_groups(qkv_own, qkv_got)
        for bit in bits:
            if bit > 2:
                small = small_step(bit)
    up_sum, down_sum, out_sum = rest
    grad_qkv, grad_out, grad_up, grad_down = [
        value.astype(full) for value in (qkv_sum, out_sum, up_sum, down_sum)
    ]
    grads = [grad_qkv, grad_out, grad_up, grad_down]
    moments = [0.5 * mom + grad for mom, grad in zip(momenta, grads)]
    most = max(moment.shape[0] for moment in moments)
    stack = jnp.stack(
        [jnp.pad(moment.astype(low), ((0, most - moment.shape[0]), (0, 0))) for moment in moments]
    )

    def pick(turn):
        return lax.dynamic_index_in_dim(stack, jnp.bitwise_xor(ffn_here, turn), keepdims=False)

    picked = [swap(pick(turn), "ffn", turn) for turn in (1, 2, 3)]
    picked, gx_sent = after((picked, gx_sent))
    matrix = jnp.concatenate([pick(0)] + picked, axis=0)
    gx_first, gx_second = [swap(value, "ffn", 2) for value in cut_outer(gx_sent)]
    panels = sum_parts(packed_gram(matrix).astype(low))
    panels, gx_first = after((panels, gx_first))
    panels, gx_second = spread_parts(panels, gx_second)
    panels, small = after((panels, small))
    gx_other = jnp.concatenate([gx_first, gx_second], axis=0)
    steps = schulz(panels, matrix).reshape(4, most, D)
    input_grad = dresidual + (gx_kept.astype(full) + gx_other.astype(full))
    home = jnp.stack([steps[0]] + [swap(steps[turn], "ffn", turn) for turn in (1, 2, 3)])
    step_rates = (
        0.5 * math.sqrt(3.0),
        0.5 * math.sqrt(CLUSTER / 3.0),
        0.5 * math.sqrt(FF / D),
        0.5,
    )
    masters = []
    for member in range(4):
        own = lax.dynamic_index_in_dim(home, jnp.bitwise_xor(ffn_here, member), keepdims=False)
        own = own[: moments[member].shape[0]].astype(full)
        masters.append(weights[member] - step_rates[member] * own)

    grad_norm = small[:4]
    occupancy = small[4, : 4 * heads * clusters].reshape(4 * heads, clusters)
    first_fix = 1.0 - 0.9**ADAM_STEP
    second_fix = 1.0 - 0.999**ADAM_STEP
    first_new = 0.9 * norm_first + 0.1 * grad_norm
    second_new = 0.999 * norm_second + 0.001 * grad_norm * grad_norm
    first_hat = first_new / first_fix
    second_hat = second_new / second_fix
    norm_new = norm_params - 0.5 * (first_hat / (jnp.sqrt(second_hat) + 1e-08) + 0.01 * norm_params)

    def shaped(four):
        return (unrows_qkv(four[0], w_qkv.shape), four[1].reshape(w_out.shape), four[2].T, four[3])

    return (
        (block_out, input_grad)
        + shaped(grads)
        + (grad_norm,)
        + shaped(moments)
        + shaped(masters)
        + (first_new, second_new, norm_new, occupancy)
    )


def solution(mesh):
    rows = P(("seq", "ffn"), None)
    placed = (
        rows,
        rows,
        P("seq", "ffn", None),
        P(None, None, "ffn", "seq"),
        P("ffn", "seq", None),
        P(None, ("seq", "ffn")),
        rows,
        P(None, None, "ffn", "seq"),
        P("ffn", "seq", None),
        P(None, ("seq", "ffn")),
        rows,
        P(),
        P(),
        P(),
    )
    four = placed[3:7]
    return jax.shard_map(
        on_device,
        mesh=mesh,
        in_specs=placed,
        out_specs=(rows, rows) + four + (P(),) + four + four + (P(), P(), P(), P()),
        check_vma=False,
    )
```

```python
import math

import jax
import jax.numpy as jnp
from jax import lax
from jax.experimental import pallas as pl
from jax.experimental.pallas import tpu as pltpu
from jax.sharding import PartitionSpec as P

D = 768
HD = 64
FF = 3072
CLUSTER = 128
NS_STEPS = 3
ADAM_STEP = 10

schulz_coeffs = (3.4445, -4.775, 2.0315)
norm_epsilon = 1e-05
low = jnp.bfloat16
full = jnp.float32
LANES = 128
GROUP = 4
score_scale = 1.0 / math.sqrt(HD)


def contract(left, right, left_axis, right_axis):
    return lax.dot_general(
        left, right, (((left_axis,), (right_axis,)), ((), ())), preferred_element_type=full
    )


def swap(value, axis, bit):
    size = lax.axis_size(axis)
    return lax.ppermute(value, axis, [(place, place ^ bit) for place in range(size)])


def seq_bits():
    bits = []
    bit = lax.axis_size("seq") // 2
    while bit >= 1:
        bits.append(bit)
        bit //= 2
    return bits


def seq_stages():
    return [("seq", bit) for bit in seq_bits()]


def far_stages():
    return [("seq", bit) for bit in seq_bits() if bit > 1]


def spread(shard, stages):
    for axis, bit in stages:
        shard = jnp.concatenate([shard, swap(shard, axis, bit)], axis=0)
    return shard


def fold(partial, stages):
    for axis, bit in reversed(stages):
        half = partial.shape[0] // 2
        kept = partial[:half]
        other = swap(partial[half:].astype(low), axis, bit)
        partial = kept.astype(full) + other.astype(full)
    return partial


def after(values, *tokens):
    return lax.optimization_barrier((values, tokens))[0]


def join_inner(near, other):
    rows = near.shape[0] // 2
    return jnp.concatenate([near[:rows], other[:rows], near[rows:], other[rows:]], axis=0)


def cut_outer(value):
    half = value.shape[0] // 2
    return value[:half], value[half:]


def cut_inner(value):
    rows = value.shape[0] // 4
    quarters = [value[part * rows : (part + 1) * rows] for part in range(4)]
    return tuple(jnp.concatenate(quarters[side::2], axis=0) for side in range(2))


def add_low(kept, other):
    return (kept.astype(full) + other.astype(full)).astype(low)


def fold_step(value, cut, axis, bit):
    kept, sent = cut(value)
    return add_low(kept, swap(sent, axis, bit))


def send_on(near, far_got, axis=0):
    return swap(jnp.concatenate([near, far_got], axis=axis), "ffn", 1)


def add_many(first, others):
    value = first.astype(full)
    for other in others:
        value = value + other.astype(full)
    return value


def seq_groups():
    bits = sorted(seq_bits())
    return [tuple(bits[:1])] + [tuple(bits[at : at + 2]) for at in range(1, len(bits), 2)]


def masks_of(bits):
    masks = [0]
    for bit in bits:
        masks = [mask | more for mask in masks for more in (0, bit)]
    return masks


def cut_many(value, count):
    rows = value.shape[0] // count
    return [value[part * rows : (part + 1) * rows] for part in range(count)]


def place_in(bits):
    me = lax.axis_index("seq")
    place = 0
    for bit in bits:
        place = 2 * place + ((me & bit) != 0).astype(jnp.int32)
    return place


def sum_parts(value):
    for bits in seq_groups():
        masks = masks_of(bits)
        place = place_in(bits)
        parts = value.reshape((len(masks), value.shape[0] // len(masks)) + value.shape[1:])

        def part(turn):
            return lax.dynamic_index_in_dim(parts, jnp.bitwise_xor(place, turn), keepdims=False)

        got = [swap(part(turn), "seq", masks[turn]) for turn in range(1, len(masks))]
        value = add_many(part(0), got).astype(low)
    return value


def spread_parts(value, beside, later):
    for turn, bits in enumerate(reversed(seq_groups())):
        masks = masks_of(bits)
        got = [value] + [swap(value, "seq", mask) for mask in masks[1:]]
        if turn == 0:
            got, beside = after((got, beside))
        if turn == len(seq_groups()) - 1:
            got, later = after((got, later))
        me = lax.axis_index("seq")
        for at, bit in enumerate(bits):
            flip = 2 ** (len(bits) - 1 - at)
            side = (me & bit) != 0
            got = [jnp.where(side, got[turn ^ flip], got[turn]) for turn in range(len(masks))]
        value = jnp.concatenate(got, axis=0)
    return value, beside, later


def in_turns(perm_ref, seq_len, fetch, work, place):
    count = GROUP * CLUSTER
    groups = seq_len // count

    def rows_of(turn):
        return pl.multiple_of(jnp.clip(turn, 0, groups - 1) * count, count)

    def fetch_some(side, turn, rows):
        base = rows_of(turn)
        for row in rows:
            fetch(side, perm_ref[0, base + row], row)

    def place_some(side, turn, rows):
        base = rows_of(turn)
        for row in rows:
            place(side, perm_ref[0, base + row], row)

    def step(pair, carry):
        for side in range(2):
            turn = 2 * pair + side
            done = 0
            for at in work(side, rows_of(turn)):
                rows = range(done, min(count, int(at * count)))
                fetch_some(1 - side, turn + 1, rows)
                place_some(1 - side, turn - 1, rows)
                done = max(done, rows.stop)
            fetch_some(1 - side, turn + 1, range(done, count))
            place_some(1 - side, turn - 1, range(done, count))
        return carry

    fetch_some(0, 0, range(count))
    lax.fori_loop(0, groups // 2, step, 0)
    place_some(1, groups - 1, range(count))


def softmax_rows(scores):
    peak = jnp.max(scores, axis=1, keepdims=True)
    powers = jnp.exp((scores - peak) * score_scale)
    return powers * (1.0 / jnp.sum(powers, axis=1, keepdims=True))


def left_half(rows):
    return lax.broadcasted_iota(jnp.int32, (rows, LANES), 1) < HD


def attend_kernel(
    perm_ref, x0, x1, x2, x3, w_ref, own_ref, near_ref, far_ref, qv_ref, key_ref, qv_rows, key_rows, o_rows, *got
):
    qv_got, key_got, o_got = got[0:2], got[2:4], got[4:6]
    here = x0.shape[0]
    seq_len = 4 * here
    half = here // 2
    for block, x_ref in enumerate((x0, x1, x2, x3)):
        for cut in range(2):
            both = contract(x_ref[pl.ds(cut * half, half), :], w_ref[...], 1, 1)
            rows = pl.ds(block * here + cut * half, half)
            qv_rows[rows, :] = both[:, :LANES]
            key_rows[rows, :] = both[:, LANES:]
    spans = [slice(part * CLUSTER, (part + 1) * CLUSTER) for part in range(GROUP)]

    def fetch(side, index, row):
        qv_got[side][pl.ds(row, 1), :] = qv_rows[pl.ds(index, 1), :]
        key_got[side][pl.ds(row, 1), :] = key_rows[pl.ds(index, 1), :]

    def work(side, base):
        qvs = [qv_got[side][span].astype(low) for span in spans]
        keys = [key_got[side][span].astype(low) for span in spans]
        for part in range(GROUP):
            rows = pl.ds(base + part * CLUSTER, CLUSTER)
            qv_ref[rows, :] = qvs[part]
            key_ref[rows, :] = keys[part]
        scores = [contract(qv, key, 1, 1) for qv, key in zip(qvs, keys)]
        yield 0.3
        probs = []
        for part in range(GROUP):
            probs.append(softmax_rows(scores[part]).astype(low))
            yield 0.3 + 0.6 * (part + 1) / GROUP
        for part in range(GROUP):
            o_got[side][spans[part]] = contract(probs[part], qvs[part], 1, 0)

    def place(side, index, row):
        o_rows[pl.ds(index, 1), :] = o_got[side][pl.ds(row, 1), :]

    in_turns(perm_ref, seq_len, fetch, work, place)
    outs = (own_ref, near_ref, far_ref.at[pl.ds(0, half), :], far_ref.at[pl.ds(half, half), :])
    for block, out_ref in enumerate(outs):
        top = pltpu.roll(o_rows[pl.ds(block * here, half), :], HD, 1)
        bottom = o_rows[pl.ds(block * here + half, half), :]
        out_ref[...] = jnp.where(left_half(half), top, bottom).astype(low)


def vmem(*shape):
    return pl.BlockSpec(shape, memory_space=pltpu.VMEM)


def attend(perm, tokens, weights, name):
    seq_len = perm.shape[1]
    here = tokens[0].shape[0]
    rows_got = pltpu.VMEM((GROUP * CLUSTER, LANES), full)
    rows_all = pltpu.VMEM((seq_len, LANES), full)
    in_vmem = pl.BlockSpec(memory_space=pltpu.VMEM)
    return pl.pallas_call(
        attend_kernel,
        in_specs=[pl.BlockSpec(memory_space=pltpu.SMEM)] + [in_vmem] * 5,
        out_specs=[in_vmem] * 5,
        out_shape=[
            jax.ShapeDtypeStruct((here // 2, LANES), low),
            jax.ShapeDtypeStruct((here // 2, LANES), low),
            jax.ShapeDtypeStruct((here, LANES), low),
            jax.ShapeDtypeStruct((seq_len, LANES), low),
            jax.ShapeDtypeStruct((seq_len, LANES), low),
        ],
        scratch_shapes=[rows_all] * 3 + [rows_got] * 6,
        compiler_params=pltpu.CompilerParams(vmem_limit_bytes=40 * 2**20),
        cost_estimate=pl.CostEstimate(flops=18 * 10**9, bytes_accessed=1000, transcendentals=0),
        name=name,
    )(perm, *tokens, weights)


def attend_back_kernel(
    perm_ref, qv_ref, key_ref, do0, do1, do2, do3, x0, x1, x2, x3, gw_ref, dboth_ref, d_rows, dqv_rows, dkey_rows, *got
):
    d_got, dqv_got, dkey_got = got[0:2], got[2:4], got[4:6]
    here = x0.shape[0]
    seq_len = 4 * here
    half = here // 2
    for block, do_ref in enumerate((do0, do1, do2, do3)):
        rows = do_ref[...].astype(full)
        top = pltpu.roll(rows, HD, 1)
        d_rows[pl.ds(block * here, half), :] = jnp.where(left_half(half), 0.0, top)
        d_rows[pl.ds(block * here + half, half), :] = jnp.where(left_half(half), 0.0, rows)
    spans = [slice(part * CLUSTER, (part + 1) * CLUSTER) for part in range(GROUP)]

    def fetch(side, index, row):
        d_got[side][pl.ds(row, 1), :] = d_rows[pl.ds(index, 1), :]

    def work(side, base):
        rows = [pl.ds(base + part * CLUSTER, CLUSTER) for part in range(GROUP)]
        qvs = [qv_ref[span, :] for span in rows]
        keys = [key_ref[span, :] for span in rows]
        dos = [d_got[side][span].astype(low) for span in spans]
        scores = [contract(qv, key, 1, 1) for qv, key in zip(qvs, keys)]
        dprobs = [contract(do, qv, 1, 1) for do, qv in zip(dos, qvs)]
        yield 0.2
        probs = []
        for part in range(GROUP):
            probs.append(softmax_rows(scores[part]))
            yield 0.2 + 0.3 * (part + 1) / GROUP
        probs_low = [prob.astype(low) for prob in probs]
        dscores = []
        for prob, dprob in zip(probs, dprobs):
            dscores.append((prob * (dprob - jnp.sum(prob * dprob, axis=1, keepdims=True))).astype(low))
            yield 0.5 + 0.3 * len(dscores) / GROUP
        for part in range(GROUP):
            dqv_got[side][spans[part]] = score_scale * contract(dscores[part], keys[part], 1, 0) + contract(
                probs_low[part], dos[part], 0, 0
            )
            dkey_got[side][spans[part]] = score_scale * contract(dscores[part], qvs[part], 0, 0)

    def place(side, index, row):
        dqv_rows[pl.ds(index, 1), :] = dqv_got[side][pl.ds(row, 1), :]
        dkey_rows[pl.ds(index, 1), :] = dkey_got[side][pl.ds(row, 1), :]

    in_turns(perm_ref, seq_len, fetch, work, place)
    gw = jnp.zeros((2 * LANES, D), full)
    for block, x_ref in enumerate((x0, x1, x2, x3)):
        rows = pl.ds(block * here, here)
        dboth_ref[rows, :LANES] = dqv_rows[rows, :].astype(low)
        dboth_ref[rows, LANES:] = dkey_rows[rows, :].astype(low)
        gw = gw + contract(dboth_ref[rows, :], x_ref[...], 0, 0)
    gw_ref[...] = gw.astype(low)


def attend_back(perm, head, kept, do, tokens):
    seq_len = perm.shape[1]
    here = tokens[0].shape[0]
    half = here // 2
    rows_got = pltpu.VMEM((GROUP * CLUSTER, LANES), full)
    rows_all = pltpu.VMEM((seq_len, LANES), full)
    in_vmem = pl.BlockSpec(memory_space=pltpu.VMEM)
    own, near, far = do

    at = head if near.shape[0] > 1 else 0

    def part(at, turn):
        return pl.BlockSpec((None, None, half, LANES), lambda step: (at, turn, 0, 0))


    return pl.pallas_call(
        attend_back_kernel,
        grid=(1,),
        in_specs=[pl.BlockSpec(memory_space=pltpu.SMEM)]
        + [in_vmem] * 2
        + [part(head, 0), part(at, 0), part(at, 0), part(at, 1)]
        + [in_vmem] * 4,
        out_specs=[in_vmem] * 2,
        out_shape=[
            jax.ShapeDtypeStruct((2 * LANES, D), low),
            jax.ShapeDtypeStruct((seq_len, 2 * LANES), low),
        ],
        scratch_shapes=[rows_all] * 3 + [rows_got] * 6,
        compiler_params=pltpu.CompilerParams(vmem_limit_bytes=40 * 2**20),
        cost_estimate=pl.CostEstimate(flops=22 * 10**9, bytes_accessed=1000, transcendentals=0),
        name="attend_back",
    )(perm, *kept, own, near, far, near, *tokens)


def token_grad_kernel(d0, d1, d2, w_ref, kept_ref, sent_ref):
    sums = None
    for head, d_ref in enumerate((d0, d1, d2)):
        piece = contract(d_ref[...], w_ref[pl.ds(head * 2 * LANES, 2 * LANES), :], 1, 0)
        sums = piece if sums is None else sums + piece

    @pl.when(pl.program_id(0) < 2)
    def _():
        sent_ref[...] = sums.astype(low)

    @pl.when(pl.program_id(0) >= 2)
    def _():
        kept_ref[...] = sums.astype(low)


def token_grad(dboth, weights, here):
    split = 2
    rows = here // split

    def from_block(slot, part):
        return ((2 * (slot % 2) + 1 - slot // 2) * split + part, 0)

    def to_sent(slot, part):
        return (jnp.minimum(slot * split + part, 2 * split - 1), 0)

    def to_kept(slot, part):
        return (jnp.maximum(slot * split + part - 2 * split, 0), 0)

    return pl.pallas_call(
        token_grad_kernel,
        grid=(4, split),
        in_specs=[pl.BlockSpec((rows, 2 * LANES), from_block)] * 3
        + [pl.BlockSpec((6 * LANES, D), lambda slot, part: (0, 0))],
        out_specs=[pl.BlockSpec((rows, D), to_kept), pl.BlockSpec((rows, D), to_sent)],
        out_shape=[jax.ShapeDtypeStruct((2 * here, D), low)] * 2,
        compiler_params=pltpu.CompilerParams(vmem_limit_bytes=32 * 2**20),
        cost_estimate=pl.CostEstimate(flops=8 * 10**9, bytes_accessed=1000, transcendentals=0),
        name="token_grad",
    )(*dboth, weights)


def row_mean(value):
    return jnp.mean(value, axis=-1, keepdims=True)


def norm_forward(inputs, gains, biases):
    center = inputs - row_mean(inputs)
    inv_std = lax.rsqrt(row_mean(center * center) + norm_epsilon)
    normed = center * inv_std
    return (normed * gains + biases, normed, inv_std)


def norm_backward(upstream, normed, inv_std, gains):
    scaled = upstream * gains
    inside = scaled - row_mean(scaled) - normed * row_mean(scaled * normed)
    sums = [jnp.sum(upstream * normed, axis=0, keepdims=True), jnp.sum(upstream, axis=0, keepdims=True)]
    return (inside * inv_std, sums)


def layer_kernel(heads, *refs):
    o_refs = refs[: 4 * heads]
    (x_ref, cot_ref, wo_ref, norm_ref) = refs[4 * heads : 4 * heads + 4]
    up_refs = refs[4 * heads + 4 : 4 * heads + 8]
    down_refs = refs[4 * heads + 8 : 4 * heads + 12]
    outs = refs[4 * heads + 12 :]
    do_own, near_first, near_last, far_first, far_last, block_ref, da_ref = outs[:7]
    g_refs = outs[7:9]
    du_refs = outs[9:11]
    (df_ref, hb_ref, dattn_ref, o_ref, sums_ref, slope_ref) = outs[11:]

    def store_do(head, turn, value):
        near, far, at = (near_first, far_first, head) if head < heads - 1 else (near_last, far_last, 0)
        if turn == 0:
            do_own[head, 0] = value
        elif turn == 1:
            near[at, 0] = value
        else:
            far[at, turn - 2] = value
    part = x_ref.shape[1]
    rows = 2 * part
    left = left_half(part)

    def load(ref):
        return jnp.concatenate([ref[0], ref[1]], axis=0)

    def store(ref, value):
        ref[0] = value[:part]
        ref[1] = value[part:]

    packed = []
    for turn in range(4):
        for head in range(heads):
            packed.append(o_refs[4 * head + turn][...].astype(full))
    for pair in range(len(packed) // 2):
        first, second = packed[2 * pair], packed[2 * pair + 1]
        lanes = slice(pair * LANES, (pair + 1) * LANES)
        o_ref[0, :, lanes] = jnp.where(left, first, pltpu.roll(second, HD, 1)).astype(low)
        o_ref[1, :, lanes] = jnp.where(left, pltpu.roll(first, HD, 1), second).astype(low)

    gain_a, bias_a = norm_ref[0:1, :], norm_ref[1:2, :]
    gain_b, bias_b = norm_ref[2:3, :], norm_ref[3:4, :]
    residual = load(x_ref).astype(full) + contract(load(o_ref), wo_ref[...], 1, 0)
    hidden, normed_a, inv_a = norm_forward(residual, gain_a, bias_a)
    hidden_low = hidden.astype(low)
    store(hb_ref, hidden_low)
    branch = jnp.zeros((rows, D), full)
    quarter = FF // 4
    cuts = [slice(at, at + quarter) for at in range(0, FF, quarter)]
    for turn, cut in enumerate(cuts):
        side = turn // 2
        columns = slice(turn % 2 * quarter, (turn % 2 + 1) * quarter)
        preact = contract(hidden_low, up_refs[turn][...], 1, 1)
        cumulative = 0.5 * (1.0 + lax.erf(preact * 0.7071067811865476))
        gelu_low = (preact * cumulative).astype(low)
        slope_ref[:, cut] = cumulative + preact * (jnp.exp(-0.5 * preact * preact) * 0.3989422804014327)
        g_refs[side][0, :, columns] = gelu_low[:part]
        g_refs[side][1, :, columns] = gelu_low[part:]
        branch = branch + contract(gelu_low, down_refs[turn][...], 1, 0)
    outputs, normed_b, inv_b = norm_forward(hidden + branch, gain_b, bias_b)
    store(block_ref, outputs.astype(low))
    dsum, sums_b = norm_backward(load(cot_ref).astype(full), normed_b, inv_b, gain_b)
    dsum_low = dsum.astype(low)
    store(df_ref, dsum_low)
    dhidden = dsum
    for turn, cut in enumerate(cuts):
        side = turn // 2
        columns = slice(turn % 2 * quarter, (turn % 2 + 1) * quarter)
        dinner = (contract(dsum_low, down_refs[turn][...], 1, 1) * slope_ref[:, cut]).astype(low)
        du_refs[side][0, :, columns] = dinner[:part]
        du_refs[side][1, :, columns] = dinner[part:]
        dhidden = dhidden + contract(dinner, up_refs[turn][...], 1, 0)
    dresidual, sums_a = norm_backward(dhidden, normed_a, inv_a, gain_a)
    store(da_ref, dresidual)
    dattn = dresidual.astype(low)
    store(dattn_ref, dattn)
    dheads = contract(dattn, wo_ref[...], 1, 1)
    for pair in range(len(packed) // 2):
        lanes = slice(pair * LANES, (pair + 1) * LANES)
        top, bottom = dheads[:part, lanes], dheads[part:, lanes]
        both = (
            jnp.where(left, top, pltpu.roll(bottom, HD, 1)).astype(low),
            jnp.where(left, pltpu.roll(top, HD, 1), bottom).astype(low),
        )
        for side in range(2):
            turn, head = divmod(2 * pair + side, heads)
            store_do(head, turn, both[side])
    sums = jnp.concatenate(sums_a + sums_b, axis=0)

    @pl.when(pl.program_id(0) == 0)
    def _():
        sums_ref[...] = sums

    @pl.when(pl.program_id(0) > 0)
    def _():
        sums_ref[...] += sums


LAYER_STEPS = 4


def layer(o_got, block_in, block_cot, out_rows, up_rows, down_rows, norm_params):
    heads = len(o_got)
    here = block_in.shape[0]
    half = here // 2
    part = half // LAYER_STEPS
    once = pl.Buffered(1)

    def lead(count, width):
        return pl.BlockSpec((count, part, width), lambda step: (0, step, 0))

    do_sizes = ((heads, 1), (heads - 1, 1), (1, 1), (heads - 1, 2), (1, 2))

    def do_part(count, turns):
        return pl.BlockSpec((count, turns, part, LANES), lambda step: (0, 0, step, 0))

    def still(rows):
        return pl.BlockSpec((rows, D), lambda step: (0, 0), pipeline_mode=once)

    def pairs(width, kind):
        return jax.ShapeDtypeStruct((2, half, width), kind)

    o_args = [piece for own, near, far in o_got for piece in (own, near, far, near)]
    later = pl.BlockSpec((part, LANES), lambda step: (step + LAYER_STEPS, 0))
    lanes = pl.BlockSpec((part, LANES), lambda step: (step, 0))
    two = lead(2, D)
    wide = lead(2, FF // 2)
    flat = pl.pallas_call(
        lambda *refs: layer_kernel(heads, *refs),
        grid=(LAYER_STEPS,),
        in_specs=[lanes, lanes, lanes, later] * heads
        + [two, two, still(D), still(4)]
        + [still(FF // 4)] * 8,
        out_specs=[do_part(*sizes) for sizes in do_sizes] + [two, two] + [wide] * 4 + [two] * 4
        + [pl.BlockSpec((4, D), lambda step: (0, 0))],
        out_shape=[jax.ShapeDtypeStruct((count, turns, half, LANES), low) for count, turns in do_sizes]
        + [
            pairs(D, low),
            pairs(D, full),
            pairs(FF // 2, low),
            pairs(FF // 2, low),
            pairs(FF // 2, low),
            pairs(FF // 2, low),
            pairs(D, low),
            pairs(D, low),
            pairs(D, low),
            pairs(D, low),
            jax.ShapeDtypeStruct((4, D), full),
        ],
        scratch_shapes=[pltpu.VMEM((2 * part, FF), full)],
        compiler_params=pltpu.CompilerParams(vmem_limit_bytes=60 * 2**20),
        cost_estimate=pl.CostEstimate(flops=40 * 10**9, bytes_accessed=1000, transcendentals=0),
        name="layer",
    )(
        *o_args,
        block_in.reshape(2, half, D),
        block_cot.reshape(2, half, D),
        out_rows,
        norm_params,
        *up_rows,
        *down_rows,
    )
    tokenwise = [value.reshape(here, value.shape[2]) for value in flat[5:-1]]
    return flat[:5], tokenwise, flat[-1]


def weight_grad_kernel(left_ref, right_ref, *refs):
    value = contract(left_ref[...], right_ref[...], 0, 0)
    if len(refs) > 1:
        value = value + refs[0][...].astype(full)
    refs[-1][...] = value.astype(low)


def weight_grad(left, right, other=None):
    rows, width = left.shape
    part = 384
    args = [left, right]
    in_specs = [
        pl.BlockSpec((rows, part), lambda step: (0, step)),
        pl.BlockSpec((rows, D), lambda step: (0, 0)),
    ]
    block = pl.BlockSpec((part, D), lambda step: (step, 0))
    if other is not None:
        args.append(other)
        in_specs.append(block)
    return pl.pallas_call(
        weight_grad_kernel,
        grid=(width // part,),
        in_specs=in_specs,
        out_specs=block,
        out_shape=jax.ShapeDtypeStruct((width, D), low),
        compiler_params=pltpu.CompilerParams(vmem_limit_bytes=32 * 2**20),
        cost_estimate=pl.CostEstimate(flops=4 * 10**9, bytes_accessed=1000, transcendentals=0),
        name="weight_grad",
    )(*args)


def packed_gram(matrix):
    gram = contract(matrix, matrix, 0, 0)
    panels = [gram[: at + LANES, at : at + LANES] for at in range(0, D, LANES)]
    return jnp.concatenate(panels, axis=0)


def schulz_kernel(panels_ref, matrix_ref, out_ref, gram_ref, low_ref, mix_ref, once_ref, it_ref):
    one, two, three = schulz_coeffs
    blocks = D // LANES
    diagonal = lax.broadcasted_iota(jnp.int32, (LANES, LANES), 0) == lax.broadcasted_iota(
        jnp.int32, (LANES, LANES), 1
    )
    trace = jnp.zeros((1, 1), full)
    first = 0
    for col in range(blocks):
        for row in range(col + 1):
            block = panels_ref[first : first + LANES, :].astype(full)
            first += LANES
            rows = slice(row * LANES, (row + 1) * LANES)
            cols = slice(col * LANES, (col + 1) * LANES)
            gram_ref[rows, cols] = block
            if row < col:
                gram_ref[cols, rows] = block.T
            else:
                mine = jnp.where(diagonal, block, 0.0)
                trace = trace + jnp.sum(jnp.sum(mine, axis=1, keepdims=True), axis=0, keepdims=True)
    shrink = 1.0 / (jnp.sqrt(trace) + 1e-07)
    cuts = [slice(at, at + SCHULZ_CUT) for at in range(0, D, SCHULZ_CUT)]
    its = [slice(at, at + SCHULZ_ITS) for at in range(0, matrix_ref.shape[0], SCHULZ_ITS)]
    for cut in cuts:
        gram = gram_ref[cut, :] * (shrink * shrink)
        gram_ref[cut, :] = gram
        low_ref[cut, :] = gram.astype(low)
    for part in its:
        it_ref[part, :] = matrix_ref[part, :].astype(full) * shrink
    for step in range(NS_STEPS):
        for cut in cuts:
            square = contract(low_ref[cut, :], low_ref[...], 1, 0)
            mix_ref[cut, :] = (two * gram_ref[cut, :] + three * square).astype(low)
        for part in its:
            iterate = it_ref[part, :]
            iterate = one * iterate + contract(iterate.astype(low), mix_ref[...], 1, 0)
            if step < NS_STEPS - 1:
                it_ref[part, :] = iterate
            else:
                out_ref[part, :] = iterate.astype(low)
        if step < NS_STEPS - 1:
            for cut in cuts:
                once = contract(mix_ref[cut, :], low_ref[...], 1, 0)
                gram_ref[cut, :] = one * one * gram_ref[cut, :] + 2.0 * one * once
                once_ref[cut, :] = once.astype(low)
            for cut in cuts:
                gram = gram_ref[cut, :] + contract(once_ref[cut, :], mix_ref[...], 1, 0)
                gram_ref[cut, :] = gram
            for cut in cuts:
                low_ref[cut, :] = gram_ref[cut, :].astype(low)


SCHULZ_CUT = 256
SCHULZ_ITS = 192


def schulz(panels, matrix):
    in_vmem = pl.BlockSpec(memory_space=pltpu.VMEM)
    return pl.pallas_call(
        schulz_kernel,
        in_specs=[in_vmem, in_vmem],
        out_specs=in_vmem,
        out_shape=jax.ShapeDtypeStruct(matrix.shape, low),
        scratch_shapes=[
            pltpu.VMEM((D, D), full),
            pltpu.VMEM((D, D), low),
            pltpu.VMEM((D, D), low),
            pltpu.VMEM((D, D), low),
            pltpu.VMEM(matrix.shape, full),
        ],
        compiler_params=pltpu.CompilerParams(vmem_limit_bytes=32 * 2**20),
        cost_estimate=pl.CostEstimate(flops=8 * 10**9, bytes_accessed=1000, transcendentals=0),
        name="schulz",
    )(panels, matrix)


def rows_qkv(value):
    kinds, depth, heads, cut = value.shape
    return value.transpose(0, 2, 3, 1).reshape(kinds * heads * cut, depth)


def unrows_qkv(rows, shape):
    kinds, depth, heads, cut = shape
    return rows.reshape(kinds, heads, cut, depth).transpose(0, 3, 1, 2)


def on_device(
    block_in,
    block_cot,
    cluster_perm,
    w_qkv,
    w_out,
    w_up,
    w_down,
    mom_qkv,
    mom_out,
    mom_up,
    mom_down,
    norm_params,
    norm_first,
    norm_second,
):
    ffn_here = lax.axis_index("ffn")
    seqs = lax.axis_size("seq")
    n_bits = len(seq_bits())
    here = block_in.shape[0]
    half = here // 2
    heads = w_out.shape[0]
    cut = w_out.shape[1]
    seq_len = cluster_perm.shape[2]
    clusters = seq_len // CLUSTER

    weights = [rows_qkv(w_qkv), w_out.reshape(heads * cut, D), w_up.T, w_down]
    momenta = [rows_qkv(mom_qkv), mom_out.reshape(heads * cut, D), mom_up.T, mom_down]

    wide_qkv = weights[0].astype(low)
    far_groups = seq_groups()[1:]

    def gather_group(values, bits):
        sent = jnp.concatenate(values, axis=0)
        return [swap(sent, "seq", mask) for mask in masks_of(bits)[1:]]

    def join_group(values, got):
        joined = []
        at = 0
        for value in values:
            joined.append(jnp.concatenate([value] + [other[at : at + value.shape[0]] for other in got], axis=0))
            at += value.shape[0]
        return joined

    got = gather_group([wide_qkv], far_groups[-1])
    tokens = [block_in, swap(block_in, "ffn", 1), swap(block_in, "ffn", 2)]
    tokens.append(swap(tokens[2], "ffn", 1))
    for bits in reversed(far_groups[:-1]):
        (wide_qkv,) = join_group([wide_qkv], got)
        got = gather_group([wide_qkv], bits)
    shards = [weights[2].astype(low), weights[3].astype(low), weights[1].astype(low)]
    shards, got = after((shards, got))
    (wide_qkv,) = join_group([wide_qkv], got)
    last_got = swap(wide_qkv, "seq", 1)
    for turn, bits in enumerate(reversed(far_groups)):
        got = gather_group(shards, bits)
        if turn == 0:
            got, last_got = after((got, last_got))
        shards = join_group(shards, got)
    up_rows, down_rows, out_wide = shards
    wide_qkv = jnp.concatenate([wide_qkv, last_got], axis=0)
    wide_qkv = wide_qkv.reshape(seqs, 3, heads, cut, D).transpose(1, 2, 0, 3, 4).reshape(3, heads, HD, D)
    head_rows = jnp.stack(
        [wide_qkv[0], wide_qkv[2], wide_qkv[1], jnp.zeros_like(wide_qkv[1])], axis=1
    ).reshape(heads * 2 * LANES, D)
    low_rows = down_rows.shape[0]
    shards = (up_rows, jnp.concatenate([down_rows, out_wide], axis=0))
    first_at = (("seq", 1), ("ffn", 2))
    then_at = (("ffn", 2), ("seq", 1))

    def swaps(values, places):
        return tuple(swap(value, *place) for value, place in zip(values, places))

    first_got = swaps(shards, first_at)

    perm = jnp.bitwise_xor(cluster_perm[0], ffn_here * here)
    kept = []
    o_sent = []
    far_got = []
    near_got = []
    for head in range(heads):
        mine = head_rows[head * 2 * LANES : (head + 1) * 2 * LANES]
        order_rows = perm[head : head + 1]
        if head == 1:
            order_rows, first_got, shards = after((order_rows, first_got, shards), kept[0])
            own_got = swaps(shards, then_at)
            up_pieces = [jnp.concatenate([shards[0], first_got[0]], axis=0)]
            up_pieces.append(swap(up_pieces[0], "ffn", 1))
        if head == 2:
            order_rows, own_got, first_got, far_got[0], up_pieces[1] = after(
                (order_rows, own_got, first_got, far_got[0], up_pieces[1]), kept[1]
            )
            other_got = swaps(first_got, then_at)
            near_got.append(send_on(o_sent[0][0], far_got[0][half:]))
            down_pieces = [jnp.concatenate([shards[1][:low_rows], own_got[1][:low_rows]], axis=0)]
            down_pieces.append(swap(down_pieces[0], "ffn", 1))
        own, near, far, qv, key = attend(order_rows, tokens, mine, "attend")
        kept.append((qv, key))
        o_sent.append((near, own))
        far_got.append(swap(far, "ffn", 2))
    other_got, far_got[1], near_got[0], down_pieces[1] = after(
        (other_got, far_got[1], near_got[0], down_pieces[1]), kept[2]
    )
    up_pieces.insert(1, jnp.concatenate([own_got[0], other_got[0]], axis=0))
    down_pieces.insert(1, jnp.concatenate([first_got[1][:low_rows], other_got[1][:low_rows]], axis=0))
    out_wide = jnp.concatenate(
        [value[low_rows:] for value in (shards[1], own_got[1], first_got[1], other_got[1])], axis=0
    )
    out_wide = spread(out_wide, [("ffn", 1)])
    up_pieces.append(swap(up_pieces[1], "ffn", 1))
    down_pieces.append(swap(down_pieces[1], "ffn", 1))
    near_got += [send_on(o_sent[head][0], far_got[head][half:]) for head in (1, 2)]
    o_got = [(sent[1], near, far) for sent, near, far in zip(o_sent, near_got, far_got)]
    up_rows, down_rows = up_pieces, down_pieces

    digits = (2, 2, 2) + (2,) * (n_bits - 1)
    order = (1, 0, 2 + n_bits, 2) + tuple(range(3, 2 + n_bits)) + (3 + n_bits, 4 + n_bits)
    back = tuple(sorted(range(len(order)), key=lambda at: order[at]))
    sizes = digits + (heads, cut, D)
    out_rows = out_wide.reshape(sizes).transpose(order).reshape(4 * heads * HD, D)

    do_blocks, tokenwise, norm_part = layer(
        o_got, block_in, block_cot, out_rows, up_rows, down_rows, norm_params
    )
    block_out, dresidual, gelu_a, gelu_b, dinner_a, dinner_b, dbranch, hidden_low, dattn, o_rows = tokenwise
    do_own, *do_near = do_blocks[:3]
    do_far = [swap(value, "ffn", 2) for value in do_blocks[3:]]

    early_half = (cluster_perm[0] < seq_len // 2).astype(full).reshape(heads, clusters, CLUSTER)
    share = lax.dynamic_update_slice(
        jnp.zeros((4 * heads, clusters), full), jnp.sum(early_half, axis=2) / CLUSTER, (ffn_here * heads, 0)
    ).reshape(1, 4 * heads * clusters)
    small = jnp.concatenate([norm_part, jnp.pad(share, ((0, 0), (0, D - share.shape[1])))])

    down_sent = weight_grad(gelu_b, dbranch)
    dinner_b, do_far[0] = after((dinner_b, do_far[0]), down_sent)
    do_near[0] = send_on(do_near[0], do_far[0][:, 1:], 1)
    up_sent = weight_grad(dinner_b, hidden_low)
    part_out = weight_grad(o_rows, dattn)
    part_out = part_out.reshape(tuple(sizes[at] for at in order)).transpose(back)
    part_out = part_out.reshape(4 * heads * HD, D)
    out_kept, out_sent = cut_outer(part_out)
    down_got, up_got, out_got = [swap(value, "ffn", 1) for value in (down_sent, up_sent, out_sent)]
    down_got, do_far[1] = after((down_got, do_far[1]), part_out)
    do_near[1] = send_on(do_near[1], do_far[1][:, 1:], 1)
    small = small + swap(after(small, down_got), "ffn", 1)
    down_sum = weight_grad(gelu_a, dbranch, down_got)
    up_got, do_near[0], out_got = after((up_got, do_near[0], out_got), down_sum)
    up_sum = weight_grad(dinner_a, hidden_low, up_got)
    out_sum = add_low(out_kept, out_got)

    def quarters(value):
        rows = value.shape[0] // 4
        return [value[part * rows : (part + 1) * rows] for part in range(4)]

    low_sums = [jnp.concatenate(pair, axis=0) for pair in zip(quarters(down_sum), quarters(out_sum))]
    up_sums = [quarters(up_sum)[part] for part in (0, 2, 1, 3)]
    sums = list(zip(up_sums, low_sums))
    places = (("ffn", 2), ("seq", 1))
    then_places = (("seq", 1), ("ffn", 2))

    def send_groups(values, bits):
        masks = masks_of(bits)
        cuts = [cut_many(value, len(masks)) for value in values]
        sent = [jnp.concatenate([parts[turn] for parts in cuts], axis=0) for turn in range(1, len(masks))]
        got = [swap(value, "seq", mask) for value, mask in zip(sent, masks[1:])]
        return [parts[0] for parts in cuts], got

    def add_groups(own, got):
        values = []
        at = 0
        for part in own:
            values.append(add_many(part, [other[at : at + part.shape[0]] for other in got]).astype(low))
            at += part.shape[0]
        return values

    def small_step(bit):
        return small + swap(small, "seq", bit)

    do_near[0] = after(do_near[0], sums)
    part_heads = []
    dboth = []
    for head in range(heads):
        if head == 0:
            first_got = swaps(sums[3], places)
            small_got = swap(small, "ffn", 2)
        if head == 1:
            do_near[0], first_got, small_got = after((do_near[0], first_got, small_got), part_heads[0])
            then_sent = [add_low(value, other) for value, other in zip(sums[2], first_got)]
            second_got = swaps(sums[1], places)
            then_got = swaps(then_sent, then_places)
            small = small + small_got
            small_got = swap(small, "seq", 1)
        if head == 2:
            do_near[1], second_got, then_got, small_got = after(
                (do_near[1], second_got, then_got, small_got), part_heads[1]
            )
            up_sum, low_sum = [
                (value.astype(full) + second.astype(full) + then.astype(full)).astype(low)
                for value, second, then in zip(sums[0], second_got, then_got)
            ]
            small = small + small_got
            rest = [up_sum, low_sum[:low_rows], low_sum[low_rows:]]
            own, rest_got = send_groups(rest, far_groups[0])
            small_got = swap(small, "seq", 2)
        do = (do_own, do_near[head // (heads - 1)], do_far[head // (heads - 1)])
        gw, both = attend_back(perm[head : head + 1], head, kept[head], do, tokens)
        part_heads.append(gw)
        dboth.append(both)
    small_got, dboth = after((small_got, dboth), part_heads[2])
    small = small + small_got
    part_qkv = jnp.stack(part_heads).reshape(heads, 4, HD, D)
    part_qkv = jnp.stack([part_qkv[:, 0], part_qkv[:, 2], part_qkv[:, 1]])
    part_qkv = part_qkv.reshape(3, heads, seqs, cut, D).transpose(2, 0, 1, 3, 4)
    qkv_kept, qkv_sent = cut_outer(part_qkv.reshape(seqs * 3 * heads * cut, D))
    qkv_got = swap(qkv_sent, "seq", 1)
    gx_kept, gx_sent = token_grad(dboth, head_rows, here)
    qkv_got, gx_kept, gx_sent, rest_got = after((qkv_got, gx_kept, gx_sent, rest_got))
    qkv_sum = add_low(qkv_kept, qkv_got)
    rest = add_groups(own, rest_got)
    gx_got = swap(gx_sent, "ffn", 1)
    for turn, bits in enumerate(far_groups):
        if turn > 0:
            rest = add_groups(*send_groups(rest, bits))
        qkv_own, qkv_got = send_groups([qkv_sum], bits)
        if turn == 0:
            qkv_got, gx_got = after((qkv_got, gx_got))
            gx_kept, gx_sent = cut_outer(add_low(gx_kept, gx_got))
        (qkv_sum,) = add_groups(qkv_own, qkv_got)
    up_sum, down_sum, out_sum = rest
    grad_qkv, grad_out, grad_up, grad_down = [
        value.astype(full) for value in (qkv_sum, out_sum, up_sum, down_sum)
    ]
    grads = [grad_qkv, grad_out, grad_up, grad_down]
    moments = [0.5 * mom + grad for mom, grad in zip(momenta, grads)]
    most = max(moment.shape[0] for moment in moments)
    stack = jnp.stack(
        [jnp.pad(moment.astype(low), ((0, most - moment.shape[0]), (0, 0))) for moment in moments]
    )

    def pick(turn):
        return lax.dynamic_index_in_dim(stack, jnp.bitwise_xor(ffn_here, turn), keepdims=False)

    picked = [swap(pick(turn), "ffn", turn) for turn in (1, 2, 3)]
    picked, gx_sent = after((picked, gx_sent))
    matrix = jnp.concatenate([pick(0)] + picked, axis=0)
    *middle_bits, last_bit = [bit for bits in far_groups for bit in bits][1:]
    for bit in middle_bits:
        small = small_step(bit)
    ends = (0, here * 7 // 16, here * 49 // 64, here)
    gx_got = [swap(gx_sent[at:to], "ffn", 2) for at, to in zip(ends, ends[1:])]
    panels = sum_parts(packed_gram(matrix).astype(low))
    panels, gx_got[0] = after((panels, gx_got[0]))
    panels, gx_got[1], (gx_got[2], small_got) = spread_parts(
        panels, gx_got[1], (gx_got[2], swap(small, "seq", last_bit))
    )
    small = small + small_got
    gx_other = jnp.concatenate(gx_got, axis=0)
    steps = schulz(panels, matrix).reshape(4, most, D)
    input_grad = dresidual + (gx_kept.astype(full) + gx_other.astype(full))
    home = jnp.stack([steps[0]] + [swap(steps[turn], "ffn", turn) for turn in (1, 2, 3)])
    step_rates = (
        0.5 * math.sqrt(3.0),
        0.5 * math.sqrt(CLUSTER / 3.0),
        0.5 * math.sqrt(FF / D),
        0.5,
    )
    masters = []
    for member in range(4):
        own = lax.dynamic_index_in_dim(home, jnp.bitwise_xor(ffn_here, member), keepdims=False)
        own = own[: moments[member].shape[0]].astype(full)
        masters.append(weights[member] - step_rates[member] * own)

    grad_norm = small[:4]
    occupancy = small[4, : 4 * heads * clusters].reshape(4 * heads, clusters)
    first_fix = 1.0 - 0.9**ADAM_STEP
    second_fix = 1.0 - 0.999**ADAM_STEP
    first_new = 0.9 * norm_first + 0.1 * grad_norm
    second_new = 0.999 * norm_second + 0.001 * grad_norm * grad_norm
    first_hat = first_new / first_fix
    second_hat = second_new / second_fix
    norm_new = norm_params - 0.5 * (first_hat / (jnp.sqrt(second_hat) + 1e-08) + 0.01 * norm_params)

    def shaped(four):
        return (unrows_qkv(four[0], w_qkv.shape), four[1].reshape(w_out.shape), four[2].T, four[3])

    return (
        (block_out, input_grad)
        + shaped(grads)
        + (grad_norm,)
        + shaped(moments)
        + shaped(masters)
        + (first_new, second_new, norm_new, occupancy)
    )


def solution(mesh):
    rows = P(("seq", "ffn"), None)
    placed = (
        rows,
        rows,
        P("seq", "ffn", None),
        P(None, None, "ffn", "seq"),
        P("ffn", "seq", None),
        P(None, ("seq", "ffn")),
        rows,
        P(None, None, "ffn", "seq"),
        P("ffn", "seq", None),
        P(None, ("seq", "ffn")),
        rows,
        P(),
        P(),
        P(),
    )
    four = placed[3:7]
    return jax.shard_map(
        on_device,
        mesh=mesh,
        in_specs=placed,
        out_specs=(rows, rows) + four + (P(),) + four + four + (P(), P(), P(), P()),
        check_vma=False,
    )
```

```python
import math

import jax
import jax.numpy as jnp
from jax import lax
from jax.experimental import pallas as pl
from jax.experimental.pallas import tpu as pltpu
from jax.sharding import PartitionSpec as P

D = 768
HD = 64
FF = 3072
CLUSTER = 128
NS_STEPS = 3
ADAM_STEP = 10

schulz_coeffs = (3.4445, -4.775, 2.0315)
norm_epsilon = 1e-05
low = jnp.bfloat16
full = jnp.float32
LANES = 128
GROUP = 4
score_scale = 1.0 / math.sqrt(HD)


def contract(left, right, left_axis, right_axis):
    return lax.dot_general(
        left, right, (((left_axis,), (right_axis,)), ((), ())), preferred_element_type=full
    )


def swap(value, axis, bit):
    size = lax.axis_size(axis)
    return lax.ppermute(value, axis, [(place, place ^ bit) for place in range(size)])


def seq_bits():
    bits = []
    bit = lax.axis_size("seq") // 2
    while bit >= 1:
        bits.append(bit)
        bit //= 2
    return bits


def seq_stages():
    return [("seq", bit) for bit in seq_bits()]


def far_stages():
    return [("seq", bit) for bit in seq_bits() if bit > 1]


def spread(shard, stages):
    for axis, bit in stages:
        shard = jnp.concatenate([shard, swap(shard, axis, bit)], axis=0)
    return shard


def fold(partial, stages):
    for axis, bit in reversed(stages):
        half = partial.shape[0] // 2
        kept = partial[:half]
        other = swap(partial[half:].astype(low), axis, bit)
        partial = kept.astype(full) + other.astype(full)
    return partial


def after(values, *tokens):
    return lax.optimization_barrier((values, tokens))[0]


def join_inner(near, other):
    rows = near.shape[0] // 2
    return jnp.concatenate([near[:rows], other[:rows], near[rows:], other[rows:]], axis=0)


def cut_outer(value):
    half = value.shape[0] // 2
    return value[:half], value[half:]


def cut_inner(value):
    rows = value.shape[0] // 4
    quarters = [value[part * rows : (part + 1) * rows] for part in range(4)]
    return tuple(jnp.concatenate(quarters[side::2], axis=0) for side in range(2))


def add_low(kept, other):
    return (kept.astype(full) + other.astype(full)).astype(low)


def fold_step(value, cut, axis, bit):
    kept, sent = cut(value)
    return add_low(kept, swap(sent, axis, bit))


def send_on(near, far_got, axis=0):
    return swap(jnp.concatenate([near, far_got], axis=axis), "ffn", 1)


def add_many(first, others):
    value = first.astype(full)
    for other in others:
        value = value + other.astype(full)
    return value


def seq_groups():
    bits = sorted(seq_bits())
    return [tuple(bits[:1])] + [tuple(bits[at : at + 2]) for at in range(1, len(bits), 2)]


def masks_of(bits):
    masks = [0]
    for bit in bits:
        masks = [mask | more for mask in masks for more in (0, bit)]
    return masks


def cut_many(value, count):
    rows = value.shape[0] // count
    return [value[part * rows : (part + 1) * rows] for part in range(count)]


def place_in(bits):
    me = lax.axis_index("seq")
    place = 0
    for bit in bits:
        place = 2 * place + ((me & bit) != 0).astype(jnp.int32)
    return place


def sum_parts(value):
    for bits in seq_groups():
        masks = masks_of(bits)
        place = place_in(bits)
        parts = value.reshape((len(masks), value.shape[0] // len(masks)) + value.shape[1:])

        def part(turn):
            return lax.dynamic_index_in_dim(parts, jnp.bitwise_xor(place, turn), keepdims=False)

        got = [swap(part(turn), "seq", masks[turn]) for turn in range(1, len(masks))]
        value = add_many(part(0), got).astype(low)
    return value


def spread_parts(value, beside, later):
    for turn, bits in enumerate(reversed(seq_groups())):
        masks = masks_of(bits)
        got = [value] + [swap(value, "seq", mask) for mask in masks[1:]]
        if turn == 0:
            got, beside = after((got, beside))
        if turn == len(seq_groups()) - 1:
            got, later = after((got, later))
        me = lax.axis_index("seq")
        for at, bit in enumerate(bits):
            flip = 2 ** (len(bits) - 1 - at)
            side = (me & bit) != 0
            got = [jnp.where(side, got[turn ^ flip], got[turn]) for turn in range(len(masks))]
        value = jnp.concatenate(got, axis=0)
    return value, beside, later


def in_turns(perm_ref, seq_len, fetch, work, place):
    count = GROUP * CLUSTER
    groups = seq_len // count

    def rows_of(turn):
        return pl.multiple_of(jnp.clip(turn, 0, groups - 1) * count, count)

    def fetch_some(side, turn, rows):
        base = rows_of(turn)
        for row in rows:
            fetch(side, perm_ref[0, base + row], row)

    def place_some(side, turn, rows):
        base = rows_of(turn)
        for row in rows:
            place(side, perm_ref[0, base + row], row)

    def step(pair, carry):
        for side in range(2):
            turn = 2 * pair + side
            done = 0
            for at in work(side, rows_of(turn)):
                rows = range(done, min(count, int(at * count)))
                fetch_some(1 - side, turn + 1, rows)
                place_some(1 - side, turn - 1, rows)
                done = max(done, rows.stop)
            fetch_some(1 - side, turn + 1, range(done, count))
            place_some(1 - side, turn - 1, range(done, count))
        return carry

    fetch_some(0, 0, range(count))
    lax.fori_loop(0, groups // 2, step, 0)
    place_some(1, groups - 1, range(count))


def softmax_rows(scores):
    peak = jnp.max(scores, axis=1, keepdims=True)
    powers = jnp.exp((scores - peak) * score_scale)
    return powers * (1.0 / jnp.sum(powers, axis=1, keepdims=True))


def left_half(rows):
    return lax.broadcasted_iota(jnp.int32, (rows, LANES), 1) < HD


def attend_kernel(
    perm_ref, x0, x1, x2, x3, w_ref, own_ref, near_ref, far_ref, qv_ref, key_ref, qv_rows, key_rows, o_rows, *got
):
    qv_got, key_got, o_got = got[0:2], got[2:4], got[4:6]
    here = x0.shape[0]
    seq_len = 4 * here
    half = here // 2
    for block, x_ref in enumerate((x0, x1, x2, x3)):
        for cut in range(2):
            both = contract(x_ref[pl.ds(cut * half, half), :], w_ref[...], 1, 1)
            rows = pl.ds(block * here + cut * half, half)
            qv_rows[rows, :] = both[:, :LANES]
            key_rows[rows, :] = both[:, LANES:]
    spans = [slice(part * CLUSTER, (part + 1) * CLUSTER) for part in range(GROUP)]

    def fetch(side, index, row):
        qv_got[side][pl.ds(row, 1), :] = qv_rows[pl.ds(index, 1), :]
        key_got[side][pl.ds(row, 1), :] = key_rows[pl.ds(index, 1), :]

    def work(side, base):
        qvs = [qv_got[side][span].astype(low) for span in spans]
        keys = [key_got[side][span].astype(low) for span in spans]
        for part in range(GROUP):
            rows = pl.ds(base + part * CLUSTER, CLUSTER)
            qv_ref[rows, :] = qvs[part]
            key_ref[rows, :] = keys[part]
        scores = [contract(qv, key, 1, 1) for qv, key in zip(qvs, keys)]
        yield 0.3
        probs = []
        for part in range(GROUP):
            probs.append(softmax_rows(scores[part]).astype(low))
            yield 0.3 + 0.6 * (part + 1) / GROUP
        for part in range(GROUP):
            o_got[side][spans[part]] = contract(probs[part], qvs[part], 1, 0)

    def place(side, index, row):
        o_rows[pl.ds(index, 1), :] = o_got[side][pl.ds(row, 1), :]

    in_turns(perm_ref, seq_len, fetch, work, place)
    outs = (own_ref, near_ref, far_ref.at[pl.ds(0, half), :], far_ref.at[pl.ds(half, half), :])
    for block, out_ref in enumerate(outs):
        top = pltpu.roll(o_rows[pl.ds(block * here, half), :], HD, 1)
        bottom = o_rows[pl.ds(block * here + half, half), :]
        out_ref[...] = jnp.where(left_half(half), top, bottom).astype(low)


def vmem(*shape):
    return pl.BlockSpec(shape, memory_space=pltpu.VMEM)


def attend(perm, tokens, weights, name):
    seq_len = perm.shape[1]
    here = tokens[0].shape[0]
    rows_got = pltpu.VMEM((GROUP * CLUSTER, LANES), full)
    rows_all = pltpu.VMEM((seq_len, LANES), full)
    in_vmem = pl.BlockSpec(memory_space=pltpu.VMEM)
    return pl.pallas_call(
        attend_kernel,
        in_specs=[pl.BlockSpec(memory_space=pltpu.SMEM)] + [in_vmem] * 5,
        out_specs=[in_vmem] * 5,
        out_shape=[
            jax.ShapeDtypeStruct((here // 2, LANES), low),
            jax.ShapeDtypeStruct((here // 2, LANES), low),
            jax.ShapeDtypeStruct((here, LANES), low),
            jax.ShapeDtypeStruct((seq_len, LANES), low),
            jax.ShapeDtypeStruct((seq_len, LANES), low),
        ],
        scratch_shapes=[rows_all] * 3 + [rows_got] * 6,
        compiler_params=pltpu.CompilerParams(vmem_limit_bytes=40 * 2**20),
        cost_estimate=pl.CostEstimate(flops=18 * 10**9, bytes_accessed=1000, transcendentals=0),
        name=name,
    )(perm, *tokens, weights)


def attend_back_kernel(
    perm_ref, qv_ref, key_ref, do0, do1, do2, do3, x0, x1, x2, x3, gw_ref, dboth_ref, d_rows, dqv_rows, dkey_rows, *got
):
    d_got, dqv_got, dkey_got = got[0:2], got[2:4], got[4:6]
    here = x0.shape[0]
    seq_len = 4 * here
    half = here // 2
    for block, do_ref in enumerate((do0, do1, do2, do3)):
        rows = do_ref[...].astype(full)
        top = pltpu.roll(rows, HD, 1)
        d_rows[pl.ds(block * here, half), :] = jnp.where(left_half(half), 0.0, top)
        d_rows[pl.ds(block * here + half, half), :] = jnp.where(left_half(half), 0.0, rows)
    spans = [slice(part * CLUSTER, (part + 1) * CLUSTER) for part in range(GROUP)]

    def fetch(side, index, row):
        d_got[side][pl.ds(row, 1), :] = d_rows[pl.ds(index, 1), :]

    def work(side, base):
        rows = [pl.ds(base + part * CLUSTER, CLUSTER) for part in range(GROUP)]
        qvs = [qv_ref[span, :] for span in rows]
        keys = [key_ref[span, :] for span in rows]
        dos = [d_got[side][span].astype(low) for span in spans]
        scores = [contract(qv, key, 1, 1) for qv, key in zip(qvs, keys)]
        dprobs = [contract(do, qv, 1, 1) for do, qv in zip(dos, qvs)]
        yield 0.2
        probs = []
        for part in range(GROUP):
            probs.append(softmax_rows(scores[part]))
            yield 0.2 + 0.3 * (part + 1) / GROUP
        probs_low = [prob.astype(low) for prob in probs]
        dscores = []
        for prob, dprob in zip(probs, dprobs):
            dscores.append((prob * (dprob - jnp.sum(prob * dprob, axis=1, keepdims=True))).astype(low))
            yield 0.5 + 0.3 * len(dscores) / GROUP
        for part in range(GROUP):
            dqv_got[side][spans[part]] = score_scale * contract(dscores[part], keys[part], 1, 0) + contract(
                probs_low[part], dos[part], 0, 0
            )
            dkey_got[side][spans[part]] = score_scale * contract(dscores[part], qvs[part], 0, 0)

    def place(side, index, row):
        dqv_rows[pl.ds(index, 1), :] = dqv_got[side][pl.ds(row, 1), :]
        dkey_rows[pl.ds(index, 1), :] = dkey_got[side][pl.ds(row, 1), :]

    in_turns(perm_ref, seq_len, fetch, work, place)
    gw = jnp.zeros((2 * LANES, D), full)
    for block, x_ref in enumerate((x0, x1, x2, x3)):
        rows = pl.ds(block * here, here)
        dboth_ref[rows, :LANES] = dqv_rows[rows, :].astype(low)
        dboth_ref[rows, LANES:] = dkey_rows[rows, :].astype(low)
        gw = gw + contract(dboth_ref[rows, :], x_ref[...], 0, 0)
    gw_ref[...] = gw.astype(low)


def attend_back(perm, head, kept, do, tokens):
    seq_len = perm.shape[1]
    here = tokens[0].shape[0]
    half = here // 2
    rows_got = pltpu.VMEM((GROUP * CLUSTER, LANES), full)
    rows_all = pltpu.VMEM((seq_len, LANES), full)
    in_vmem = pl.BlockSpec(memory_space=pltpu.VMEM)
    own, near, far = do

    at = head if near.shape[0] > 1 else 0

    def part(at, turn):
        return pl.BlockSpec((None, None, half, LANES), lambda step: (at, turn, 0, 0))


    return pl.pallas_call(
        attend_back_kernel,
        grid=(1,),
        in_specs=[pl.BlockSpec(memory_space=pltpu.SMEM)]
        + [in_vmem] * 2
        + [part(head, 0), part(at, 0), part(at, 0), part(at, 1)]
        + [in_vmem] * 4,
        out_specs=[in_vmem] * 2,
        out_shape=[
            jax.ShapeDtypeStruct((2 * LANES, D), low),
            jax.ShapeDtypeStruct((seq_len, 2 * LANES), low),
        ],
        scratch_shapes=[rows_all] * 3 + [rows_got] * 6,
        compiler_params=pltpu.CompilerParams(vmem_limit_bytes=40 * 2**20),
        cost_estimate=pl.CostEstimate(flops=22 * 10**9, bytes_accessed=1000, transcendentals=0),
        name="attend_back",
    )(perm, *kept, own, near, far, near, *tokens)


def token_grad_kernel(d0, d1, d2, w_ref, kept_ref, sent_ref):
    sums = None
    for head, d_ref in enumerate((d0, d1, d2)):
        piece = contract(d_ref[...], w_ref[pl.ds(head * 2 * LANES, 2 * LANES), :], 1, 0)
        sums = piece if sums is None else sums + piece

    @pl.when(pl.program_id(0) < 2)
    def _():
        sent_ref[...] = sums.astype(low)

    @pl.when(pl.program_id(0) >= 2)
    def _():
        kept_ref[...] = sums.astype(low)


def token_grad(dboth, weights, here):
    split = 2
    rows = here // split

    def from_block(slot, part):
        return ((2 * (slot % 2) + 1 - slot // 2) * split + part, 0)

    def to_sent(slot, part):
        return (jnp.minimum(slot * split + part, 2 * split - 1), 0)

    def to_kept(slot, part):
        return (jnp.maximum(slot * split + part - 2 * split, 0), 0)

    return pl.pallas_call(
        token_grad_kernel,
        grid=(4, split),
        in_specs=[pl.BlockSpec((rows, 2 * LANES), from_block)] * 3
        + [pl.BlockSpec((6 * LANES, D), lambda slot, part: (0, 0))],
        out_specs=[pl.BlockSpec((rows, D), to_kept), pl.BlockSpec((rows, D), to_sent)],
        out_shape=[jax.ShapeDtypeStruct((2 * here, D), low)] * 2,
        compiler_params=pltpu.CompilerParams(vmem_limit_bytes=32 * 2**20),
        cost_estimate=pl.CostEstimate(flops=8 * 10**9, bytes_accessed=1000, transcendentals=0),
        name="token_grad",
    )(*dboth, weights)


def row_mean(value):
    return jnp.mean(value, axis=-1, keepdims=True)


def norm_forward(inputs, gains, biases):
    center = inputs - row_mean(inputs)
    inv_std = lax.rsqrt(row_mean(center * center) + norm_epsilon)
    normed = center * inv_std
    return (normed * gains + biases, normed, inv_std)


def norm_backward(upstream, normed, inv_std, gains):
    scaled = upstream * gains
    inside = scaled - row_mean(scaled) - normed * row_mean(scaled * normed)
    sums = [jnp.sum(upstream * normed, axis=0, keepdims=True), jnp.sum(upstream, axis=0, keepdims=True)]
    return (inside * inv_std, sums)


def layer_kernel(heads, *refs):
    o_refs = refs[: 4 * heads]
    (x_ref, cot_ref, wo_ref, norm_ref) = refs[4 * heads : 4 * heads + 4]
    up_refs = refs[4 * heads + 4 : 4 * heads + 8]
    down_refs = refs[4 * heads + 8 : 4 * heads + 12]
    outs = refs[4 * heads + 12 :]
    do_own, near_first, near_last, far_first, far_last, block_ref, da_ref = outs[:7]
    g_refs = outs[7:9]
    du_refs = outs[9:11]
    (df_ref, hb_ref, dattn_ref, o_ref, sums_ref, slope_ref) = outs[11:]

    def store_do(head, turn, value):
        near, far, at = (near_first, far_first, head) if head < heads - 1 else (near_last, far_last, 0)
        if turn == 0:
            do_own[head, 0] = value
        elif turn == 1:
            near[at, 0] = value
        else:
            far[at, turn - 2] = value
    part = x_ref.shape[1]
    rows = 2 * part
    left = left_half(part)

    def load(ref):
        return jnp.concatenate([ref[0], ref[1]], axis=0)

    def store(ref, value):
        ref[0] = value[:part]
        ref[1] = value[part:]

    packed = []
    for turn in range(4):
        for head in range(heads):
            packed.append(o_refs[4 * head + turn][...].astype(full))
    for pair in range(len(packed) // 2):
        first, second = packed[2 * pair], packed[2 * pair + 1]
        lanes = slice(pair * LANES, (pair + 1) * LANES)
        o_ref[0, :, lanes] = jnp.where(left, first, pltpu.roll(second, HD, 1)).astype(low)
        o_ref[1, :, lanes] = jnp.where(left, pltpu.roll(first, HD, 1), second).astype(low)

    gain_a, bias_a = norm_ref[0:1, :], norm_ref[1:2, :]
    gain_b, bias_b = norm_ref[2:3, :], norm_ref[3:4, :]
    residual = load(x_ref).astype(full) + contract(load(o_ref), wo_ref[...], 1, 0)
    hidden, normed_a, inv_a = norm_forward(residual, gain_a, bias_a)
    hidden_low = hidden.astype(low)
    store(hb_ref, hidden_low)
    branch = jnp.zeros((rows, D), full)
    quarter = FF // 4
    cuts = [slice(at, at + quarter) for at in range(0, FF, quarter)]
    for turn, cut in enumerate(cuts):
        side = turn // 2
        columns = slice(turn % 2 * quarter, (turn % 2 + 1) * quarter)
        preact = contract(hidden_low, up_refs[turn][...], 1, 1)
        cumulative = 0.5 * (1.0 + lax.erf(preact * 0.7071067811865476))
        gelu_low = (preact * cumulative).astype(low)
        slope_ref[:, cut] = cumulative + preact * (jnp.exp(-0.5 * preact * preact) * 0.3989422804014327)
        g_refs[side][0, :, columns] = gelu_low[:part]
        g_refs[side][1, :, columns] = gelu_low[part:]
        branch = branch + contract(gelu_low, down_refs[turn][...], 1, 0)
    outputs, normed_b, inv_b = norm_forward(hidden + branch, gain_b, bias_b)
    store(block_ref, outputs.astype(low))
    dsum, sums_b = norm_backward(load(cot_ref).astype(full), normed_b, inv_b, gain_b)
    dsum_low = dsum.astype(low)
    store(df_ref, dsum_low)
    dhidden = dsum
    for turn, cut in enumerate(cuts):
        side = turn // 2
        columns = slice(turn % 2 * quarter, (turn % 2 + 1) * quarter)
        dinner = (contract(dsum_low, down_refs[turn][...], 1, 1) * slope_ref[:, cut]).astype(low)
        du_refs[side][0, :, columns] = dinner[:part]
        du_refs[side][1, :, columns] = dinner[part:]
        dhidden = dhidden + contract(dinner, up_refs[turn][...], 1, 0)
    dresidual, sums_a = norm_backward(dhidden, normed_a, inv_a, gain_a)
    store(da_ref, dresidual)
    dattn = dresidual.astype(low)
    store(dattn_ref, dattn)
    dheads = contract(dattn, wo_ref[...], 1, 1)
    for pair in range(len(packed) // 2):
        lanes = slice(pair * LANES, (pair + 1) * LANES)
        top, bottom = dheads[:part, lanes], dheads[part:, lanes]
        both = (
            jnp.where(left, top, pltpu.roll(bottom, HD, 1)).astype(low),
            jnp.where(left, pltpu.roll(top, HD, 1), bottom).astype(low),
        )
        for side in range(2):
            turn, head = divmod(2 * pair + side, heads)
            store_do(head, turn, both[side])
    sums = jnp.concatenate(sums_a + sums_b, axis=0)

    @pl.when(pl.program_id(0) == 0)
    def _():
        sums_ref[...] = sums

    @pl.when(pl.program_id(0) > 0)
    def _():
        sums_ref[...] += sums


LAYER_STEPS = 4


def layer(o_got, block_in, block_cot, out_rows, up_rows, down_rows, norm_params):
    heads = len(o_got)
    here = block_in.shape[0]
    half = here // 2
    part = half // LAYER_STEPS
    once = pl.Buffered(1)

    def lead(count, width):
        return pl.BlockSpec((count, part, width), lambda step: (0, step, 0))

    do_sizes = ((heads, 1), (heads - 1, 1), (1, 1), (heads - 1, 2), (1, 2))

    def do_part(count, turns):
        return pl.BlockSpec((count, turns, part, LANES), lambda step: (0, 0, step, 0))

    def still(rows):
        return pl.BlockSpec((rows, D), lambda step: (0, 0), pipeline_mode=once)

    def pairs(width, kind):
        return jax.ShapeDtypeStruct((2, half, width), kind)

    o_args = [piece for own, near, far in o_got for piece in (own, near, far, near)]
    later = pl.BlockSpec((part, LANES), lambda step: (step + LAYER_STEPS, 0))
    lanes = pl.BlockSpec((part, LANES), lambda step: (step, 0))
    two = lead(2, D)
    wide = lead(2, FF // 2)
    flat = pl.pallas_call(
        lambda *refs: layer_kernel(heads, *refs),
        grid=(LAYER_STEPS,),
        in_specs=[lanes, lanes, lanes, later] * heads
        + [two, two, still(D), still(4)]
        + [still(FF // 4)] * 8,
        out_specs=[do_part(*sizes) for sizes in do_sizes] + [two, two] + [wide] * 4 + [two] * 4
        + [pl.BlockSpec((4, D), lambda step: (0, 0))],
        out_shape=[jax.ShapeDtypeStruct((count, turns, half, LANES), low) for count, turns in do_sizes]
        + [
            pairs(D, low),
            pairs(D, full),
            pairs(FF // 2, low),
            pairs(FF // 2, low),
            pairs(FF // 2, low),
            pairs(FF // 2, low),
            pairs(D, low),
            pairs(D, low),
            pairs(D, low),
            pairs(D, low),
            jax.ShapeDtypeStruct((4, D), full),
        ],
        scratch_shapes=[pltpu.VMEM((2 * part, FF), full)],
        compiler_params=pltpu.CompilerParams(vmem_limit_bytes=60 * 2**20),
        cost_estimate=pl.CostEstimate(flops=40 * 10**9, bytes_accessed=1000, transcendentals=0),
        name="layer",
    )(
        *o_args,
        block_in.reshape(2, half, D),
        block_cot.reshape(2, half, D),
        out_rows,
        norm_params,
        *up_rows,
        *down_rows,
    )
    tokenwise = [value.reshape(here, value.shape[2]) for value in flat[5:-1]]
    return flat[:5], tokenwise, flat[-1]


def weight_grad_kernel(left_ref, right_ref, *refs):
    value = contract(left_ref[...], right_ref[...], 0, 0)
    if len(refs) > 1:
        value = value + refs[0][...].astype(full)
    refs[-1][...] = value.astype(low)


def weight_grad(left, right, other=None):
    rows, width = left.shape
    part = 512 if width % 512 == 0 else 384
    args = [left, right]
    in_specs = [
        pl.BlockSpec((rows, part), lambda step: (0, step)),
        pl.BlockSpec((rows, D), lambda step: (0, 0)),
    ]
    block = pl.BlockSpec((part, D), lambda step: (step, 0))
    if other is not None:
        args.append(other)
        in_specs.append(block)
    return pl.pallas_call(
        weight_grad_kernel,
        grid=(width // part,),
        in_specs=in_specs,
        out_specs=block,
        out_shape=jax.ShapeDtypeStruct((width, D), low),
        compiler_params=pltpu.CompilerParams(vmem_limit_bytes=32 * 2**20),
        cost_estimate=pl.CostEstimate(flops=4 * 10**9, bytes_accessed=1000, transcendentals=0),
        name="weight_grad",
    )(*args)


def packed_gram(matrix):
    gram = contract(matrix, matrix, 0, 0)
    panels = [gram[: at + LANES, at : at + LANES] for at in range(0, D, LANES)]
    return jnp.concatenate(panels, axis=0)


def schulz_kernel(panels_ref, matrix_ref, out_ref, gram_ref, low_ref, mix_ref, once_ref, it_ref):
    one, two, three = schulz_coeffs
    blocks = D // LANES
    diagonal = lax.broadcasted_iota(jnp.int32, (LANES, LANES), 0) == lax.broadcasted_iota(
        jnp.int32, (LANES, LANES), 1
    )
    trace = jnp.zeros((1, 1), full)
    first = 0
    for col in range(blocks):
        for row in range(col + 1):
            block = panels_ref[first : first + LANES, :].astype(full)
            first += LANES
            rows = slice(row * LANES, (row + 1) * LANES)
            cols = slice(col * LANES, (col + 1) * LANES)
            gram_ref[rows, cols] = block
            if row < col:
                gram_ref[cols, rows] = block.T
            else:
                mine = jnp.where(diagonal, block, 0.0)
                trace = trace + jnp.sum(jnp.sum(mine, axis=1, keepdims=True), axis=0, keepdims=True)
    shrink = 1.0 / (jnp.sqrt(trace) + 1e-07)
    cuts = [slice(at, at + SCHULZ_CUT) for at in range(0, D, SCHULZ_CUT)]
    its = [slice(at, at + SCHULZ_ITS) for at in range(0, matrix_ref.shape[0], SCHULZ_ITS)]
    for cut in cuts:
        gram = gram_ref[cut, :] * (shrink * shrink)
        gram_ref[cut, :] = gram
        low_ref[cut, :] = gram.astype(low)
    for part in its:
        it_ref[part, :] = matrix_ref[part, :].astype(full) * shrink
    for step in range(NS_STEPS):
        for cut in cuts:
            square = contract(low_ref[cut, :], low_ref[...], 1, 0)
            mix_ref[cut, :] = (two * gram_ref[cut, :] + three * square).astype(low)
        for part in its:
            iterate = it_ref[part, :]
            iterate = one * iterate + contract(iterate.astype(low), mix_ref[...], 1, 0)
            if step < NS_STEPS - 1:
                it_ref[part, :] = iterate
            else:
                out_ref[part, :] = iterate.astype(low)
        if step < NS_STEPS - 1:
            for cut in cuts:
                once = contract(mix_ref[cut, :], low_ref[...], 1, 0)
                gram_ref[cut, :] = one * one * gram_ref[cut, :] + 2.0 * one * once
                once_ref[cut, :] = once.astype(low)
            for cut in cuts:
                gram = gram_ref[cut, :] + contract(once_ref[cut, :], mix_ref[...], 1, 0)
                gram_ref[cut, :] = gram
            for cut in cuts:
                low_ref[cut, :] = gram_ref[cut, :].astype(low)


SCHULZ_CUT = 256
SCHULZ_ITS = 192


def schulz(panels, matrix):
    in_vmem = pl.BlockSpec(memory_space=pltpu.VMEM)
    return pl.pallas_call(
        schulz_kernel,
        in_specs=[in_vmem, in_vmem],
        out_specs=in_vmem,
        out_shape=jax.ShapeDtypeStruct(matrix.shape, low),
        scratch_shapes=[
            pltpu.VMEM((D, D), full),
            pltpu.VMEM((D, D), low),
            pltpu.VMEM((D, D), low),
            pltpu.VMEM((D, D), low),
            pltpu.VMEM(matrix.shape, full),
        ],
        compiler_params=pltpu.CompilerParams(vmem_limit_bytes=32 * 2**20),
        cost_estimate=pl.CostEstimate(flops=8 * 10**9, bytes_accessed=1000, transcendentals=0),
        name="schulz",
    )(panels, matrix)


def rows_qkv(value):
    kinds, depth, heads, cut = value.shape
    return value.transpose(0, 2, 3, 1).reshape(kinds * heads * cut, depth)


def unrows_qkv(rows, shape):
    kinds, depth, heads, cut = shape
    return rows.reshape(kinds, heads, cut, depth).transpose(0, 3, 1, 2)


def on_device(
    block_in,
    block_cot,
    cluster_perm,
    w_qkv,
    w_out,
    w_up,
    w_down,
    mom_qkv,
    mom_out,
    mom_up,
    mom_down,
    norm_params,
    norm_first,
    norm_second,
):
    ffn_here = lax.axis_index("ffn")
    seqs = lax.axis_size("seq")
    n_bits = len(seq_bits())
    here = block_in.shape[0]
    half = here // 2
    heads = w_out.shape[0]
    cut = w_out.shape[1]
    seq_len = cluster_perm.shape[2]
    clusters = seq_len // CLUSTER

    weights = [rows_qkv(w_qkv), w_out.reshape(heads * cut, D), w_up.T, w_down]
    momenta = [rows_qkv(mom_qkv), mom_out.reshape(heads * cut, D), mom_up.T, mom_down]

    wide_qkv = weights[0].astype(low)
    far_groups = seq_groups()[1:]

    def gather_group(values, bits):
        sent = jnp.concatenate(values, axis=0)
        return [swap(sent, "seq", mask) for mask in masks_of(bits)[1:]]

    def join_group(values, got):
        joined = []
        at = 0
        for value in values:
            joined.append(jnp.concatenate([value] + [other[at : at + value.shape[0]] for other in got], axis=0))
            at += value.shape[0]
        return joined

    got = gather_group([wide_qkv], far_groups[-1])
    tokens = [block_in, swap(block_in, "ffn", 1), swap(block_in, "ffn", 2)]
    tokens.append(swap(tokens[2], "ffn", 1))
    for bits in reversed(far_groups[:-1]):
        (wide_qkv,) = join_group([wide_qkv], got)
        got = gather_group([wide_qkv], bits)
    shards = [weights[2].astype(low), weights[3].astype(low), weights[1].astype(low)]
    shards, got = after((shards, got))
    (wide_qkv,) = join_group([wide_qkv], got)
    last_got = swap(wide_qkv, "seq", 1)
    for turn, bits in enumerate(reversed(far_groups)):
        got = gather_group(shards, bits)
        if turn == 0:
            got, last_got = after((got, last_got))
        shards = join_group(shards, got)
    up_rows, down_rows, out_wide = shards
    wide_qkv = jnp.concatenate([wide_qkv, last_got], axis=0)
    wide_qkv = wide_qkv.reshape(seqs, 3, heads, cut, D).transpose(1, 2, 0, 3, 4).reshape(3, heads, HD, D)
    head_rows = jnp.stack(
        [wide_qkv[0], wide_qkv[2], wide_qkv[1], jnp.zeros_like(wide_qkv[1])], axis=1
    ).reshape(heads * 2 * LANES, D)
    low_rows = down_rows.shape[0]
    shards = (up_rows, jnp.concatenate([down_rows, out_wide], axis=0))
    first_at = (("seq", 1), ("ffn", 2))
    then_at = (("ffn", 2), ("seq", 1))

    def swaps(values, places):
        return tuple(swap(value, *place) for value, place in zip(values, places))

    first_got = swaps(shards, first_at)

    perm = jnp.bitwise_xor(cluster_perm[0], ffn_here * here)
    kept = []
    o_sent = []
    far_got = []
    near_got = []
    for head in range(heads):
        mine = head_rows[head * 2 * LANES : (head + 1) * 2 * LANES]
        order_rows = perm[head : head + 1]
        if head == 1:
            order_rows, first_got, shards = after((order_rows, first_got, shards), kept[0])
            own_got = swaps(shards, then_at)
            up_pieces = [jnp.concatenate([shards[0], first_got[0]], axis=0)]
            up_pieces.append(swap(up_pieces[0], "ffn", 1))
        if head == 2:
            order_rows, own_got, first_got, far_got[0], up_pieces[1] = after(
                (order_rows, own_got, first_got, far_got[0], up_pieces[1]), kept[1]
            )
            other_got = swaps(first_got, then_at)
            near_got.append(send_on(o_sent[0][0], far_got[0][half:]))
            down_pieces = [jnp.concatenate([shards[1][:low_rows], own_got[1][:low_rows]], axis=0)]
            down_pieces.append(swap(down_pieces[0], "ffn", 1))
        own, near, far, qv, key = attend(order_rows, tokens, mine, "attend")
        kept.append((qv, key))
        o_sent.append((near, own))
        far_got.append(swap(far, "ffn", 2))
    other_got, far_got[1], near_got[0], down_pieces[1] = after(
        (other_got, far_got[1], near_got[0], down_pieces[1]), kept[2]
    )
    up_pieces.insert(1, jnp.concatenate([own_got[0], other_got[0]], axis=0))
    down_pieces.insert(1, jnp.concatenate([first_got[1][:low_rows], other_got[1][:low_rows]], axis=0))
    out_wide = jnp.concatenate(
        [value[low_rows:] for value in (shards[1], own_got[1], first_got[1], other_got[1])], axis=0
    )
    out_wide = spread(out_wide, [("ffn", 1)])
    up_pieces.append(swap(up_pieces[1], "ffn", 1))
    down_pieces.append(swap(down_pieces[1], "ffn", 1))
    near_got += [send_on(o_sent[head][0], far_got[head][half:]) for head in (1, 2)]
    o_got = [(sent[1], near, far) for sent, near, far in zip(o_sent, near_got, far_got)]
    up_rows, down_rows = up_pieces, down_pieces

    digits = (2, 2, 2) + (2,) * (n_bits - 1)
    order = (1, 0, 2 + n_bits, 2) + tuple(range(3, 2 + n_bits)) + (3 + n_bits, 4 + n_bits)
    back = tuple(sorted(range(len(order)), key=lambda at: order[at]))
    sizes = digits + (heads, cut, D)
    out_rows = out_wide.reshape(sizes).transpose(order).reshape(4 * heads * HD, D)

    do_blocks, tokenwise, norm_part = layer(
        o_got, block_in, block_cot, out_rows, up_rows, down_rows, norm_params
    )
    block_out, dresidual, gelu_a, gelu_b, dinner_a, dinner_b, dbranch, hidden_low, dattn, o_rows = tokenwise
    do_own, *do_near = do_blocks[:3]
    do_far = [swap(value, "ffn", 2) for value in do_blocks[3:]]

    early_half = (cluster_perm[0] < seq_len // 2).astype(full).reshape(heads, clusters, CLUSTER)
    share = lax.dynamic_update_slice(
        jnp.zeros((4 * heads, clusters), full), jnp.sum(early_half, axis=2) / CLUSTER, (ffn_here * heads, 0)
    ).reshape(1, 4 * heads * clusters)
    small = jnp.concatenate([norm_part, jnp.pad(share, ((0, 0), (0, D - share.shape[1])))])

    down_sent = weight_grad(gelu_b, dbranch)
    dinner_b, do_far[0] = after((dinner_b, do_far[0]), down_sent)
    do_near[0] = send_on(do_near[0], do_far[0][:, 1:], 1)
    up_sent = weight_grad(dinner_b, hidden_low)
    part_out = weight_grad(o_rows, dattn)
    part_out = part_out.reshape(tuple(sizes[at] for at in order)).transpose(back)
    part_out = part_out.reshape(4 * heads * HD, D)
    out_kept, out_sent = cut_outer(part_out)
    down_got, up_got, out_got = [swap(value, "ffn", 1) for value in (down_sent, up_sent, out_sent)]
    down_got, do_far[1] = after((down_got, do_far[1]), part_out)
    do_near[1] = send_on(do_near[1], do_far[1][:, 1:], 1)
    small = small + swap(after(small, down_got), "ffn", 1)
    down_sum = weight_grad(gelu_a, dbranch, down_got)
    up_got, do_near[0], out_got = after((up_got, do_near[0], out_got), down_sum)
    up_sum = weight_grad(dinner_a, hidden_low, up_got)
    out_sum = add_low(out_kept, out_got)

    def quarters(value):
        rows = value.shape[0] // 4
        return [value[part * rows : (part + 1) * rows] for part in range(4)]

    low_sums = [jnp.concatenate(pair, axis=0) for pair in zip(quarters(down_sum), quarters(out_sum))]
    up_sums = [quarters(up_sum)[part] for part in (0, 2, 1, 3)]
    sums = list(zip(up_sums, low_sums))
    places = (("ffn", 2), ("seq", 1))
    then_places = (("seq", 1), ("ffn", 2))

    def send_groups(values, bits):
        masks = masks_of(bits)
        cuts = [cut_many(value, len(masks)) for value in values]
        sent = [jnp.concatenate([parts[turn] for parts in cuts], axis=0) for turn in range(1, len(masks))]
        got = [swap(value, "seq", mask) for value, mask in zip(sent, masks[1:])]
        return [parts[0] for parts in cuts], got

    def add_groups(own, got):
        values = []
        at = 0
        for part in own:
            values.append(add_many(part, [other[at : at + part.shape[0]] for other in got]).astype(low))
            at += part.shape[0]
        return values

    def small_step(bit):
        return small + swap(small, "seq", bit)

    do_near[0] = after(do_near[0], sums)
    part_heads = []
    dboth = []
    for head in range(heads):
        if head == 0:
            first_got = swaps(sums[3], places)
            small_got = swap(small, "ffn", 2)
        if head == 1:
            do_near[0], first_got, small_got = after((do_near[0], first_got, small_got), part_heads[0])
            then_sent = [add_low(value, other) for value, other in zip(sums[2], first_got)]
            second_got = swaps(sums[1], places)
            then_got = swaps(then_sent, then_places)
            small = small + small_got
            small_got = swap(small, "seq", 1)
        if head == 2:
            do_near[1], second_got, then_got, small_got = after(
                (do_near[1], second_got, then_got, small_got), part_heads[1]
            )
            up_sum, low_sum = [
                (value.astype(full) + second.astype(full) + then.astype(full)).astype(low)
                for value, second, then in zip(sums[0], second_got, then_got)
            ]
            small = small + small_got
            rest = [up_sum, low_sum[:low_rows], low_sum[low_rows:]]
            own, rest_got = send_groups(rest, far_groups[0])
            small_got = swap(small, "seq", 2)
        do = (do_own, do_near[head // (heads - 1)], do_far[head // (heads - 1)])
        gw, both = attend_back(perm[head : head + 1], head, kept[head], do, tokens)
        part_heads.append(gw)
        dboth.append(both)
    small_got, dboth = after((small_got, dboth), part_heads[2])
    small = small + small_got
    part_qkv = jnp.stack(part_heads).reshape(heads, 4, HD, D)
    part_qkv = jnp.stack([part_qkv[:, 0], part_qkv[:, 2], part_qkv[:, 1]])
    part_qkv = part_qkv.reshape(3, heads, seqs, cut, D).transpose(2, 0, 1, 3, 4)
    qkv_kept, qkv_sent = cut_outer(part_qkv.reshape(seqs * 3 * heads * cut, D))
    qkv_got = swap(qkv_sent, "seq", 1)
    gx_kept, gx_sent = token_grad(dboth, head_rows, here)
    qkv_got, gx_kept, gx_sent, rest_got = after((qkv_got, gx_kept, gx_sent, rest_got))
    qkv_sum = add_low(qkv_kept, qkv_got)
    rest = add_groups(own, rest_got)
    gx_got = swap(gx_sent, "ffn", 1)
    for turn, bits in enumerate(far_groups):
        if turn > 0:
            rest = add_groups(*send_groups(rest, bits))
        qkv_own, qkv_got = send_groups([qkv_sum], bits)
        if turn == 0:
            qkv_got, gx_got = after((qkv_got, gx_got))
            gx_kept, gx_sent = cut_outer(add_low(gx_kept, gx_got))
        (qkv_sum,) = add_groups(qkv_own, qkv_got)
    up_sum, down_sum, out_sum = rest
    grad_qkv, grad_out, grad_up, grad_down = [
        value.astype(full) for value in (qkv_sum, out_sum, up_sum, down_sum)
    ]
    grads = [grad_qkv, grad_out, grad_up, grad_down]
    moments = [0.5 * mom + grad for mom, grad in zip(momenta, grads)]
    most = max(moment.shape[0] for moment in moments)
    stack = jnp.stack(
        [jnp.pad(moment.astype(low), ((0, most - moment.shape[0]), (0, 0))) for moment in moments]
    )

    def pick(turn):
        return lax.dynamic_index_in_dim(stack, jnp.bitwise_xor(ffn_here, turn), keepdims=False)

    picked = [swap(pick(turn), "ffn", turn) for turn in (1, 2, 3)]
    picked, gx_sent = after((picked, gx_sent))
    matrix = jnp.concatenate([pick(0)] + picked, axis=0)
    *middle_bits, last_bit = [bit for bits in far_groups for bit in bits][1:]
    for bit in middle_bits:
        small = small_step(bit)
    ends = (0, here * 7 // 16, here * 49 // 64, here)
    gx_got = [swap(gx_sent[at:to], "ffn", 2) for at, to in zip(ends, ends[1:])]
    panels = sum_parts(packed_gram(matrix).astype(low))
    panels, gx_got[0] = after((panels, gx_got[0]))
    panels, gx_got[1], (gx_got[2], small_got) = spread_parts(
        panels, gx_got[1], (gx_got[2], swap(small, "seq", last_bit))
    )
    small = small + small_got
    gx_other = jnp.concatenate(gx_got, axis=0)
    steps = schulz(panels, matrix).reshape(4, most, D)
    input_grad = dresidual + (gx_kept.astype(full) + gx_other.astype(full))
    home = [steps[0]] + [swap(steps[turn], "ffn", turn) for turn in (1, 2, 3)]
    step_rates = (
        0.5 * math.sqrt(3.0),
        0.5 * math.sqrt(CLUSTER / 3.0),
        0.5 * math.sqrt(FF / D),
        0.5,
    )
    masters = []
    for member in range(4):
        rows = moments[member].shape[0]
        own = home[member ^ 3][:rows]
        for place in (2, 1, 0):
            own = jnp.where(ffn_here == place, home[member ^ place][:rows], own)
        own = own.astype(full)
        masters.append(weights[member] - step_rates[member] * own)

    grad_norm = small[:4]
    occupancy = small[4, : 4 * heads * clusters].reshape(4 * heads, clusters)
    first_fix = 1.0 - 0.9**ADAM_STEP
    second_fix = 1.0 - 0.999**ADAM_STEP
    first_new = 0.9 * norm_first + 0.1 * grad_norm
    second_new = 0.999 * norm_second + 0.001 * grad_norm * grad_norm
    first_hat = first_new / first_fix
    second_hat = second_new / second_fix
    norm_new = norm_params - 0.5 * (first_hat / (jnp.sqrt(second_hat) + 1e-08) + 0.01 * norm_params)

    def shaped(four):
        return (unrows_qkv(four[0], w_qkv.shape), four[1].reshape(w_out.shape), four[2].T, four[3])

    return (
        (block_out, input_grad)
        + shaped(grads)
        + (grad_norm,)
        + shaped(moments)
        + shaped(masters)
        + (first_new, second_new, norm_new, occupancy)
    )


def solution(mesh):
    rows = P(("seq", "ffn"), None)
    placed = (
        rows,
        rows,
        P("seq", "ffn", None),
        P(None, None, "ffn", "seq"),
        P("ffn", "seq", None),
        P(None, ("seq", "ffn")),
        rows,
        P(None, None, "ffn", "seq"),
        P("ffn", "seq", None),
        P(None, ("seq", "ffn")),
        rows,
        P(),
        P(),
        P(),
    )
    four = placed[3:7]
    return jax.shard_map(
        on_device,
        mesh=mesh,
        in_specs=placed,
        out_specs=(rows, rows) + four + (P(),) + four + four + (P(), P(), P(), P()),
        check_vma=False,
    )
```
